32 devices in a mesh: exp: 8 (over z, y), tp: 4 (over x, core).
Axes of the slice: x: 2, y: 2, z: 4, core: 2. Of those that a mesh axis runs over, the one named last changes fastest.
Arguments:
- tokens: bfloat16 [3072, 768], P('exp', 'tp'), may hold values from -6 to 6
- w_query: bfloat16 [768, 768], P(None, 'tp'), may hold values from -0.02734375 to 0.02734375
- w_key: bfloat16 [768, 768], P(None, 'tp'), may hold values from -0.21875 to 0.21875
- w_value: bfloat16 [768, 768], P(None, 'tp'), may hold values from -0.21875 to 0.21875
- w_output: bfloat16 [768, 768], P('tp'), may hold values from -1.75 to 1.75
- bias_table: bfloat16 [32, 12], P(None, 'tp'), may hold values from -4 to 4
- w_router: bfloat16 [768, 8], P('tp'), may hold values from -0.15625 to 0.15625
- w_in: bfloat16 [8, 768, 3072], P('exp', None, 'tp'), may hold values from -0.21875 to 0.21875
- w_out: bfloat16 [8, 3072, 768], P('exp', 'tp'), may hold values from -3.5 to 3.5
- gain_attn: bfloat16 [768], P('tp'), may hold values from 0.5 to 1.5
- gain_ffn: bfloat16 [768], P('tp'), may hold values from 0.5 to 1.5
- routes: int32 [3072, 1], P('exp'), may hold values from 0 to 7; in each aligned block of 384 rows (0 to 383, 384 to 767, ...) at most 54 rows name the same one
- segments: int32 [8, 384], P('exp'), may hold values from 0 to 3, never falling along the last dimension, each value on 1 to 192 neighbouring positions
- buckets: int32 [767], replicated, may hold values from 0 to 31
- cotangent: bfloat16 [3072, 768], P('exp', 'tp'), may hold values from -6 to 6
Outputs:
- layer_out: bfloat16 [3072, 768], P('exp', 'tp')
- grad_tokens: bfloat16 [3072, 768], P('exp', 'tp')
- grad_query: bfloat16 [768, 768], P(None, 'tp')
- grad_key: bfloat16 [768, 768], P(None, 'tp')
- grad_value: bfloat16 [768, 768], P(None, 'tp')
- grad_output: bfloat16 [768, 768], P('tp')
- grad_table: bfloat16 [32, 12], P(None, 'tp')
- grad_router: bfloat16 [768, 8], P('tp')
- grad_in: bfloat16 [8, 768, 3072], P('exp', None, 'tp')
- grad_out: bfloat16 [8, 3072, 768], P('exp', 'tp')
- grad_gain_attn: bfloat16 [768], P('tp')
- grad_gain_ffn: bfloat16 [768], P('tp')
The draws below stay inside these ranges and needn't reach their ends.
Inputs may be any that keep to these rules, and one draw needn't show every extreme that they name: `routes`: in the 384 tokens of one sequence no expert is named more than 54 times, a bound that some block reaches. `segments`: within a sequence the numbers never fall; each document has 1 to 192 tokens.
All inputs are finite; a program needn't handle non-finite values.
Results may differ from the reference program's by a relative error of at most 0.025.
Values may be sent and summed in bfloat16 or wider, within the bound.
No kernel may reach another device: no remote copies, remote signals or barrier semaphores. Data moves between devices by JAX's collectives and lax.ppermute only.
A program may use at most 128 MiB of HBM per device.

```python
import math
import jax
import jax.numpy as jnp
import numpy as np
from jax import lax

D = 768
HEADS = 12
HD = 64
FF = 3072
NB = 32
SEQ_LEN = 384
DOCS = 4
SEQS = 8
TOKENS = 3072
EXPERTS = 8
CAP = 54


def set_ends(drawn, stream_key, least, top_value):
    dims = drawn.shape
    spot = [jax.random.randint(jax.random.fold_in(stream_key, axis), (), 0, dims[axis]) for axis in range(len(dims))]
    drawn = drawn.at[tuple(spot)].set(least)
    longest = dims.index(max(dims))
    spot[longest] = (spot[longest] + 1) % dims[longest]
    return drawn.at[tuple(spot)].set(top_value)


def steps_of(rng, extent, cuts, low, top_value):
    level = 1.0
    for position, blocks in cuts:
        steps = jax.random.uniform(jax.random.fold_in(jax.random.fold_in(rng, 6), position), (blocks,), jnp.float32, low / len(cuts), top_value / len(cuts))
        level = level * jnp.repeat(jnp.exp(steps), extent[position] // blocks).reshape((-1,) + (1,) * (len(extent) - 1 - position))
    return level


def profile(number_of, total, most, skew):
    portions = [(1 << 20) // math.isqrt(rank ** skew) + 1 for rank in range(2, number_of + 1)]
    rest, given = total - most - (number_of - 1), [1] * (number_of - 1)
    while rest > 0:
        movable = [i for i in range(number_of - 1) if given[i] < most]
        mass, budget = sum([portions[i] for i in movable]), rest
        for i in movable:
            extra = min(most - given[i], max(1, budget * portions[i] // mass), rest)
            given[i] = given[i] + extra
            rest = rest - extra
    return np.array([most] + given)


def ragged_sizes(stream_key, amount, total, most, lean):
    if amount == 2:
        one = jax.random.randint(stream_key, (), max(1, total - most), min(most, total - 1) + 1)
        return jnp.stack([one, total - one])
    sizes = jnp.asarray(profile(amount, total, most, lean), jnp.int32)
    couples = (amount - 1) // 2
    source_of, sink = sizes[1:1 + 2 * couples:2], sizes[2:2 + 2 * couples:2]
    room = jnp.minimum(source_of - 1, most - sink)
    moved = jax.random.randint(jax.random.fold_in(stream_key, 1), (couples,), 0, 1 << 20) % (room + 1)
    sizes = sizes.at[1:1 + 2 * couples:2].set(source_of - moved).at[2:2 + 2 * couples:2].set(sink + moved)
    return sizes[jax.random.permutation(jax.random.fold_in(stream_key, 2), amount)]


def routed_block(own_key, own, number, rows, amount, top, reach, lean):
    ranking = jax.random.permutation(own_key, amount)
    crowded, common = load_shares(amount, rows * top, reach, lean, True), load_shares(amount, rows * top, reach, lean, False)
    places = jnp.arange(amount)

    def named(tallies, offset_by):
        used = int((tallies > 0).sum())
        fixed = max(1, used // 4)
        moved = fixed + (places - fixed + offset_by * (used - fixed)) % max(1, amount - fixed)
        return jnp.zeros((amount,), jnp.int32).at[ranking[jnp.where(places < fixed, places, moved)]].set(jnp.asarray(tallies, jnp.int32))

    tallies = jnp.where(number % 4 == 0, named(crowded, number // 4), named(common, number - number // 4 - 1))
    mixed = jax.random.permutation(jax.random.fold_in(own, 3), amount)
    giver, taker = mixed[0:amount // 2 * 2:2], mixed[1:amount // 2 * 2:2]
    slack = jnp.minimum(tallies[giver] - 1, reach - tallies[taker]) // 2
    slack = jnp.where((giver == ranking[0]) | (taker == ranking[0]) | (tallies[taker] == 0), 0, jnp.maximum(slack, 0))
    moved = jax.random.randint(jax.random.fold_in(own, 4), (amount // 2,), 0, 1 << 20) % (slack + 1)
    tallies = tallies.at[giver].add(-moved).at[taker].add(moved)
    labels = jnp.searchsorted(jnp.cumsum(tallies), jnp.arange(rows * top), side="right").astype(jnp.int32)
    table = labels.reshape(top, rows).T
    table = table[jax.random.permutation(jax.random.fold_in(own, 1), rows)]
    offset_by = jax.random.randint(jax.random.fold_in(own, 2), (rows, 1), 0, top)
    return jnp.take_along_axis(table, (jnp.arange(top)[None, :] + offset_by) % top, axis=1)


def load_shares(count, total, reach, skew, full):
    loads = [(1 << 20) // math.isqrt(rank ** skew) + 1 for rank in range(1, count + 1)]
    largest = reach if full else min(reach, max(-(-total // count), total * loads[0] // sum(loads)))
    least = 1 if total - largest >= count - 1 else 0
    given, spare = [largest] + [least] * (count - 1), total - largest - least * (count - 1)
    while spare > 0:
        free = [i for i in range(1, count) if given[i] < largest] or [i for i in range(1, count) if given[i] < reach]
        pool, remaining = sum([loads[i] for i in free]), spare
        for i in free:
            more = min(reach - given[i], max(1, remaining * loads[i] // pool), spare)
            given[i] = given[i] + more
            spare = spare - more
    return np.array(given)


def scatter_about(key, shape, width, limit, cuts=(), held_as=jnp.bfloat16):
    array = width * jax.random.normal(key, shape, jnp.float32)
    if cuts:
        array = array * steps_of(key, shape, cuts, -0.22, 0.18)
    return jnp.clip(array, -limit, limit).astype(held_as)


def setup_inputs(seed: int = 0) -> dict:
    seeds = jax.random.split(jax.random.key(seed), 16)
    tokens = scatter_about(seeds[0], (TOKENS, D), 1.0, 6.0, ((0, 8), (1, 4)))
    w_query = scatter_about(seeds[1], (D, D), (D * HD) ** -0.5, 0.02734375, ((1, 4),))
    w_key = scatter_about(seeds[2], (D, D), D ** -0.5, 0.21875, ((1, 4),))
    w_value = scatter_about(seeds[3], (D, D), D ** -0.5, 0.21875, ((1, 4),))
    w_output = scatter_about(seeds[4], (D, D), (D // 64) ** -0.5, 1.75, ((0, 4),))
    bias_table = scatter_about(seeds[5], (NB, HEADS), 1.0, 4.0, ((1, 4),))
    w_router = scatter_about(seeds[6], (D, EXPERTS), (2 * D) ** -0.5, 0.15625, ((0, 4),))
    w_in = scatter_about(seeds[7], (EXPERTS, D, FF), D ** -0.5, 0.21875, ((0, 8), (2, 4)))
    w_out = scatter_about(seeds[8], (EXPERTS, FF, D), (1.6 * EXPERTS / FF ** 0.5), 3.5, ((0, 8), (1, 4)))
    gain_attn = jnp.clip(1.0 + 0.1 * jax.random.normal(seeds[9], (D,), jnp.float32), 0.5, 1.5).astype(jnp.bfloat16)
    gain_ffn = jnp.clip(1.0 + 0.1 * jax.random.normal(seeds[10], (D,), jnp.float32), 0.5, 1.5).astype(jnp.bfloat16)
    routes_keys = jax.random.split(jax.random.fold_in(seeds[11], 1), TOKENS // SEQ_LEN)
    routes_turns = jax.random.permutation(jax.random.fold_in(seeds[11], 3), TOKENS // SEQ_LEN)
    routes = jax.vmap(lambda own, number: routed_block(jax.random.fold_in(seeds[11], 2), own, number, SEQ_LEN, EXPERTS, 1, CAP, 2))(routes_keys, routes_turns).reshape((TOKENS, 1))
    segments = jax.vmap(lambda own: jnp.searchsorted(jnp.cumsum(ragged_sizes(own, DOCS, SEQ_LEN, SEQ_LEN // 2, 2)), jnp.arange(SEQ_LEN), side="right"))(jax.random.split(seeds[12], SEQS)).reshape((SEQS, SEQ_LEN)).astype(jnp.int32)
    buckets = set_ends(jax.random.randint(seeds[13], (2 * SEQ_LEN - 1,), 0, NB), jax.random.fold_in(seeds[13], 1), 0, NB - 1).astype(jnp.int32)
    cotangent = scatter_about(seeds[14], (TOKENS, D), 1.0, 6.0, ((0, 8), (1, 4)))
    return dict(tokens=tokens, w_query=w_query, w_key=w_key, w_value=w_value, w_output=w_output, bias_table=bias_table, w_router=w_router, w_in=w_in, w_out=w_out, gain_attn=gain_attn, gain_ffn=gain_ffn, routes=routes, segments=segments, buckets=buckets, cotangent=cotangent)


@jax.custom_vjp
def low(v):
    return lax.optimization_barrier(v.astype(jnp.bfloat16)).astype(jnp.float32)

@jax.custom_vjp
def low_back(v):
    return v

def low_keep(v):
    return (low(v), None)

def low_pass(kept, grad):
    return (grad,)

def back_keep(v):
    return (v, None)

def back_low(kept, grad):
    return (low(grad),)
low.defvjp(low_keep, low_pass)
low_back.defvjp(back_keep, back_low)
EPSILON = 1e-06
NEG_FILL = -1e+30
HIGHEST = lax.Precision.HIGHEST

def matmul(left, right):
    return jnp.dot(left, right, precision=HIGHEST, preferred_element_type=jnp.float32)

def attend(queries, keys_all, values_all, doc_ids, bias_full):
    scores = jnp.einsum('qhd,khd->hqk', queries, keys_all, precision=HIGHEST) + bias_full
    scores = low_back(scores)
    same_doc = doc_ids[:, None] == doc_ids[None, :]
    scores = jnp.where(same_doc[None], scores, NEG_FILL)
    row_max = lax.optimization_barrier(jnp.max(scores, axis=-1, keepdims=True))
    exps = jnp.exp(scores - row_max)
    weights = exps / lax.optimization_barrier(jnp.sum(exps, axis=-1, keepdims=True))
    return jnp.einsum('hqk,khd->qhd', low(weights), values_all, precision=HIGHEST)

def expert_ffn(rows_in, first, second):
    hidden = low_back(matmul(rows_in, first))
    activated = low(jax.nn.gelu(hidden))
    return matmul(activated, second)

def reference(tokens, w_query, w_key, w_value, w_output, bias_table, w_router, w_in, w_out, gain_attn, gain_ffn, routes, segments, buckets, cotangent):
    positions = jnp.arange(SEQ_LEN)
    rel_pos = positions[:, None] - positions[None, :] + SEQ_LEN - 1
    bucket_of = buckets[rel_pos]
    expert_of = routes[:, 0].reshape(SEQS, SEQ_LEN)
    route_hot = (expert_of[:, :, None] == jnp.arange(EXPERTS)[None, None, :]).astype(jnp.int32)
    slot_of = lax.optimization_barrier(jnp.sum((jnp.cumsum(route_hot, axis=1) - 1) * route_hot, axis=-1))
    row_index = jnp.arange(SEQS)[:, None] * CAP + slot_of
    hot_float = route_hot.reshape(TOKENS, EXPERTS).astype(jnp.float32)

    def forward(tok_rows, wq_f, wk_f, wv_f, wo_f, table_f, router_f, first_f, second_f, gain_one, gain_two):
        scale_one = lax.rsqrt(lax.optimization_barrier(jnp.mean(tok_rows * tok_rows, axis=-1, keepdims=True)) + EPSILON)
        normed_one = low(tok_rows * scale_one * gain_one)
        queries = low(low_back(matmul(normed_one, wq_f))).reshape(SEQS, SEQ_LEN, HEADS, HD)
        keys_all = low(low_back(matmul(normed_one, wk_f))).reshape(SEQS, SEQ_LEN, HEADS, HD)
        values_all = low(low_back(matmul(normed_one, wv_f))).reshape(SEQS, SEQ_LEN, HEADS, HD)
        bias_full = jnp.transpose(table_f[bucket_of], (2, 0, 1))

        def one_seq(packed):
            return attend(packed[0], packed[1], packed[2], packed[3], bias_full)
        attn = lax.map(jax.checkpoint(one_seq), (queries, keys_all, values_all, segments))
        attn = low(low_back(attn.reshape(TOKENS, D)))
        attn_sum = low_back(matmul(attn, wo_f))
        residual = tok_rows + attn_sum
        scale_two = lax.rsqrt(lax.optimization_barrier(jnp.mean(residual * residual, axis=-1, keepdims=True)) + EPSILON)
        normed_two = residual * scale_two * gain_two
        logits = matmul(normed_two, router_f)
        router_probs = jax.nn.softmax(logits, axis=-1)
        gate_value = lax.optimization_barrier(jnp.sum(router_probs * hot_float, axis=-1))
        sent = low(low_back(normed_two)).reshape(SEQS, SEQ_LEN, D)
        buffer = jnp.zeros((EXPERTS, SEQS * CAP, D), jnp.float32).at[expert_of, row_index].set(sent)

        def one_expert(packed):
            return expert_ffn(packed[0], packed[1], packed[2])
        expert_rows = lax.map(jax.checkpoint(one_expert), (buffer, first_f, second_f))
        expert_rows = low(low_back(expert_rows))
        returned = expert_rows[expert_of, row_index].reshape(TOKENS, D)
        return residual + gate_value[:, None] * returned
    floats = [a.astype(jnp.float32) for a in (tokens, w_query, w_key, w_value, w_output, bias_table, w_router, w_in, w_out, gain_attn, gain_ffn)]
    result, pullback = jax.vjp(forward, *floats)
    grads = pullback(cotangent.astype(jnp.float32))
    low_grads = [g.astype(jnp.bfloat16) for g in grads]
    return (result.astype(jnp.bfloat16), low_grads[0], low_grads[1], low_grads[2], low_grads[3], low_grads[4], low_grads[5], low_grads[6], low_grads[7], low_grads[8], low_grads[9], low_grads[10])
```

```python
import math

import jax
import jax.numpy as jnp
from jax import lax
from jax.experimental import pallas as pl
from jax.experimental.pallas import tpu as pltpu
from jax.sharding import PartitionSpec as P

HD = 64
EPSILON = 1e-06
NEG_FILL = -1e30
HIGHEST = lax.Precision.HIGHEST
f32 = jnp.float32
bf16 = jnp.bfloat16
PART_ORDER = (0, 2, 1, 3)
VMEM = pl.BlockSpec(memory_space=pltpu.VMEM)
SMEM = pl.BlockSpec(memory_space=pltpu.SMEM)


def run(body, outs, args, name, flops=0):
    specs = [SMEM if a.ndim == 1 else VMEM for a in args]
    moved = sum(a.size * a.dtype.itemsize for a in args)
    moved += sum(math.prod(s) * jnp.dtype(d).itemsize for s, d in outs)
    return pl.pallas_call(
        body,
        out_shape=[jax.ShapeDtypeStruct(s, d) for s, d in outs],
        in_specs=specs,
        out_specs=[VMEM] * len(outs),
        compiler_params=pltpu.CompilerParams(vmem_limit_bytes=48 * 2**20),
        cost_estimate=pl.CostEstimate(flops=flops, bytes_accessed=moved, transcendentals=0),
        name=name,
    )(*args)


def swap(value, axis, mask):
    size = lax.axis_size(axis)
    return lax.ppermute(value, axis, [(i, i ^ mask) for i in range(size)])


def mm(left, right):
    return jnp.dot(left, right, preferred_element_type=f32)


def mm_tn(left, right):
    return lax.dot_general(left, right, (((0,), (0,)), ((), ())), preferred_element_type=f32)


def mm_nt(left, right):
    return lax.dot_general(left, right, (((1,), (1,)), ((), ())), preferred_element_type=f32)


def iota(shape, dim):
    return lax.broadcasted_iota(jnp.int32, shape, dim)


def absolute(pieces, me, place):
    picked = pieces[place]
    for rel in range(1, len(pieces)):
        picked = jnp.where((me ^ rel) == place, pieces[rel], picked)
    return jnp.where(me == place, pieces[0], picked)


def join_lanes(pieces):
    return jnp.concatenate(pieces, axis=1)


def gather_pieces(value):
    across = swap(value, "tp", 2)
    beside = swap(value, "tp", 1)
    return value, beside, across, swap(across, "tp", 1)


def scatter_sum(parts):
    half = parts[:2] + swap(parts[2:], "tp", 1)
    return half[0], swap(half[1], "tp", 2)


def reduce_all(total, order):
    place = lax.axis_index("exp")
    for mask in order:
        half = total.shape[0] // 2
        bit = (place // mask) % 2
        keep = lax.dynamic_slice_in_dim(total, bit * half, half, 0)
        send = lax.dynamic_slice_in_dim(total, (1 - bit) * half, half, 0)
        total = keep + swap(send, "exp", mask)
    for mask in order[::-1]:
        bit = (place // mask) % 2
        other = swap(total, "exp", mask)
        total = jnp.where(
            bit == 0,
            jnp.concatenate([total, other], 0),
            jnp.concatenate([other, total], 0),
        )
    return total


def local(
    tokens,
    w_query,
    w_key,
    w_value,
    w_output,
    bias_table,
    w_router,
    w_in,
    w_out,
    gain_attn,
    gain_ffn,
    routes,
    segments,
    buckets,
    cotangent,
):
    length, quarter = tokens.shape
    ways = lax.axis_size("tp")
    owners = lax.axis_size("exp")
    width = quarter * ways
    here = w_query.shape[1]
    heads = here // HD
    experts = w_router.shape[1]
    bins = bias_table.shape[0]
    hidden_here = w_in.shape[2]
    capacity = max(2, length // owners * 9 // 8)
    per = -(-capacity // ways)
    while experts * per % 128:
        per += 1
    rows = experts * per
    span = 2 * length
    extra = -(-(experts + 2) // 16) * 16
    me_tp = lax.axis_index("tp").astype(jnp.int32)
    me = me_tp[None]
    lanes = 128

    def slot_body(me_ref, route_ref, cot_ref, dest_row_ref, dest_col_ref, cots_ref):
        mine = me_ref[0]
        col = route_ref[...]
        above = iota((length, length), 0)
        along = iota((length, length), 1)
        eye = above == along
        row = jnp.sum(jnp.where(eye, col, 0), axis=0, keepdims=True)
        same = col == row

        def dest(slot, expert):
            chunk = jnp.zeros_like(slot)
            for t in range(1, ways):
                chunk = chunk + (slot >= t * per).astype(jnp.int32)
            return (chunk ^ mine) * rows + expert * per + slot - chunk * per

        slot_row = jnp.sum(jnp.where(same & (above < along), 1, 0), axis=0, keepdims=True)
        slot_col = jnp.sum(jnp.where(same & (along < above), 1, 0), axis=1, keepdims=True)
        dest_row = dest(slot_row, row)
        dest_row_ref[...] = dest_row
        dest_col_ref[...] = dest(slot_col, col)
        cot = cot_ref[...]
        for rel in range(ways):
            hot = (iota((rows, length), 0) + rel * rows == dest_row).astype(bf16)
            cots_ref[rel] = mm(hot, cot).astype(bf16)

    dest_row, dest_col, cots = run(
        slot_body,
        [((1, length), jnp.int32), ((length, 1), jnp.int32), ((ways, rows, quarter), bf16)],
        (me, routes, cotangent),
        "slots",
    )

    shards = jnp.concatenate(
        [
            tokens,
            w_router.T,
            gain_attn[None],
            gain_ffn[None],
            jnp.zeros((extra - experts - 2, quarter), bf16),
        ],
        axis=0,
    )
    shards = gather_pieces(shards)
    cot_pieces = [cots[0]] + [swap(cots[rel], "tp", rel) for rel in range(1, ways)]

    bucket_row = jnp.pad(buckets, (0, span - buckets.shape[0]), constant_values=-1)[None]

    def attend_body(
        me_ref,
        s0,
        s1,
        s2,
        s3,
        wq_ref,
        wk_ref,
        wv_ref,
        wo_ref,
        table_ref,
        bucket_ref,
        seg_ref,
        dest_ref,
        x_ref,
        small_ref,
        r1_ref,
        n1_ref,
        q_ref,
        k_ref,
        v_ref,
        p_ref,
        attn_ref,
        part_ref,
        xrow_ref,
    ):
        mine = me_ref[0]
        pieces = [s0[...], s1[...], s2[...], s3[...]]
        full = join_lanes([absolute(pieces, mine, t) for t in range(ways)])
        x_low = full[:length]
        small = full[length:]
        x_ref[...] = x_low
        small_ref[...] = small
        x = x_low.astype(f32)
        gain = small[experts : experts + 1].astype(f32)
        r1 = lax.rsqrt(jnp.mean(x * x, axis=-1, keepdims=True) + EPSILON)
        r1_ref[...] = r1
        n1 = (x * r1 * gain).astype(bf16)
        n1_ref[...] = n1
        q = mm(n1, wq_ref[...]).astype(bf16)
        k = mm(n1, wk_ref[...]).astype(bf16)
        v = mm(n1, wv_ref[...]).astype(bf16)
        q_ref[...] = q
        k_ref[...] = k
        v_ref[...] = v
        hot = (iota((bins, span), 0) == bucket_ref[...]).astype(bf16)
        offsets = mm_tn(table_ref[...], hot)
        above = iota((length, length), 0)
        along = iota((length, length), 1)
        seg_row = seg_ref[...]
        seg_col = jnp.sum(jnp.where(above == along, seg_row, 0), axis=1, keepdims=True)
        same = seg_col == seg_row
        head_of = iota((1, here), 1) // HD
        attn = jnp.zeros((length, here), f32)
        for h in range(heads):
            mask = (head_of == h).astype(bf16)
            spread = jnp.broadcast_to(offsets[h : h + 1], (length, span))
            bias = pltpu.roll(spread, length + 1, 1, stride=1, stride_axis=0)[:, :length]
            s = jnp.where(same, mm_nt(k * mask, q) + bias, NEG_FILL)
            e = jnp.exp(s - jnp.max(s, axis=0, keepdims=True))
            p = (e / jnp.sum(e, axis=0, keepdims=True)).astype(bf16)
            p_ref[h] = p
            attn = attn + mm_tn(p, v * mask)
        attn = attn.astype(bf16)
        attn_ref[...] = attn
        dest = dest_ref[...]
        for at, rel in enumerate(PART_ORDER):
            hot = (iota((rows, length), 0) + rel * rows == dest).astype(bf16)
            part_ref[at] = mm(mm(hot, attn).astype(bf16), wo_ref[...]).astype(bf16)
            if rel == 0:
                xrow_ref[...] = mm(hot, x_low).astype(bf16)

    x_full, small, r1, n1, q, k, v, probs, attn, o_parts, x_rows = run(
        attend_body,
        [
            ((length, width), bf16),
            ((extra, width), bf16),
            ((length, 1), f32),
            ((length, width), bf16),
            ((length, here), bf16),
            ((length, here), bf16),
            ((length, here), bf16),
            ((heads, length, length), bf16),
            ((length, here), bf16),
            ((ways, rows, width), bf16),
            ((rows, width), bf16),
        ],
        (
            me,
            *shards,
            w_query,
            w_key,
            w_value,
            w_output,
            bias_table,
            bucket_row,
            segments,
            dest_row,
        ),
        "attend",
    )
    o_kept, o_came = scatter_sum(o_parts)

    def route_body(
        me_ref,
        kept_ref,
        came_ref,
        xrow_ref,
        small_ref,
        c0,
        c1,
        c2,
        c3,
        h_ref,
        aux_ref,
        dout_ref,
        send_ref,
    ):
        mine = me_ref[0]
        h = xrow_ref[...].astype(f32) + (kept_ref[...].astype(f32) + came_ref[...].astype(f32))
        h_ref[...] = h
        r2 = lax.rsqrt(jnp.mean(h * h, axis=-1, keepdims=True) + EPSILON)
        gain = small_ref[experts + 1 : experts + 2].astype(f32)
        n2 = h * r2 * gain
        router = small_ref[0:experts].astype(f32)
        logits = lax.dot_general(
            n2, router, (((1,), (1,)), ((), ())), precision=HIGHEST, preferred_element_type=f32
        )
        e = jnp.exp(logits - jnp.max(logits, axis=-1, keepdims=True))
        p = e / jnp.sum(e, axis=-1, keepdims=True)
        owner = iota((rows, experts), 0) - iota((rows, experts), 1) * per
        own = (owner >= 0) & (owner < per)
        g = jnp.sum(jnp.where(own, p, 0.0), axis=-1, keepdims=True)
        pieces = [c0[...], c1[...], c2[...], c3[...]]
        dout = join_lanes([absolute(pieces, mine, t) for t in range(ways)])
        dout_ref[...] = dout
        aux_ref[...] = jnp.zeros_like(aux_ref)
        aux_ref[:, 0:experts] = p
        aux_ref[:, lanes - 2 : lanes - 1] = r2
        aux_ref[:, lanes - 1 : lanes] = g
        send_ref[:, 0:width] = n2.astype(bf16)
        send_ref[:, width : 2 * width] = (g * dout.astype(f32)).astype(bf16)

    h_rows, aux, dout_rows, send = run(
        route_body,
        [
            ((rows, width), f32),
            ((rows, lanes), f32),
            ((rows, width), bf16),
            ((rows, 2 * width), bf16),
        ],
        (me, o_kept, o_came, x_rows, small, *cot_pieces),
        "route",
    )

    def over_experts(value):
        blocks = value.reshape(experts, per, value.shape[1])
        moved = lax.all_to_all(blocks, "exp", split_axis=0, concat_axis=0, tiled=True)
        return moved.reshape(rows, value.shape[1])

    arrived = gather_pieces(over_experts(send))

    def expert_body(a0, a1, a2, a3, win_ref, wout_ref, act_ref, dz_ref, du_ref):
        pieces = [a0, a1, a2, a3]
        u = jnp.concatenate([a[:, 0:width] for a in pieces], axis=0)
        dy = jnp.concatenate([a[:, width : 2 * width] for a in pieces], axis=0)
        z = mm(u, win_ref[0])
        c = math.sqrt(2.0 / math.pi)
        t = jnp.tanh(c * (z + 0.044715 * z * z * z))
        act = (0.5 * z * (1.0 + t)).astype(bf16)
        act_ref[...] = act
        slope = 0.5 * (1.0 + t) + 0.5 * z * (1.0 - t * t) * (c * (1.0 + 3 * 0.044715 * z * z))
        dact = mm_nt(dy, wout_ref[0])
        dot = jnp.sum(dact * act.astype(f32), axis=-1, keepdims=True)
        dz = (dact * slope).astype(bf16)
        dz_ref[...] = dz
        du = mm_nt(dz, win_ref[0]).astype(bf16)
        high = dot.astype(bf16)
        low = (dot - high.astype(f32)).astype(bf16)
        lane = iota((ways * rows, lanes), 1)
        tail = jnp.where(lane == 0, high.astype(f32), jnp.where(lane == 1, low.astype(f32), 0.0))
        tail = tail.astype(bf16)
        for at, rel in enumerate(PART_ORDER):
            du_ref[at, :, 0:width] = du[rel * rows : (rel + 1) * rows]
            du_ref[at, :, width : width + lanes] = tail[rel * rows : (rel + 1) * rows]

    act, dz, du_parts = run(
        expert_body,
        [
            ((ways * rows, hidden_here), bf16),
            ((ways * rows, hidden_here), bf16),
            ((ways, rows, width + lanes), bf16),
        ],
        (*arrived, w_in, w_out),
        "expert",
    )
    du_kept, du_came = scatter_sum(du_parts)
    du_rows = over_experts(du_kept + du_came)

    def value_body(act_ref, wout_ref, y_ref):
        y = mm(act_ref[...], wout_ref[0]).astype(bf16)
        for at, rel in enumerate(PART_ORDER):
            y_ref[at] = y[rel * rows : (rel + 1) * rows]

    (y_parts,) = run(value_body, [((ways, rows, width), bf16)], (act, w_out), "value")
    y_kept, y_came = scatter_sum(y_parts)
    y_rows = over_experts(y_kept + y_came)

    def weights_body(a0, a1, a2, a3, act_ref, dz_ref, gin_ref, gout_ref):
        pieces = [a0, a1, a2, a3]
        u = jnp.concatenate([a[:, 0:width] for a in pieces], axis=0)
        dy = jnp.concatenate([a[:, width : 2 * width] for a in pieces], axis=0)
        gin_ref[0] = mm_tn(u, dz_ref[...]).astype(bf16)
        gout_ref[0] = mm_tn(act_ref[...], dy).astype(bf16)

    grad_in, grad_out = run(
        weights_body,
        [((1, width, hidden_here), bf16), ((1, hidden_here, width), bf16)],
        (*arrived, act, dz),
        "expert_weights",
    )

    def back_body(du_ref, h_ref, aux_ref, dout_ref, small_ref, do_ref, parts_ref):
        du = du_ref[:, 0:width].astype(f32)
        gg = du_ref[:, width : width + 1].astype(f32) + du_ref[
            :, width + 1 : width + 2
        ].astype(f32)
        h = h_ref[...]
        p = aux_ref[:, 0:experts]
        r2 = aux_ref[:, lanes - 2 : lanes - 1]
        gain = small_ref[experts + 1 : experts + 2].astype(f32)
        router = small_ref[0:experts].astype(f32)
        owner = iota((rows, experts), 0) - iota((rows, experts), 1) * per
        own = ((owner >= 0) & (owner < per)).astype(f32)
        dlogits = gg * (own - p)
        dn2 = du + lax.dot_general(
            dlogits, router, (((1,), (0,)), ((), ())), precision=HIGHEST, preferred_element_type=f32
        )
        hr = h * r2
        n2 = hr * gain
        inner = jnp.sum(dn2 * gain * h, axis=-1, keepdims=True)
        dh = dout_ref[...].astype(f32) + r2 * gain * dn2 - hr * (r2 * r2 / width) * inner
        do_ref[...] = dh.astype(bf16)
        parts_ref[...] = jnp.zeros_like(parts_ref)
        parts_ref[0:experts] = lax.dot_general(
            dlogits, n2, (((0,), (0,)), ((), ())), precision=HIGHEST, preferred_element_type=f32
        )
        parts_ref[experts : experts + 1] = jnp.sum(dn2 * hr, axis=0, keepdims=True)

    do_rows, small_parts = run(
        back_body,
        [((rows, width), bf16), ((extra, width), f32)],
        (du_rows, h_rows, aux, dout_rows, small),
        "residual_back",
    )
    do_pieces = gather_pieces(do_rows)

    def outer_body(me_ref, d0, d1, d2, d3, dest_ref, wo_ref, attn_ref, da_ref, own_ref, gwo_ref):
        mine = me_ref[0]
        dest = dest_ref[...]
        total = jnp.zeros((length, width), f32)
        for rel, piece in enumerate((d0, d1, d2, d3)):
            hot = (iota((length, rows), 1) + rel * rows == dest).astype(bf16)
            total = total + mm(hot, piece[...])
        do = total.astype(bf16)
        gwo_ref[...] = mm_tn(attn_ref[...], do).astype(bf16)
        da_ref[...] = mm_nt(do, wo_ref[...]).astype(bf16)
        own = do[:, 0:quarter]
        for t in range(1, ways):
            own = jnp.where(mine == t, do[:, t * quarter : (t + 1) * quarter], own)
        own_ref[...] = own

    da, dh_own, grad_output = run(
        outer_body,
        [((length, here), bf16), ((length, quarter), bf16), ((here, width), bf16)],
        (me, *do_pieces, dest_col, w_output, attn),
        "output_back",
    )

    def softmax_back_body(
        me_ref,
        q_ref,
        k_ref,
        v_ref,
        p_ref,
        da_ref,
        n1_ref,
        bucket_ref,
        dq_ref,
        dk_ref,
        dv_ref,
        grads_ref,
        table_ref,
    ):
        mine = me_ref[0]
        q, k, v, da = q_ref[...], k_ref[...], v_ref[...], da_ref[...]
        head_of = iota((1, here), 1) // HD
        hot = (iota((bins, span), 0) == bucket_ref[...]).astype(f32)
        flip = (iota((length, length), 0) + iota((length, length), 1) == length - 1).astype(bf16)
        dq = jnp.zeros((length, here), f32)
        dk = jnp.zeros((length, here), f32)
        dv = jnp.zeros((length, here), f32)
        tables = []
        for h in range(heads):
            mask = (head_of == h).astype(bf16)
            p_low = p_ref[h]
            p = p_low.astype(f32)
            da_h = da * mask
            dp = mm_nt(v, da_h)
            dv = dv + mm(p_low, da_h)
            inner = jnp.sum(p * dp, axis=0, keepdims=True)
            ds = (p * (dp - inner)).astype(bf16)
            dq = dq + mm_tn(ds, k * mask)
            dk = dk + mm(ds, q * mask)
            flipped = mm(flip, ds)
            flipped = jnp.concatenate([flipped, jnp.zeros_like(flipped)], axis=1)
            offsets = jnp.sum(
                pltpu.roll(flipped, 0, 1, stride=1, stride_axis=0), axis=0, keepdims=True
            )
            tables.append(
                lax.dot_general(
                    offsets,
                    hot,
                    (((1,), (1,)), ((), ())),
                    precision=HIGHEST,
                    preferred_element_type=f32,
                )
            )
        dq, dk, dv = dq.astype(bf16), dk.astype(bf16), dv.astype(bf16)
        dq_ref[...] = dq
        dk_ref[...] = dk
        dv_ref[...] = dv
        n1 = n1_ref[...]
        grads_ref[0:width, 0:here] = mm_tn(n1, dq).astype(bf16)
        grads_ref[0:width, here : 2 * here] = mm_tn(n1, dk).astype(bf16)
        gv = mm_tn(n1, dv).astype(bf16)
        grads_ref[width : width + width // 2, 0:here] = gv[0 : width // 2]
        grads_ref[width : width + width // 2, here : 2 * here] = gv[width // 2 :]
        table_ref[...] = jnp.zeros_like(table_ref)
        for t in range(ways):
            keep = (mine == t).astype(f32)
            for h in range(heads):
                table_ref[h : h + 1, t * bins : (t + 1) * bins] = tables[h] * keep

    dq, dk, dv, grads, table_part = run(
        softmax_back_body,
        [
            ((length, here), bf16),
            ((length, here), bf16),
            ((length, here), bf16),
            ((width + width // 2, 2 * here), bf16),
            ((8, width), f32),
        ],
        (me, q, k, v, probs, da, n1, bucket_row),
        "softmax_back",
    )

    def norm_back_body(me_ref, dq_ref, dk_ref, dv_ref, wq, wk, wv, x_ref, r1_ref, small_ref, *outs):
        part_ref, gain_ref = outs
        mine = me_ref[0]
        dn1 = mm_nt(dq_ref[...], wq[...])
        dn1 = dn1 + mm_nt(dk_ref[...], wk[...])
        dn1 = dn1 + mm_nt(dv_ref[...], wv[...])
        x = x_ref[...].astype(f32)
        gain = small_ref[experts : experts + 1].astype(f32)
        prod = dn1 * x
        gain_ref[...] = jnp.zeros_like(gain_ref)
        gain_ref[0:1] = jnp.sum(prod * r1_ref[...], axis=0, keepdims=True)
        dot = jnp.sum(prod * gain, axis=-1, keepdims=True)
        high = dot.astype(bf16).astype(f32)
        lane = iota((length, lanes), 1)
        tail = jnp.where(lane == 0, high, jnp.where(lane == 1, dot - high, 0.0)).astype(bf16)
        low = dn1.astype(bf16)
        wide = part_ref.shape[2]
        for at, rel in enumerate(PART_ORDER):
            piece = low[:, 0:quarter]
            for t in range(1, ways):
                piece = jnp.where((mine ^ rel) == t, low[:, t * quarter : (t + 1) * quarter], piece)
            part_ref[at, :, 0:quarter] = piece
            part_ref[at, :, quarter:wide] = tail[:, 0 : wide - quarter]

    wide = -(-(quarter + 2) // 128) * 128
    dn1_parts, gain_part = run(
        norm_back_body,
        [((ways, length, wide), bf16), ((8, width), f32)],
        (me, dq, dk, dv, w_query, w_key, w_value, x_full, r1, small),
        "norm_back",
    )
    dn1_kept, dn1_came = scatter_sum(dn1_parts)

    def tokens_body(kept_ref, came_ref, dh_ref, tok_ref, r1_ref, gain_ref, out_ref):
        total = kept_ref[...].astype(f32) + came_ref[...].astype(f32)
        dn1 = total[:, 0:quarter]
        dot = total[:, quarter : quarter + 1] + total[:, quarter + 1 : quarter + 2]
        one = r1_ref[...]
        x = tok_ref[...].astype(f32)
        out_ref[...] = (
            dh_ref[...].astype(f32)
            + one * gain_ref[...].astype(f32) * dn1
            - x * (one * one * one / width) * dot
        ).astype(bf16)

    (grad_tokens,) = run(
        tokens_body,
        [((length, quarter), bf16)],
        (dn1_kept, dn1_came, dh_own, tokens, r1, gain_attn[None]),
        "tokens_back",
    )

    def out_rows_body(me_ref, h_ref, aux_ref, y_ref, out_ref):
        mine = me_ref[0]
        out = (h_ref[...] + aux_ref[:, lanes - 1 : lanes] * y_ref[...].astype(f32)).astype(bf16)
        for rel in range(ways):
            piece = out[:, 0:quarter]
            for t in range(1, ways):
                piece = jnp.where((mine ^ rel) == t, out[:, t * quarter : (t + 1) * quarter], piece)
            out_ref[rel] = piece

    (lo,) = run(
        out_rows_body,
        [((ways, rows, quarter), bf16)],
        (me, h_rows, aux, y_rows),
        "layer_rows",
    )
    lo_pieces = [lo[0]] + [swap(lo[rel], "tp", rel) for rel in range(1, ways)]

    def out_body(dest_ref, l0, l1, l2, l3, out_ref):
        dest = dest_ref[...]
        total = jnp.zeros((length, quarter), f32)
        for rel, piece in enumerate((l0, l1, l2, l3)):
            hot = (iota((length, rows), 1) + rel * rows == dest).astype(bf16)
            total = total + mm(hot, piece[...])
        out_ref[...] = total.astype(bf16)

    (layer_out,) = run(
        out_body, [((length, quarter), bf16)], (dest_col, *lo_pieces), "layer_out"
    )

    bits = [1 << b for b in range(owners.bit_length() - 1)]
    turned = bits[1:] + bits[:1]
    grad_output = reduce_all(grad_output, bits)
    half = grads.shape[0] // 2
    first = reduce_all(grads[:half], bits)
    second = reduce_all(grads[half:], turned)
    few = jnp.concatenate([small_parts, gain_part, table_part], axis=0)
    for mask in (1, 2):
        few = few + swap(few, "tp", mask)
    for mask in bits:
        few = few + swap(few, "exp", mask)
    both = jnp.concatenate([first, second], axis=0)
    grad_query = both[:width, :here]
    grad_key = both[:width, here:]
    grad_value = jnp.concatenate([both[width:, :here], both[width:, here:]], axis=0)
    mine = lax.dynamic_slice_in_dim(few, me_tp * quarter, quarter, 1)
    tables = lax.dynamic_slice_in_dim(few[extra + 8 :], me_tp * bins, bins, 1)
    return (
        layer_out,
        grad_tokens,
        grad_query,
        grad_key,
        grad_value,
        grad_output,
        tables[:heads].T.astype(bf16),
        mine[:experts].T.astype(bf16),
        grad_in,
        grad_out,
        mine[extra].astype(bf16),
        mine[experts].astype(bf16),
    )


def solution(mesh):
    placed = (
        P("exp", "tp"),
        P(None, "tp"),
        P(None, "tp"),
        P(None, "tp"),
        P("tp", None),
        P(None, "tp"),
        P("tp", None),
        P("exp", None, "tp"),
        P("exp", "tp", None),
        P("tp"),
        P("tp"),
        P("exp", None),
        P("exp", None),
        P(),
        P("exp", "tp"),
    )
    return jax.shard_map(
        local,
        mesh=mesh,
        in_specs=placed,
        out_specs=(
            P("exp", "tp"),
            P("exp", "tp"),
            P(None, "tp"),
            P(None, "tp"),
            P(None, "tp"),
            P("tp", None),
            P(None, "tp"),
            P("tp", None),
            P("exp", None, "tp"),
            P("exp", "tp", None),
            P("tp"),
            P("tp"),
        ),
        check_vma=False,
    )
```

```python
import math

import jax
import jax.numpy as jnp
from jax import lax
from jax.experimental import pallas as pl
from jax.experimental.pallas import tpu as pltpu
from jax.sharding import PartitionSpec as P

HD = 64
EPSILON = 1e-06
NEG_FILL = -1e30
HIGHEST = lax.Precision.HIGHEST
LANES = 128
f32 = jnp.float32
bf16 = jnp.bfloat16
VMEM = pl.BlockSpec(memory_space=pltpu.VMEM)
SMEM = pl.BlockSpec(memory_space=pltpu.SMEM)


def run(body, outs, args, name, us=1.0, scratch=(), limit=16):
    specs = [SMEM if a.shape == (1,) else VMEM for a in args]
    moved = sum(a.size * a.dtype.itemsize for a in args)
    moved += sum(math.prod(s) * jnp.dtype(d).itemsize for s, d in outs)
    return pl.pallas_call(
        body,
        out_shape=[jax.ShapeDtypeStruct(s, d) for s, d in outs],
        in_specs=specs,
        out_specs=[VMEM] * len(outs),
        scratch_shapes=list(scratch),
        compiler_params=pltpu.CompilerParams(vmem_limit_bytes=limit * 2**20),
        cost_estimate=pl.CostEstimate(
            flops=int(us * 1.1e9), bytes_accessed=moved, transcendentals=0
        ),
        name=name,
    )(*args)


def swap(value, axis, mask):
    size = lax.axis_size(axis)
    return lax.ppermute(value, axis, [(i, i ^ mask) for i in range(size)])


def after(value, *others):
    return lax.optimization_barrier((value, *others))[0]


def mm(left, right):
    return jnp.dot(left, right, preferred_element_type=f32)


def mm_tn(left, right):
    return lax.dot_general(left, right, (((0,), (0,)), ((), ())), preferred_element_type=f32)


def mm_nt(left, right, precision=None):
    return lax.dot_general(
        left, right, (((1,), (1,)), ((), ())), precision=precision, preferred_element_type=f32
    )


def iota(shape, dim):
    return lax.broadcasted_iota(jnp.int32, shape, dim)


def absolute(pieces, me, place):
    picked = pieces[0]
    for rel in range(1, len(pieces)):
        picked = jnp.where((me ^ rel) == place, pieces[rel], picked)
    return picked


def split_low(value):
    high = value.astype(bf16)
    return high.astype(f32), value - high.astype(f32)


def two_lanes(value, count):
    high, low = split_low(value)
    lane = iota((value.shape[0], count), 1)
    return jnp.where(lane == 0, high, jnp.where(lane == 1, low, 0.0)).astype(bf16)


def gather_pieces(value):
    across = swap(value, "tp", 2)
    beside = swap(value, "tp", 1)
    return value, beside, across, swap(across, "tp", 1)


def scatter_sum(kept, passed, sent):
    came = swap(sent, "tp", 1)
    return kept, came, swap(passed + came[1], "tp", 2)


def chain_sum(keep, send, masks, tail):
    body = keep.shape[0] - tail
    total = keep
    for at, mask in enumerate(masks):
        total = keep + swap(send, "exp", mask)
        if at + 1 < len(masks):
            half = body // 2
            keep = total[:half]
            if tail:
                keep = jnp.concatenate([keep, total[body:]], axis=0)
            send = total[half:]
            body = half
    mine, few = total[:body], total[body:]
    for mask in masks[:0:-1]:
        mine = jnp.concatenate([mine, swap(mine, "exp", mask)], axis=0)
    return mine, swap(mine, "exp", masks[0]), few


def rel_of(place, masks):
    top = len(masks) - 1
    return sum(mask for at, mask in enumerate(masks) if (place >> (top - at)) & 1)


def local(
    tokens,
    w_query,
    w_key,
    w_value,
    w_output,
    bias_table,
    w_router,
    w_in,
    w_out,
    gain_attn,
    gain_ffn,
    routes,
    segments,
    buckets,
    cotangent,
):
    length, quarter = tokens.shape
    ways = lax.axis_size("tp")
    owners = lax.axis_size("exp")
    width = quarter * ways
    here = w_query.shape[1]
    heads = here // HD
    experts = w_router.shape[1]
    bins = bias_table.shape[0]
    hidden_here = w_in.shape[2]
    capacity = max(2, length // owners * 9 // 8)
    per = -(-capacity // ways)
    while experts * per % LANES:
        per += 1
    rows = experts * per
    span = 2 * length
    extra = -(-(experts + 2) // 16) * 16
    few_rows = -(-(experts + 2 + heads) // 16) * 16
    me = lax.axis_index(("exp", "tp")).astype(jnp.int32)[None]
    bits = [1 << b for b in range(owners.bit_length() - 1)]
    order_a = bits
    order_b = bits[1:] + bits[:1]
    shift = ways.bit_length() - 1

    tok_t = tokens.T
    wq_t, wk_t, wv_t = w_query.T, w_key.T, w_value.T

    tok_pieces = gather_pieces(tok_t)

    def slot_body(
        me_ref, route_ref, cot_ref, router_ref, g1_ref, g2_ref, drow_ref, dcol_ref, cots_ref, d_ref
    ):
        mine = me_ref[0] & (ways - 1)
        row = route_ref[...]
        above = iota((length, length), 0)
        along = iota((length, length), 1)
        col = jnp.sum(jnp.where(above == along, row, 0), axis=1, keepdims=True)
        same = col == row

        def dest(slot, expert):
            chunk = jnp.zeros_like(slot)
            for t in range(1, ways):
                chunk = chunk + (slot >= t * per).astype(jnp.int32)
            return (chunk ^ mine) * rows + expert * per + slot - chunk * per

        slot_row = jnp.sum(jnp.where(same & (above < along), 1, 0), axis=0, keepdims=True)
        slot_col = jnp.sum(jnp.where(same & (along < above), 1, 0), axis=1, keepdims=True)
        dest_row = dest(slot_row, row)
        drow_ref[...] = dest_row
        dcol_ref[...] = dest(slot_col, col)
        cot = cot_ref[...]
        line = iota((extra - experts, quarter), 0)
        gains = jnp.where(
            line == 0,
            g1_ref[...].astype(f32),
            jnp.where(line == 1, g2_ref[...].astype(f32), 0.0),
        )
        few = jnp.concatenate([router_ref[...].astype(f32), gains], axis=0).astype(bf16)
        for rel in range(ways):
            hot = (iota((rows, length), 0) + rel * rows == dest_row).astype(bf16)
            piece = mm_nt(hot, cot).astype(bf16)
            cots_ref[rel, 0:rows] = piece
            cots_ref[rel, rows : rows + extra] = few
            d_ref[:, rel * quarter : (rel + 1) * quarter] = piece

    dest_row, dest_col, cots, d_send = run(
        slot_body,
        [
            ((1, length), jnp.int32),
            ((length, 1), jnp.int32),
            ((ways, rows + extra, quarter), bf16),
            ((rows, width), bf16),
        ],
        (me, routes.T, cotangent.T, w_router.T, gain_attn[None], gain_ffn[None]),
        "slots",
        us=0.7,
    )
    cot_pieces = [cots[0]] + [swap(cots[rel], "tp", rel) for rel in range(1, ways)]

    def over_experts(value):
        blocks = value.reshape(experts, per, value.shape[1])
        moved = lax.all_to_all(blocks, "exp", split_axis=0, concat_axis=0, tiled=True)
        return moved.reshape(rows, value.shape[1])

    bucket_row = jnp.pad(buckets, (0, span - buckets.shape[0]), constant_values=-1)[None]

    def spread_row(few, line, count):
        pick = (iota((few.shape[0], count), 0) == line).astype(bf16)
        return mm_tn(few, pick)

    def attend_body(
        me_ref,
        t0,
        t1,
        t2,
        t3,
        c0,
        c1,
        c2,
        c3,
        wq_ref,
        wk_ref,
        wv_ref,
        wo_ref,
        table_ref,
        bucket_ref,
        seg_ref,
        dest_ref,
        x_ref,
        small_ref,
        r1_ref,
        n1_ref,
        q_ref,
        k_ref,
        v_ref,
        p_ref,
        attn_ref,
        kept_ref,
        passed_ref,
        sent_ref,
        xrow_ref,
    ):
        mine = me_ref[0] & (ways - 1)
        for rel, piece in enumerate((t0, t1, t2, t3)):
            at = pl.multiple_of((mine ^ rel) * quarter, quarter)
            x_ref[pl.ds(at, quarter), :] = piece[...]
        pieces = [c[rows : rows + extra] for c in (c0, c1, c2, c3)]
        small = jnp.concatenate([absolute(pieces, mine, t) for t in range(ways)], axis=1)
        small_ref[...] = small
        x_low = x_ref[...]
        x = x_low.astype(f32)
        r1 = lax.rsqrt(jnp.mean(x * x, axis=0, keepdims=True) + EPSILON)
        r1_ref[...] = r1
        n1 = (x * r1 * spread_row(small, experts, length)).astype(bf16)
        n1_ref[...] = n1
        q = mm(wq_ref[...], n1).astype(bf16)
        k = mm(wk_ref[...], n1).astype(bf16)
        v = mm(wv_ref[...], n1).astype(bf16)
        q_ref[...] = q
        k_ref[...] = k
        v_ref[...] = v
        hot = (iota((bins, span), 0) == bucket_ref[...]).astype(bf16)
        offsets = mm(table_ref[...], hot)
        above = iota((length, length), 0)
        along = iota((length, length), 1)
        seg_row = seg_ref[...]
        seg_col = jnp.sum(jnp.where(above == along, seg_row, 0), axis=1, keepdims=True)
        same = seg_col == seg_row
        for h in range(heads):
            part = slice(h * HD, (h + 1) * HD)
            spread = jnp.broadcast_to(offsets[h : h + 1], (length, span))
            bias = pltpu.roll(spread, length + 1, 1, stride=1, stride_axis=0)[:, :length]
            s = jnp.where(same, mm_tn(k[part], q[part]) + bias, NEG_FILL)
            e = jnp.exp(s - jnp.max(s, axis=0, keepdims=True))
            p = (e / jnp.sum(e, axis=0, keepdims=True)).astype(bf16)
            p_ref[h] = p
            attn_ref[part] = mm(v[part], p).astype(bf16)
        attn = attn_ref[...]
        dest = dest_ref[...]
        wo = wo_ref[...]
        for rel, out in enumerate((kept_ref, sent_ref.at[0], passed_ref, sent_ref.at[1])):
            hot = (iota((rows, length), 0) + rel * rows == dest).astype(bf16)
            out[...] = mm(mm_nt(hot, attn).astype(bf16), wo).astype(bf16)
            if rel == 0:
                xrow_ref[...] = mm_nt(hot, x_low).astype(bf16)

    x_full, small, r1, n1, q, k, v, probs, attn, o_kept, o_passed, o_sent, x_rows = run(
        attend_body,
        [
            ((width, length), bf16),
            ((extra, width), bf16),
            ((1, length), f32),
            ((width, length), bf16),
            ((here, length), bf16),
            ((here, length), bf16),
            ((here, length), bf16),
            ((heads, length, length), bf16),
            ((here, length), bf16),
            ((rows, width), bf16),
            ((rows, width), bf16),
            ((2, rows, width), bf16),
            ((rows, width), bf16),
        ],
        (
            me,
            *tok_pieces,
            *cot_pieces,
            wq_t,
            wk_t,
            wv_t,
            w_output,
            bias_table.T,
            bucket_row,
            segments,
            dest_row,
        ),
        "attend",
        us=4.0,
        limit=24,
    )
    o_kept, o_beside, o_across = scatter_sum(o_kept, o_passed, o_sent)

    d_pieces = gather_pieces(over_experts(d_send))

    def route_body(
        me_ref,
        kept_ref,
        beside_ref,
        across_ref,
        xrow_ref,
        small_ref,
        c0,
        c1,
        c2,
        c3,
        h_ref,
        aux_ref,
        dout_ref,
        send_ref,
    ):
        mine = me_ref[0] & (ways - 1)
        o = kept_ref[...].astype(f32) + beside_ref[0].astype(f32) + across_ref[...].astype(f32)
        h = xrow_ref[...].astype(f32) + o
        h_ref[...] = h
        r2 = lax.rsqrt(jnp.mean(h * h, axis=-1, keepdims=True) + EPSILON)
        gain = small_ref[experts + 1 : experts + 2].astype(f32)
        n2 = h * r2 * gain
        logits = mm_nt(n2, small_ref[0:experts].astype(f32), HIGHEST)
        e = jnp.exp(logits - jnp.max(logits, axis=-1, keepdims=True))
        p = e / jnp.sum(e, axis=-1, keepdims=True)
        owner = iota((rows, experts), 0) - iota((rows, experts), 1) * per
        own = (owner >= 0) & (owner < per)
        g = jnp.sum(jnp.where(own, p, 0.0), axis=-1, keepdims=True)
        pieces = [c[0:rows] for c in (c0, c1, c2, c3)]
        dout_ref[...] = jnp.concatenate([absolute(pieces, mine, t) for t in range(ways)], axis=1)
        aux_ref[...] = jnp.zeros_like(aux_ref)
        aux_ref[:, 0:experts] = p
        aux_ref[:, LANES - 2 : LANES - 1] = r2
        aux_ref[:, LANES - 1 : LANES] = g
        send_ref[:, 0:width] = n2.astype(bf16)
        send_ref[:, width : width + LANES] = two_lanes(g, LANES)

    h_rows, aux, dout_rows, send = run(
        route_body,
        [
            ((rows, width), f32),
            ((rows, LANES), f32),
            ((rows, width), bf16),
            ((rows, width + LANES), bf16),
        ],
        (me, o_kept, o_beside, o_across, x_rows, small, *cot_pieces),
        "route",
        us=0.8,
    )
    arrived = gather_pieces(over_experts(send))

    def expert_body(me_ref, a0, a1, a2, a3, d0, d1, d2, d3, win_ref, wout_ref, *outs):
        u_ref, dy_ref, act_ref, dz_ref, kept_ref, passed_ref, sent_ref = outs
        mine = me_ref[0] & (ways - 1)
        douts = (d0, d1, d2, d3)
        for rel, a in enumerate((a0, a1, a2, a3)):
            part = slice(rel * rows, (rel + 1) * rows)
            u_ref[part] = a[:, 0:width]
            g = a[:, width : width + 1].astype(f32) + a[:, width + 1 : width + 2].astype(f32)
            pieces = []
            for src in range(ways):
                at = (rel ^ src) * quarter
                pieces.append(douts[src][:, at : at + quarter])
            dout = jnp.concatenate([absolute(pieces, mine, t) for t in range(ways)], axis=1)
            dy_ref[part] = (g * dout.astype(f32)).astype(bf16)
        u = u_ref[...]
        dy = dy_ref[...]
        z = mm(u, win_ref[0])
        c = math.sqrt(2.0 / math.pi)
        t = jnp.tanh(c * (z + 0.044715 * z * z * z))
        act = (0.5 * z * (1.0 + t)).astype(bf16)
        act_ref[...] = act
        slope = 0.5 * (1.0 + t) + 0.5 * z * (1.0 - t * t) * (c * (1.0 + 3 * 0.044715 * z * z))
        dact = mm_nt(dy, wout_ref[0])
        dot = jnp.sum(dact * act.astype(f32), axis=-1, keepdims=True)
        dz = (dact * slope).astype(bf16)
        dz_ref[...] = dz
        du = mm_nt(dz, win_ref[0]).astype(bf16)
        tail = two_lanes(dot, LANES)
        for rel, out in enumerate((kept_ref, sent_ref.at[0], passed_ref, sent_ref.at[1])):
            out[:, 0:width] = du[rel * rows : (rel + 1) * rows]
            out[:, width : width + LANES] = tail[rel * rows : (rel + 1) * rows]

    u_all, dy_all, act, dz, *du_parts = run(
        expert_body,
        [
            ((ways * rows, width), bf16),
            ((ways * rows, width), bf16),
            ((ways * rows, hidden_here), bf16),
            ((ways * rows, hidden_here), bf16),
            ((rows, width + LANES), bf16),
            ((rows, width + LANES), bf16),
            ((2, rows, width + LANES), bf16),
        ],
        (me, *arrived, *d_pieces, w_in, w_out),
        "expert",
        us=4.0,
        limit=24,
    )
    du_kept, du_beside, du_across = scatter_sum(*du_parts)
    du_sum = du_kept + du_beside[0] + du_across
    du_rows = over_experts(du_sum)

    def value_body(act_ref, wout_ref, kept_ref, passed_ref, sent_ref):
        y = mm(act_ref[...], wout_ref[0]).astype(bf16)
        for rel, out in enumerate((kept_ref, sent_ref.at[0], passed_ref, sent_ref.at[1])):
            out[...] = y[rel * rows : (rel + 1) * rows]

    act_late = after(act, du_sum)
    y_parts = run(
        value_body,
        [((rows, width), bf16), ((rows, width), bf16), ((2, rows, width), bf16)],
        (act_late, w_out),
        "value",
        us=0.8,
    )
    y_kept, y_beside, y_across = scatter_sum(*y_parts)
    y_sum = y_kept + y_beside[0] + y_across

    def weights_body(u_ref, dy_ref, act_ref, dz_ref, gin_ref, gout_ref):
        gin_ref[0] = mm_tn(u_ref[...], dz_ref[...]).astype(bf16)
        gout_ref[0] = mm_tn(act_ref[...], dy_ref[...]).astype(bf16)

    grad_in, grad_out = run(
        weights_body,
        [((1, width, hidden_here), bf16), ((1, hidden_here, width), bf16)],
        (u_all, dy_all, act_late, dz),
        "expert_weights",
        us=2.5,
    )
    du_rows, y_sum, grad_in, grad_out = lax.optimization_barrier(
        (du_rows, y_sum, grad_in, grad_out)
    )
    y_rows = over_experts(y_sum)

    def back_body(du_ref, h_ref, aux_ref, dout_ref, small_ref, do_ref, parts_ref):
        du = du_ref[:, 0:width].astype(f32)
        gg = du_ref[:, width : width + 1].astype(f32)
        gg = gg + du_ref[:, width + 1 : width + 2].astype(f32)
        h = h_ref[...]
        p = aux_ref[:, 0:experts]
        r2 = aux_ref[:, LANES - 2 : LANES - 1]
        gain = small_ref[experts + 1 : experts + 2].astype(f32)
        router = small_ref[0:experts].astype(f32)
        owner = iota((rows, experts), 0) - iota((rows, experts), 1) * per
        own = ((owner >= 0) & (owner < per)).astype(f32)
        dlogits = gg * (own - p)
        dn2 = du + lax.dot_general(
            dlogits, router, (((1,), (0,)), ((), ())), precision=HIGHEST, preferred_element_type=f32
        )
        hr = h * r2
        n2 = hr * gain
        inner = jnp.sum(dn2 * gain * h, axis=-1, keepdims=True)
        dh = dout_ref[...].astype(f32) + r2 * gain * dn2 - hr * (r2 * r2 / width) * inner
        do_ref[...] = dh.astype(bf16)
        parts_ref[...] = jnp.zeros_like(parts_ref)
        parts_ref[0:experts] = lax.dot_general(
            dlogits, n2, (((0,), (0,)), ((), ())), precision=HIGHEST, preferred_element_type=f32
        )
        parts_ref[experts : experts + 1] = jnp.sum(dn2 * hr, axis=0, keepdims=True)

    do_rows, few_parts = run(
        back_body,
        [((rows, width), bf16), ((few_rows, width), f32)],
        (du_rows, h_rows, aux, dout_rows, small),
        "residual_back",
        us=2.0,
    )
    do_pieces = gather_pieces(do_rows)

    chunk = 2 * here // owners

    def attend_back_body(
        me_ref,
        d0,
        d1,
        d2,
        d3,
        drow_ref,
        dcol_ref,
        wo_ref,
        attn_ref,
        q_ref,
        k_ref,
        v_ref,
        p_ref,
        n1_ref,
        wq_ref,
        wk_ref,
        wv_ref,
        small_ref,
        few_ref,
        bucket_ref,
        own_ref,
        dq_ref,
        dk_ref,
        dv_ref,
        akeep_ref,
        asend_ref,
        bkeep_ref,
        bsend_ref,
        a_ref,
        b_ref,
    ):
        mine = me_ref[0] & (ways - 1)
        place = me_ref[0] >> shift
        stack = jnp.concatenate([d[...] for d in (d0, d1, d2, d3)], axis=0)
        hot_t = (iota((length, ways * rows), 1) == dcol_ref[...]).astype(bf16)
        do = mm(hot_t, stack).astype(bf16)
        own = stack[:, 0:quarter]
        for t in range(1, ways):
            own = jnp.where(mine == t, stack[:, t * quarter : (t + 1) * quarter], own)
        hot = (iota((ways * rows, length), 0) == drow_ref[...]).astype(bf16)
        own_ref[...] = mm_tn(own, hot).astype(bf16)
        wo = wo_ref[...]
        da = mm_nt(wo, do).astype(bf16)
        hot = (iota((bins, span), 0) == bucket_ref[...]).astype(f32)
        flip = (iota((length, length), 0) + iota((length, length), 1) == length - 1).astype(bf16)
        tables = []
        for h in range(heads):
            part = slice(h * HD, (h + 1) * HD)
            p_low = p_ref[h]
            p = p_low.astype(f32)
            dp = mm_tn(v_ref[part], da[part])
            dv_ref[part] = mm_nt(da[part], p_low).astype(bf16)
            inner = jnp.sum(p * dp, axis=0, keepdims=True)
            ds = (p * (dp - inner)).astype(bf16)
            dq_ref[part] = mm(k_ref[part], ds).astype(bf16)
            dk_ref[part] = mm_nt(q_ref[part], ds).astype(bf16)
            flipped = mm(flip, ds)
            flipped = jnp.concatenate([flipped, jnp.zeros_like(flipped)], axis=1)
            offsets = pltpu.roll(flipped, 0, 1, stride=1, stride_axis=0)
            offsets = jnp.sum(offsets, axis=0, keepdims=True)
            tables.append(mm_nt(offsets, hot, HIGHEST))
        n1 = n1_ref[...]
        gq = mm_nt(dq_ref[...], n1)
        gk = mm_nt(dk_ref[...], n1)
        gv = mm_nt(dv_ref[...], n1)
        back = gq * wq_ref[...].astype(f32) + gk * wk_ref[...].astype(f32)
        back = jnp.sum(back + gv * wv_ref[...].astype(f32), axis=0, keepdims=True)
        gain = small_ref[experts : experts + 1].astype(f32)
        gwo = mm(attn_ref[...], do)
        for c in range(owners):
            for total, ref in (((gq, gk), a_ref), ((gv, gwo), b_ref)):
                low, high = c * chunk, (c + 1) * chunk
                picked = total[0][low:high] if high <= here else total[1][low - here : high - here]
                ref[c] = picked.astype(bf16)
        tail = (owners // 2) * chunk
        for order, ref, keep, send in (
            (order_a, a_ref, akeep_ref, asend_ref),
            (order_b, b_ref, bkeep_ref, bsend_ref),
        ):
            for at in range(owners):
                out, line = (keep, at) if at < owners // 2 else (send, at - owners // 2)
                out[line * chunk : (line + 1) * chunk] = ref[rel_of(at, order) ^ place]
        few = few_ref[...]
        line = iota((few_rows, 1), 0)
        few = few + jnp.where(line == experts + 1, back / gain, 0.0)
        wide = jnp.concatenate(
            [jnp.concatenate([tables[h] * (mine == t).astype(f32) for t in range(ways)], axis=1)
             for h in range(heads)],
            axis=0,
        )
        pad = jnp.zeros((heads, width - ways * bins), f32)
        wide = jnp.concatenate([wide, pad], axis=1)
        for h in range(heads):
            few = few + jnp.where(line == experts + 2 + h, wide[h : h + 1], 0.0)
        few = few.astype(bf16)
        akeep_ref[tail : tail + few_rows] = few
        asend_ref[tail : tail + few_rows] = few

    side = (owners // 2) * chunk
    dh_own, dq, dk, dv, a_keep, a_send, b_keep, b_send = run(
        attend_back_body,
        [
            ((quarter, length), bf16),
            ((here, length), bf16),
            ((here, length), bf16),
            ((here, length), bf16),
            ((side + few_rows, width), bf16),
            ((side + few_rows, width), bf16),
            ((side, width), bf16),
            ((side, width), bf16),
        ],
        (
            me,
            *do_pieces,
            dest_row,
            dest_col,
            w_output,
            attn,
            q,
            k,
            v,
            probs,
            n1,
            wq_t,
            wk_t,
            wv_t,
            small,
            few_parts,
            bucket_row,
        ),
        "attend_back",
        us=6.0,
        scratch=[
            pltpu.VMEM((owners, chunk, width), bf16),
            pltpu.VMEM((owners, chunk, width), bf16),
        ],
        limit=24,
    )

    a_mine, a_other, few = chain_sum(a_keep, a_send, order_a, few_rows)
    b_mine, b_other, none = chain_sum(b_keep, b_send, order_b, 0)

    def norm_back_body(
        me_ref, dq_ref, dk_ref, dv_ref, wq, wk, wv, x_ref, small_ref, *outs
    ):
        kept_ref, passed_ref, sent_ref, all_ref = outs
        mine = me_ref[0] & (ways - 1)
        dn1 = mm_tn(wq[...], dq_ref[...])
        dn1 = dn1 + mm_tn(wk[...], dk_ref[...])
        dn1 = dn1 + mm_tn(wv[...], dv_ref[...])
        all_ref[...] = dn1.astype(bf16)
        gain = spread_row(small_ref[...], experts, length)
        dot = jnp.sum(dn1 * gain * x_ref[...].astype(f32), axis=0, keepdims=True)
        high, low = split_low(dot)
        line = iota((16, length), 0)
        tail = jnp.where(line == 0, high, jnp.where(line == 1, low, 0.0)).astype(bf16)
        for rel, out in enumerate((kept_ref, sent_ref.at[0], passed_ref, sent_ref.at[1])):
            at = pl.multiple_of((mine ^ rel) * quarter, quarter)
            out[0:quarter] = all_ref[pl.ds(at, quarter), :]
            out[quarter : quarter + 16] = tail

    dn1_parts = run(
        norm_back_body,
        [
            ((quarter + 16, length), bf16),
            ((quarter + 16, length), bf16),
            ((2, quarter + 16, length), bf16),
        ],
        (me, dq, dk, dv, wq_t, wk_t, wv_t, x_full, small),
        "norm_back",
        us=1.5,
        scratch=[pltpu.VMEM((width, length), bf16)],
    )
    dn1_parts = scatter_sum(*dn1_parts)

    def tokens_body(kept_ref, beside_ref, across_ref, dh_ref, tok_ref, r1_ref, c_ref, out_ref):
        total = kept_ref[...].astype(f32) + beside_ref[0].astype(f32)
        total = total + across_ref[...].astype(f32)
        dn1 = total[0:quarter]
        dot = total[quarter : quarter + 1] + total[quarter + 1 : quarter + 2]
        one = r1_ref[...]
        gain = spread_row(c_ref[rows : rows + extra], experts, length)
        x = tok_ref[...].astype(f32)
        out_ref[...] = (
            dh_ref[...].astype(f32) + one * gain * dn1 - x * (one * one * one / width) * dot
        ).astype(bf16)

    (grad_tokens,) = run(
        tokens_body,
        [((quarter, length), bf16)],
        (*dn1_parts, dh_own, tok_t, r1, cot_pieces[0]),
        "tokens_back",
        us=0.5,
    )

    def out_rows_body(me_ref, h_ref, aux_ref, y_ref, o0, o1, o2, o3, all_ref):
        mine = me_ref[0] & (ways - 1)
        out = (h_ref[...] + aux_ref[:, LANES - 1 : LANES] * y_ref[...].astype(f32)).astype(bf16)
        eye = (iota((rows, rows), 0) == iota((rows, rows), 1)).astype(bf16)
        all_ref[...] = mm_tn(out, eye).astype(bf16)
        for rel, piece in enumerate((o0, o1, o2, o3)):
            at = pl.multiple_of((mine ^ rel) * quarter, quarter)
            piece[...] = all_ref[pl.ds(at, quarter), :]

    lo = run(
        out_rows_body,
        [((quarter, rows), bf16)] * ways,
        (me, h_rows, aux, y_rows),
        "layer_rows",
        us=0.5,
        scratch=[pltpu.VMEM((width, rows), bf16)],
    )
    lo = [lo[0]] + [swap(lo[rel], "tp", rel) for rel in range(1, ways)]

    def out_body(dest_ref, l0, l1, l2, l3, out_ref):
        dest = dest_ref[...]
        total = jnp.zeros((quarter, length), f32)
        for rel, piece in enumerate((l0, l1, l2, l3)):
            hot = (iota((rows, length), 0) + rel * rows == dest).astype(bf16)
            total = total + mm(piece[...], hot)
        out_ref[...] = total.astype(bf16)

    (layer_out,) = run(
        out_body, [((quarter, length), bf16)], (dest_row, *lo), "layer_out", us=0.5
    )

    few = few.astype(f32)
    few = few + swap(few, "tp", 1)
    few_other = swap(few, "tp", 2)

    def unpack_body(
        me_ref,
        am_ref,
        ao_ref,
        bm_ref,
        bo_ref,
        few_ref,
        other_ref,
        gq_ref,
        gk_ref,
        gv_ref,
        go_ref,
        router_ref,
        g1_ref,
        g2_ref,
        table_ref,
        a_ref,
        b_ref,
    ):
        mine = me_ref[0] & (ways - 1)
        place = me_ref[0] >> shift
        for order, ref, first, second in (
            (order_a, a_ref, am_ref, ao_ref),
            (order_b, b_ref, bm_ref, bo_ref),
        ):
            for at in range(owners):
                src, line = (first, at) if at < owners // 2 else (second, at - owners // 2)
                ref[rel_of(at, order) ^ place] = src[line * chunk : (line + 1) * chunk]
        for c in range(owners):
            low, high = c * chunk, (c + 1) * chunk
            for ref, outs in ((a_ref, (gq_ref, gk_ref)), (b_ref, (gv_ref, go_ref))):
                if high <= here:
                    outs[0][low:high] = ref[c]
                else:
                    outs[1][low - here : high - here] = ref[c]
        total = few_ref[...] + other_ref[...]
        own = total[:, 0:quarter]
        for t in range(1, ways):
            own = jnp.where(mine == t, total[:, t * quarter : (t + 1) * quarter], own)
        router_ref[...] = own[0:experts].astype(bf16)
        g2_ref[...] = own[experts : experts + 1].astype(bf16)
        g1_ref[...] = own[experts + 1 : experts + 2].astype(bf16)
        lines = total[experts + 2 : experts + 2 + heads]
        table = lines[:, 0:bins]
        for t in range(1, ways):
            table = jnp.where(mine == t, lines[:, t * bins : (t + 1) * bins], table)
        table_ref[...] = table.astype(bf16)

    gq, gk, gv, go, g_router, g_one, g_two, g_table = run(
        unpack_body,
        [
            ((here, width), bf16),
            ((here, width), bf16),
            ((here, width), bf16),
            ((here, width), bf16),
            ((experts, quarter), bf16),
            ((1, quarter), bf16),
            ((1, quarter), bf16),
            ((heads, bins), bf16),
        ],
        (me, a_mine, a_other, b_mine, b_other, few, few_other),
        "unpack",
        us=1.0,
        scratch=[
            pltpu.VMEM((owners, chunk, width), bf16),
            pltpu.VMEM((owners, chunk, width), bf16),
        ],
    )
    return (
        layer_out.T,
        grad_tokens.T,
        gq.T,
        gk.T,
        gv.T,
        go,
        g_table.T,
        g_router.T,
        grad_in,
        grad_out,
        g_one[0],
        g_two[0],
    )


def solution(mesh):
    placed = (
        P("exp", "tp"),
        P(None, "tp"),
        P(None, "tp"),
        P(None, "tp"),
        P("tp", None),
        P(None, "tp"),
        P("tp", None),
        P("exp", None, "tp"),
        P("exp", "tp", None),
        P("tp"),
        P("tp"),
        P("exp", None),
        P("exp", None),
        P(),
        P("exp", "tp"),
    )
    return jax.shard_map(
        local,
        mesh=mesh,
        in_specs=placed,
        out_specs=(
            P("exp", "tp"),
            P("exp", "tp"),
            P(None, "tp"),
            P(None, "tp"),
            P(None, "tp"),
            P("tp", None),
            P(None, "tp"),
            P("tp", None),
            P("exp", None, "tp"),
            P("exp", "tp", None),
            P("tp"),
            P("tp"),
        ),
        check_vma=False,
    )
```

```python
import math

import jax
import jax.numpy as jnp
from jax import lax
from jax.experimental import pallas as pl
from jax.experimental.pallas import tpu as pltpu
from jax.sharding import PartitionSpec as P

HD = 64
EPSILON = 1e-06
NEG_FILL = -1e30
HIGHEST = lax.Precision.HIGHEST
LANES = 128
f32 = jnp.float32
bf16 = jnp.bfloat16
VMEM = pl.BlockSpec(memory_space=pltpu.VMEM)
SMEM = pl.BlockSpec(memory_space=pltpu.SMEM)


class Far:
    def __init__(self, value):
        self.value = value


class Loaded:
    def __init__(self, copy, held):
        self.copy, self.held = copy, held

    def wait(self):
        if self.copy is not None:
            self.copy.wait()
            self.copy = None

    def __getitem__(self, index):
        self.wait()
        return self.held[index]


class Stored:
    def __init__(self, copy, held):
        self.copy, self.held, self.started = copy, held, False

    def __setitem__(self, index, value):
        self.held[index] = value

    def __getitem__(self, index):
        return self.held[index]

    def send(self):
        if not self.started:
            self.started = True
            self.copy.start()


def run(body, outs, args, name, us=1.0, scratch=(), limit=16):
    far_in = [isinstance(a, Far) for a in args]
    args = [a.value if isinstance(a, Far) else a for a in args]
    far_out = [len(o) == 3 for o in outs]
    bufs = [pltpu.VMEM(a.shape, a.dtype) for a, far in zip(args, far_in) if far]
    bufs += [pltpu.VMEM(o[0], o[1]) for o, far in zip(outs, far_out) if far]
    n_in, n_out, n_own = len(args), len(outs), len(scratch)
    hbm = pl.BlockSpec(memory_space=pltpu.HBM)
    specs = [
        SMEM if a.shape == (1,) and a.dtype == jnp.int32 else hbm if far else VMEM
        for a, far in zip(args, far_in)
    ]
    moved = sum(a.size * a.dtype.itemsize for a in args)
    moved += sum(math.prod(o[0]) * jnp.dtype(o[1]).itemsize for o in outs)

    def wrapped(*refs):
        ins, results = refs[:n_in], refs[n_in : n_in + n_out]
        own = refs[n_in + n_out : n_in + n_out + n_own]
        held = refs[n_in + n_out + n_own :]
        given, at = [], 0
        for ref, far in zip((*ins, *results), (*far_in, *far_out)):
            if not far:
                given.append(ref)
                continue
            if len(given) < n_in:
                copy = pltpu.make_async_copy(ref, held[at], held[-1].at[at])
                copy.start()
                given.append(Loaded(copy, held[at]))
            else:
                copy = pltpu.make_async_copy(held[at], ref, held[-1].at[at])
                given.append(Stored(copy, held[at]))
            at += 1
        body(*given, *own)
        for g in given:
            if isinstance(g, Stored):
                g.send()
        for g in given:
            if isinstance(g, Stored):
                g.copy.wait()
            elif isinstance(g, Loaded):
                g.wait()

    sems = [pltpu.SemaphoreType.DMA((len(bufs),))] if bufs else []
    return pl.pallas_call(
        wrapped,
        out_shape=[jax.ShapeDtypeStruct(o[0], o[1]) for o in outs],
        in_specs=specs,
        out_specs=[hbm if far else VMEM for far in far_out],
        scratch_shapes=[*scratch, *bufs, *sems],
        compiler_params=pltpu.CompilerParams(vmem_limit_bytes=limit * 2**20),
        cost_estimate=pl.CostEstimate(
            flops=int(us * 1.1e9), bytes_accessed=moved, transcendentals=0
        ),
        name=name,
    )(*args)


def swap(value, axis, mask):
    size = lax.axis_size(axis)
    return lax.ppermute(value, axis, [(i, i ^ mask) for i in range(size)])


def after(value, *others):
    return lax.optimization_barrier((value, *others))[0]


def mm(left, right):
    return jnp.dot(left, right, preferred_element_type=f32)


def mm_tn(left, right):
    return lax.dot_general(left, right, (((0,), (0,)), ((), ())), preferred_element_type=f32)


def mm_nt(left, right, precision=None):
    return lax.dot_general(
        left, right, (((1,), (1,)), ((), ())), precision=precision, preferred_element_type=f32
    )


def iota(shape, dim):
    return lax.broadcasted_iota(jnp.int32, shape, dim)


def absolute(pieces, me, place):
    picked = pieces[0]
    for rel in range(1, len(pieces)):
        picked = jnp.where((me ^ rel) == place, pieces[rel], picked)
    return picked


def split_low(value):
    high = value.astype(bf16)
    return high.astype(f32), value - high.astype(f32)


def two_lanes(value, count):
    high, low = split_low(value)
    lane = iota((value.shape[0], count), 1)
    return jnp.where(lane == 0, high, jnp.where(lane == 1, low, 0.0)).astype(bf16)


def gather_pieces(value):
    across = swap(value, "tp", 2)
    beside = swap(value, "tp", 1)
    return value, beside, across, swap(across, "tp", 1)


def scatter_sum(kept, passed, sent):
    came = swap(sent, "tp", 1)
    half = passed + came[1]
    return kept, came, swap(half, "tp", 2), half


def chain_sum(keep, send, masks, tail):
    body = keep.shape[0] - tail
    total = keep
    for at, mask in enumerate(masks):
        total = keep + swap(send, "exp", mask)
        if at + 1 < len(masks):
            half = body // 2
            keep = total[:half]
            if tail:
                keep = jnp.concatenate([keep, total[body:]], axis=0)
            send = total[half:]
            body = half
    mine, few = total[:body], total[body:]
    for mask in masks[:0:-1]:
        mine = jnp.concatenate([mine, swap(mine, "exp", mask)], axis=0)
    return mine, swap(mine, "exp", masks[0]), few


def rel_of(place, masks):
    top = len(masks) - 1
    return sum(mask for at, mask in enumerate(masks) if (place >> (top - at)) & 1)


def local(
    tokens,
    w_query,
    w_key,
    w_value,
    w_output,
    bias_table,
    w_router,
    w_in,
    w_out,
    gain_attn,
    gain_ffn,
    routes,
    segments,
    buckets,
    cotangent,
):
    length, quarter = tokens.shape
    ways = lax.axis_size("tp")
    owners = lax.axis_size("exp")
    width = quarter * ways
    here = w_query.shape[1]
    heads = here // HD
    experts = w_router.shape[1]
    bins = bias_table.shape[0]
    hidden_here = w_in.shape[2]
    capacity = max(2, length // owners * 9 // 8)
    per = -(-capacity // ways)
    while experts * per % LANES:
        per += 1
    rows = experts * per
    span = 2 * length
    extra = -(-(experts + 2) // 16) * 16
    few_rows = -(-(experts + 2 + heads) // 16) * 16
    me = lax.axis_index(("exp", "tp")).astype(jnp.int32)[None]
    bits = [1 << b for b in range(owners.bit_length() - 1)]
    order_a = bits
    order_b = bits[1:] + bits[:1]
    shift = ways.bit_length() - 1

    tok_t = tokens.T
    wq_t, wk_t, wv_t = w_query.T, w_key.T, w_value.T

    tok_pieces = gather_pieces(tok_t)

    def slot_body(
        me_ref, route_ref, cot_ref, router_ref, g1_ref, g2_ref, *outs
    ):
        drow_ref, drow_far, dcol_ref, cots_ref, d_ref = outs
        mine = me_ref[0] & (ways - 1)
        row = route_ref[...]
        above = iota((length, length), 0)
        along = iota((length, length), 1)
        col = jnp.sum(jnp.where(above == along, row, 0), axis=1, keepdims=True)
        same = col == row

        def dest(slot, expert):
            chunk = jnp.zeros_like(slot)
            for t in range(1, ways):
                chunk = chunk + (slot >= t * per).astype(jnp.int32)
            return (chunk ^ mine) * rows + expert * per + slot - chunk * per

        slot_row = jnp.sum(jnp.where(same & (above < along), 1, 0), axis=0, keepdims=True)
        slot_col = jnp.sum(jnp.where(same & (along < above), 1, 0), axis=1, keepdims=True)
        dest_row = dest(slot_row, row)
        drow_ref[...] = dest_row
        drow_far[...] = dest_row
        drow_far.send()
        dcol_ref[...] = dest(slot_col, col)
        dcol_ref.send()
        cot = cot_ref[...]
        line = iota((extra - experts, quarter), 0)
        gains = jnp.where(
            line == 0,
            g1_ref[...].astype(f32),
            jnp.where(line == 1, g2_ref[...].astype(f32), 0.0),
        )
        few = jnp.concatenate([router_ref[...].astype(f32), gains], axis=0).astype(bf16)
        for rel in range(ways):
            hot = (iota((rows, length), 0) + rel * rows == dest_row).astype(bf16)
            piece = mm_nt(hot, cot).astype(bf16)
            cots_ref[rel, 0:rows] = piece
            cots_ref[rel, rows : rows + extra] = few
            d_ref[:, rel * quarter : (rel + 1) * quarter] = piece

    dest_row, dest_far, dest_col, cots, d_send = run(
        slot_body,
        [
            ((1, length), jnp.int32),
            ((1, length), jnp.int32, True),
            ((length, 1), jnp.int32, True),
            ((ways, rows + extra, quarter), bf16),
            ((rows, width), bf16),
        ],
        (
            me,
            Far(routes.T),
            Far(cotangent.T),
            Far(w_router.T),
            gain_attn[None],
            gain_ffn[None],
        ),
        "slots",
        us=0.7,
    )
    cot_pieces = [cots[0]] + [swap(cots[rel], "tp", rel) for rel in range(1, ways)]

    def over_experts(value):
        blocks = value.reshape(experts, per, value.shape[1])
        moved = lax.all_to_all(blocks, "exp", split_axis=0, concat_axis=0, tiled=True)
        return moved.reshape(rows, value.shape[1])

    bucket_row = jnp.pad(buckets, (0, span - buckets.shape[0]), constant_values=-1)[None]

    def spread_row(few, line, count):
        pick = (iota((few.shape[0], count), 0) == line).astype(bf16)
        return mm_tn(few, pick)

    def attend_body(
        me_ref,
        t0,
        t1,
        t2,
        t3,
        c0,
        c1,
        c2,
        c3,
        wq_ref,
        wk_ref,
        wv_ref,
        wo_ref,
        table_ref,
        bucket_ref,
        seg_ref,
        dest_ref,
        x_ref,
        small_ref,
        small_far,
        r1_ref,
        n1_ref,
        q_ref,
        k_ref,
        v_ref,
        p_ref,
        attn_ref,
        kept_ref,
        passed_ref,
        sent_ref,
        xrow_ref,
    ):
        mine = me_ref[0] & (ways - 1)
        for rel, piece in enumerate((t0, t1, t2, t3)):
            at = pl.multiple_of((mine ^ rel) * quarter, quarter)
            x_ref[pl.ds(at, quarter), :] = piece[...]
        pieces = [c[rows : rows + extra] for c in (c0, c1, c2, c3)]
        small = jnp.concatenate([absolute(pieces, mine, t) for t in range(ways)], axis=1)
        small_ref[...] = small
        small_far[...] = small
        small_far.send()
        x_low = x_ref[...]
        x_ref.send()
        x = x_low.astype(f32)
        r1 = lax.rsqrt(jnp.mean(x * x, axis=0, keepdims=True) + EPSILON)
        r1_ref[...] = r1
        r1_ref.send()
        n1 = (x * r1 * spread_row(small, experts, length)).astype(bf16)
        n1_ref[...] = n1
        n1_ref.send()
        q = mm(wq_ref[...], n1).astype(bf16)
        k = mm(wk_ref[...], n1).astype(bf16)
        v = mm(wv_ref[...], n1).astype(bf16)
        q_ref[...] = q
        k_ref[...] = k
        v_ref[...] = v
        q_ref.send()
        k_ref.send()
        v_ref.send()
        hot = (iota((bins, span), 0) == bucket_ref[...]).astype(bf16)
        offsets = mm(table_ref[...], hot)
        above = iota((length, length), 0)
        along = iota((length, length), 1)
        seg_row = seg_ref[...]
        seg_col = jnp.sum(jnp.where(above == along, seg_row, 0), axis=1, keepdims=True)
        same = seg_col == seg_row
        for h in range(heads):
            part = slice(h * HD, (h + 1) * HD)
            spread = jnp.broadcast_to(offsets[h : h + 1], (length, span))
            bias = pltpu.roll(spread, length + 1, 1, stride=1, stride_axis=0)[:, :length]
            s = jnp.where(same, mm_tn(k[part], q[part]) + bias, NEG_FILL)
            e = jnp.exp(s - jnp.max(s, axis=0, keepdims=True))
            p = (e / jnp.sum(e, axis=0, keepdims=True)).astype(bf16)
            p_ref[h] = p
            attn_ref[part] = mm(v[part], p).astype(bf16)
        p_ref.send()
        attn = attn_ref[...]
        attn_ref.send()
        dest = dest_ref[...]
        wo = wo_ref[...]
        for rel, out in enumerate((kept_ref, sent_ref.at[0], passed_ref, sent_ref.at[1])):
            hot = (iota((rows, length), 0) + rel * rows == dest).astype(bf16)
            out[...] = mm(mm_nt(hot, attn).astype(bf16), wo).astype(bf16)
            if rel == 0:
                xrow_ref[...] = mm_nt(hot, x_low).astype(bf16)

    x_full, small, small_far, r1, n1, q, k, v, probs, attn, *o_parts, x_rows = run(
        attend_body,
        [
            ((width, length), bf16, True),
            ((extra, width), bf16),
            ((extra, width), bf16, True),
            ((1, length), f32, True),
            ((width, length), bf16, True),
            ((here, length), bf16, True),
            ((here, length), bf16, True),
            ((here, length), bf16, True),
            ((heads, length, length), bf16, True),
            ((here, length), bf16, True),
            ((rows, width), bf16),
            ((rows, width), bf16),
            ((2, rows, width), bf16),
            ((rows, width), bf16),
        ],
        (
            me,
            *tok_pieces,
            *cot_pieces,
            wq_t,
            wk_t,
            wv_t,
            w_output,
            bias_table.T,
            bucket_row,
            segments,
            dest_row,
        ),
        "attend",
        us=4.0,
        limit=24,
    )
    o_kept, o_beside, o_across, none = scatter_sum(*o_parts)

    d_arrived = over_experts(d_send)
    o_across, d_arrived = lax.optimization_barrier((o_across, d_arrived))
    d_pieces = gather_pieces(d_arrived)

    def route_body(
        me_ref,
        kept_ref,
        beside_ref,
        across_ref,
        xrow_ref,
        small_ref,
        c0,
        c1,
        c2,
        c3,
        h_ref,
        aux_ref,
        dout_ref,
        send_ref,
    ):
        mine = me_ref[0] & (ways - 1)
        o = kept_ref[...].astype(f32) + beside_ref[0].astype(f32) + across_ref[...].astype(f32)
        h = xrow_ref[...].astype(f32) + o
        h_ref[...] = h
        r2 = lax.rsqrt(jnp.mean(h * h, axis=-1, keepdims=True) + EPSILON)
        gain = small_ref[experts + 1 : experts + 2].astype(f32)
        n2 = h * r2 * gain
        logits = mm_nt(n2, small_ref[0:experts].astype(f32), HIGHEST)
        e = jnp.exp(logits - jnp.max(logits, axis=-1, keepdims=True))
        p = e / jnp.sum(e, axis=-1, keepdims=True)
        owner = iota((rows, experts), 0) - iota((rows, experts), 1) * per
        own = (owner >= 0) & (owner < per)
        g = jnp.sum(jnp.where(own, p, 0.0), axis=-1, keepdims=True)
        pieces = [c[0:rows] for c in (c0, c1, c2, c3)]
        dout_ref[...] = jnp.concatenate([absolute(pieces, mine, t) for t in range(ways)], axis=1)
        aux_ref[...] = jnp.zeros((rows, LANES), f32)
        aux_ref[:, 0:experts] = p
        aux_ref[:, LANES - 2 : LANES - 1] = r2
        aux_ref[:, LANES - 1 : LANES] = g
        h_ref.send()
        aux_ref.send()
        dout_ref.send()
        send_ref[:, 0:width] = n2.astype(bf16)
        send_ref[:, width : width + LANES] = two_lanes(g, LANES)

    h_rows, aux, dout_rows, send = run(
        route_body,
        [
            ((rows, width), f32, True),
            ((rows, LANES), f32, True),
            ((rows, width), bf16, True),
            ((rows, width + LANES), bf16),
        ],
        (me, o_kept, o_beside, o_across, x_rows, small, *cot_pieces),
        "route",
        us=0.8,
    )
    arrived, *d_pieces = lax.optimization_barrier((over_experts(send), *d_pieces))
    arrived = gather_pieces(arrived)

    def expert_body(me_ref, a0, a1, a2, a3, d0, d1, d2, d3, win_ref, wout_ref, *outs):
        u_ref, dy_ref, act_ref, dz_ref, kept_ref, passed_ref, sent_ref = outs
        mine = me_ref[0] & (ways - 1)
        douts = (d0, d1, d2, d3)
        for rel, a in enumerate((a0, a1, a2, a3)):
            part = slice(rel * rows, (rel + 1) * rows)
            u_ref[part] = a[:, 0:width]
            g = a[:, width : width + 1].astype(f32) + a[:, width + 1 : width + 2].astype(f32)
            pieces = []
            for src in range(ways):
                at = (rel ^ src) * quarter
                pieces.append(douts[src][:, at : at + quarter])
            dout = jnp.concatenate([absolute(pieces, mine, t) for t in range(ways)], axis=1)
            dy_ref[part] = (g * dout.astype(f32)).astype(bf16)
        u_ref.send()
        dy_ref.send()
        u = u_ref[...]
        dy = dy_ref[...]
        z = mm(u, win_ref[0])
        c = math.sqrt(2.0 / math.pi)
        t = jnp.tanh(c * (z + 0.044715 * z * z * z))
        act = (0.5 * z * (1.0 + t)).astype(bf16)
        act_ref[...] = act
        act_ref.send()
        slope = 0.5 * (1.0 + t) + 0.5 * z * (1.0 - t * t) * (c * (1.0 + 3 * 0.044715 * z * z))
        dact = mm_nt(dy, wout_ref[0])
        dot = jnp.sum(dact * act.astype(f32), axis=-1, keepdims=True)
        dz = (dact * slope).astype(bf16)
        dz_ref[...] = dz
        dz_ref.send()
        du = mm_nt(dz, win_ref[0]).astype(bf16)
        tail = two_lanes(dot, LANES)
        for rel, out in enumerate((kept_ref, sent_ref.at[0], passed_ref, sent_ref.at[1])):
            out[:, 0:width] = du[rel * rows : (rel + 1) * rows]
            out[:, width : width + LANES] = tail[rel * rows : (rel + 1) * rows]

    u_all, dy_all, act, dz, *du_parts = run(
        expert_body,
        [
            ((ways * rows, width), bf16, True),
            ((ways * rows, width), bf16, True),
            ((ways * rows, hidden_here), bf16, True),
            ((ways * rows, hidden_here), bf16, True),
            ((rows, width + LANES), bf16),
            ((rows, width + LANES), bf16),
            ((2, rows, width + LANES), bf16),
        ],
        (me, *arrived, *d_pieces, w_in, w_out),
        "expert",
        us=4.0,
        limit=24,
    )
    du_kept, du_beside, du_across, du_half = scatter_sum(*du_parts)
    du_sum = du_kept + du_beside[0] + du_across
    du_rows = over_experts(du_sum)

    def value_body(act_ref, wout_ref, kept_ref, passed_ref, sent_ref):
        y = mm(act_ref[...], wout_ref[0]).astype(bf16)
        for rel, out in enumerate((kept_ref, sent_ref.at[0], passed_ref, sent_ref.at[1])):
            out[...] = y[rel * rows : (rel + 1) * rows]

    y_parts = run(
        value_body,
        [((rows, width), bf16), ((rows, width), bf16), ((2, rows, width), bf16)],
        (Far(after(act, du_half)), w_out),
        "value",
        us=0.8,
    )
    y_kept, y_passed, y_sent = y_parts
    y_beside = swap(y_sent, "tp", 1)
    y_across = swap(after(y_passed + y_beside[1], du_sum), "tp", 2)
    y_sum = y_kept + y_beside[0] + y_across

    def weights_body(u_ref, dy_ref, act_ref, dz_ref, gin_ref, gout_ref):
        gin_ref[0] = mm_tn(u_ref[...], dz_ref[...]).astype(bf16)
        gout_ref[0] = mm_tn(act_ref[...], dy_ref[...]).astype(bf16)

    grad_in, grad_out = run(
        weights_body,
        [((1, width, hidden_here), bf16), ((1, hidden_here, width), bf16)],
        (Far(u_all), Far(dy_all), Far(act), Far(after(dz, du_sum))),
        "expert_weights",
        us=2.5,
    )
    y_rows = over_experts(y_sum)
    du_rows, grad_in, grad_out = lax.optimization_barrier((du_rows, grad_in, grad_out))

    def back_body(du_ref, h_ref, aux_ref, dout_ref, small_ref, do_ref, parts_ref):
        du = du_ref[:, 0:width].astype(f32)
        gg = du_ref[:, width : width + 1].astype(f32)
        gg = gg + du_ref[:, width + 1 : width + 2].astype(f32)
        h = h_ref[...]
        p = aux_ref[:, 0:experts]
        r2 = aux_ref[:, LANES - 2 : LANES - 1]
        gain = small_ref[experts + 1 : experts + 2].astype(f32)
        router = small_ref[0:experts].astype(f32)
        owner = iota((rows, experts), 0) - iota((rows, experts), 1) * per
        own = ((owner >= 0) & (owner < per)).astype(f32)
        dlogits = gg * (own - p)
        dn2 = du + lax.dot_general(
            dlogits, router, (((1,), (0,)), ((), ())), precision=HIGHEST, preferred_element_type=f32
        )
        hr = h * r2
        n2 = hr * gain
        inner = jnp.sum(dn2 * gain * h, axis=-1, keepdims=True)
        dh = dout_ref[...].astype(f32) + r2 * gain * dn2 - hr * (r2 * r2 / width) * inner
        do_ref[...] = dh.astype(bf16)
        parts_ref[...] = jnp.zeros((few_rows, width), f32)
        parts_ref[0:experts] = lax.dot_general(
            dlogits, n2, (((0,), (0,)), ((), ())), precision=HIGHEST, preferred_element_type=f32
        )
        parts_ref[experts : experts + 1] = jnp.sum(dn2 * hr, axis=0, keepdims=True)

    do_rows, few_parts = run(
        back_body,
        [((rows, width), bf16), ((few_rows, width), f32, True)],
        (du_rows, h_rows, aux, dout_rows, small_far),
        "residual_back",
        us=2.0,
    )
    do_pieces = gather_pieces(do_rows)

    chunk = 2 * here // owners

    def attend_back_body(
        me_ref,
        d0,
        d1,
        d2,
        d3,
        drow_ref,
        dcol_ref,
        wo_ref,
        attn_ref,
        q_ref,
        k_ref,
        v_ref,
        p_ref,
        n1_ref,
        wq_ref,
        wk_ref,
        wv_ref,
        x_ref,
        small_ref,
        few_ref,
        bucket_ref,
        own_ref,
        akeep_ref,
        asend_ref,
        bkeep_ref,
        bsend_ref,
        kept_ref,
        passed_ref,
        sent_ref,
        a_ref,
        b_ref,
        dq_ref,
        dk_ref,
        dv_ref,
        all_ref,
    ):
        mine = me_ref[0] & (ways - 1)
        place = me_ref[0] >> shift
        stack = jnp.concatenate([d[...] for d in (d0, d1, d2, d3)], axis=0)
        hot_t = (iota((length, ways * rows), 1) == dcol_ref[...]).astype(bf16)
        do = mm(hot_t, stack).astype(bf16)
        own = stack[:, 0:quarter]
        for t in range(1, ways):
            own = jnp.where(mine == t, stack[:, t * quarter : (t + 1) * quarter], own)
        hot = (iota((ways * rows, length), 0) == drow_ref[...]).astype(bf16)
        own_ref[...] = mm_tn(own, hot).astype(bf16)
        own_ref.send()
        wo = wo_ref[...]
        da = mm_nt(wo, do).astype(bf16)
        hot = (iota((bins, span), 0) == bucket_ref[...]).astype(f32)
        flip = (iota((length, length), 0) + iota((length, length), 1) == length - 1).astype(bf16)
        tables = []
        for h in range(heads):
            part = slice(h * HD, (h + 1) * HD)
            p_low = p_ref[h]
            p = p_low.astype(f32)
            dp = mm_tn(v_ref[part], da[part])
            dv_ref[part] = mm_nt(da[part], p_low).astype(bf16)
            inner = jnp.sum(p * dp, axis=0, keepdims=True)
            ds = (p * (dp - inner)).astype(bf16)
            dq_ref[part] = mm(k_ref[part], ds).astype(bf16)
            dk_ref[part] = mm_nt(q_ref[part], ds).astype(bf16)
            flipped = mm(flip, ds)
            flipped = jnp.concatenate([flipped, jnp.zeros_like(flipped)], axis=1)
            offsets = pltpu.roll(flipped, 0, 1, stride=1, stride_axis=0)
            offsets = jnp.sum(offsets, axis=0, keepdims=True)
            tables.append(mm_nt(offsets, hot, HIGHEST))
        n1 = n1_ref[...]
        gq = mm_nt(dq_ref[...], n1)
        gk = mm_nt(dk_ref[...], n1)
        gv = mm_nt(dv_ref[...], n1)
        back = gq * wq_ref[...].astype(f32) + gk * wk_ref[...].astype(f32)
        back = jnp.sum(back + gv * wv_ref[...].astype(f32), axis=0, keepdims=True)
        gain = small_ref[experts : experts + 1].astype(f32)
        gwo = mm(attn_ref[...], do)
        for c in range(owners):
            for total, ref in (((gq, gk), a_ref), ((gv, gwo), b_ref)):
                low, high = c * chunk, (c + 1) * chunk
                picked = total[0][low:high] if high <= here else total[1][low - here : high - here]
                ref[c] = picked.astype(bf16)
        tail = (owners // 2) * chunk
        for order, ref, keep, send in (
            (order_a, a_ref, akeep_ref, asend_ref),
            (order_b, b_ref, bkeep_ref, bsend_ref),
        ):
            for at in range(owners):
                out, line = (keep, at) if at < owners // 2 else (send, at - owners // 2)
                out[line * chunk : (line + 1) * chunk] = ref[rel_of(at, order) ^ place]
        few = few_ref[...]
        line = iota((few_rows, 1), 0)
        few = few + jnp.where(line == experts + 1, back / gain, 0.0)
        wide = jnp.concatenate(
            [jnp.concatenate([tables[h] * (mine == t).astype(f32) for t in range(ways)], axis=1)
             for h in range(heads)],
            axis=0,
        )
        pad = jnp.zeros((heads, width - ways * bins), f32)
        wide = jnp.concatenate([wide, pad], axis=1)
        for h in range(heads):
            few = few + jnp.where(line == experts + 2 + h, wide[h : h + 1], 0.0)
        few = few.astype(bf16)
        akeep_ref[tail : tail + few_rows] = few
        asend_ref[tail : tail + few_rows] = few
        dn1 = mm_tn(wq_ref[...], dq_ref[...])
        dn1 = dn1 + mm_tn(wk_ref[...], dk_ref[...])
        dn1 = dn1 + mm_tn(wv_ref[...], dv_ref[...])
        all_ref[...] = dn1.astype(bf16)
        gain = spread_row(small_ref[...], experts, length)
        dot = jnp.sum(dn1 * gain * x_ref[...].astype(f32), axis=0, keepdims=True)
        high, low = split_low(dot)
        line = iota((16, length), 0)
        tail = jnp.where(line == 0, high, jnp.where(line == 1, low, 0.0)).astype(bf16)
        for rel, out in enumerate((kept_ref, sent_ref.at[0], passed_ref, sent_ref.at[1])):
            at = pl.multiple_of((mine ^ rel) * quarter, quarter)
            out[0:quarter] = all_ref[pl.ds(at, quarter), :]
            out[quarter : quarter + 16] = tail

    side = (owners // 2) * chunk
    dh_own, a_keep, a_send, b_keep, b_send, *dn1_parts = run(
        attend_back_body,
        [
            ((quarter, length), bf16, True),
            ((side + few_rows, width), bf16),
            ((side + few_rows, width), bf16),
            ((side, width), bf16),
            ((side, width), bf16),
            ((quarter + 16, length), bf16),
            ((quarter + 16, length), bf16),
            ((2, quarter + 16, length), bf16),
        ],
        (
            me,
            *do_pieces,
            Far(dest_far),
            Far(dest_col),
            Far(w_output),
            Far(attn),
            Far(q),
            Far(k),
            Far(v),
            Far(probs),
            Far(n1),
            Far(wq_t),
            Far(wk_t),
            Far(wv_t),
            Far(x_full),
            Far(small_far),
            Far(few_parts),
            Far(bucket_row),
        ),
        "attend_back",
        us=6.0,
        scratch=[
            pltpu.VMEM((owners, chunk, width), bf16),
            pltpu.VMEM((owners, chunk, width), bf16),
            pltpu.VMEM((here, length), bf16),
            pltpu.VMEM((here, length), bf16),
            pltpu.VMEM((here, length), bf16),
            pltpu.VMEM((width, length), bf16),
        ],
        limit=32,
    )

    a_mine, a_other, few = chain_sum(a_keep, a_send, order_a, few_rows)
    b_mine, b_other, none = chain_sum(b_keep, b_send, order_b, 0)

    *dn1_parts, none = scatter_sum(*dn1_parts)

    def tokens_body(
        me_ref, kept_ref, beside_ref, across_ref, dh_ref, tok_ref, r1_ref, small_ref, out_ref
    ):
        mine = me_ref[0] & (ways - 1)
        total = kept_ref[...].astype(f32) + beside_ref[0].astype(f32)
        total = total + across_ref[...].astype(f32)
        dn1 = total[0:quarter]
        dot = total[quarter : quarter + 1] + total[quarter + 1 : quarter + 2]
        one = r1_ref[...]
        small = small_ref[...]
        own = small[:, 0:quarter]
        for t in range(1, ways):
            own = jnp.where(mine == t, small[:, t * quarter : (t + 1) * quarter], own)
        gain = spread_row(own, experts, length)
        x = tok_ref[...].astype(f32)
        out_ref[...] = (
            dh_ref[...].astype(f32) + one * gain * dn1 - x * (one * one * one / width) * dot
        ).astype(bf16)

    (grad_tokens,) = run(
        tokens_body,
        [((quarter, length), bf16)],
        (me, *dn1_parts, Far(dh_own), Far(tok_t), Far(r1), Far(small_far)),
        "tokens_back",
        us=0.5,
    )

    def out_rows_body(me_ref, h_ref, aux_ref, y_ref, o0, o1, o2, o3, all_ref):
        mine = me_ref[0] & (ways - 1)
        out = (h_ref[...] + aux_ref[:, LANES - 1 : LANES] * y_ref[...].astype(f32)).astype(bf16)
        eye = (iota((rows, rows), 0) == iota((rows, rows), 1)).astype(bf16)
        all_ref[...] = mm_tn(out, eye).astype(bf16)
        for rel, piece in enumerate((o0, o1, o2, o3)):
            at = pl.multiple_of((mine ^ rel) * quarter, quarter)
            piece[...] = all_ref[pl.ds(at, quarter), :]

    lo = run(
        out_rows_body,
        [((quarter, rows), bf16)] * ways,
        (me, Far(h_rows), Far(aux), y_rows),
        "layer_rows",
        us=0.5,
        scratch=[pltpu.VMEM((width, rows), bf16)],
    )
    lo = [lo[0]] + [swap(lo[rel], "tp", rel) for rel in range(1, ways)]

    def out_body(dest_ref, l0, l1, l2, l3, out_ref):
        dest = dest_ref[...]
        total = jnp.zeros((quarter, length), f32)
        for rel, piece in enumerate((l0, l1, l2, l3)):
            hot = (iota((rows, length), 0) + rel * rows == dest).astype(bf16)
            total = total + mm(piece[...], hot)
        out_ref[...] = total.astype(bf16)

    (layer_out,) = run(
        out_body, [((quarter, length), bf16)], (Far(dest_far), *lo), "layer_out", us=0.5
    )

    few = few.astype(f32)
    few = few + swap(few, "tp", 1)
    few_other = swap(few, "tp", 2)

    def unpack_body(
        me_ref,
        am_ref,
        ao_ref,
        bm_ref,
        bo_ref,
        few_ref,
        other_ref,
        gq_ref,
        gk_ref,
        gv_ref,
        go_ref,
        router_ref,
        g1_ref,
        g2_ref,
        table_ref,
        a_ref,
        b_ref,
    ):
        mine = me_ref[0] & (ways - 1)
        place = me_ref[0] >> shift
        for order, ref, first, second in (
            (order_a, a_ref, am_ref, ao_ref),
            (order_b, b_ref, bm_ref, bo_ref),
        ):
            for at in range(owners):
                src, line = (first, at) if at < owners // 2 else (second, at - owners // 2)
                ref[rel_of(at, order) ^ place] = src[line * chunk : (line + 1) * chunk]
        for c in range(owners):
            low, high = c * chunk, (c + 1) * chunk
            for ref, outs in ((a_ref, (gq_ref, gk_ref)), (b_ref, (gv_ref, go_ref))):
                if high <= here:
                    outs[0][low:high] = ref[c]
                else:
                    outs[1][low - here : high - here] = ref[c]
        total = few_ref[...] + other_ref[...]
        own = total[:, 0:quarter]
        for t in range(1, ways):
            own = jnp.where(mine == t, total[:, t * quarter : (t + 1) * quarter], own)
        router_ref[...] = own[0:experts].astype(bf16)
        g2_ref[...] = own[experts : experts + 1].astype(bf16)
        g1_ref[...] = own[experts + 1 : experts + 2].astype(bf16)
        lines = total[experts + 2 : experts + 2 + heads]
        table = lines[:, 0:bins]
        for t in range(1, ways):
            table = jnp.where(mine == t, lines[:, t * bins : (t + 1) * bins], table)
        table_ref[...] = table.astype(bf16)

    gq, gk, gv, go, g_router, g_one, g_two, g_table = run(
        unpack_body,
        [
            ((here, width), bf16),
            ((here, width), bf16),
            ((here, width), bf16),
            ((here, width), bf16),
            ((experts, quarter), bf16),
            ((1, quarter), bf16),
            ((1, quarter), bf16),
            ((heads, bins), bf16),
        ],
        (me, a_mine, a_other, b_mine, b_other, few, few_other),
        "unpack",
        us=1.0,
        scratch=[
            pltpu.VMEM((owners, chunk, width), bf16),
            pltpu.VMEM((owners, chunk, width), bf16),
        ],
    )
    return (
        layer_out.T,
        grad_tokens.T,
        gq.T,
        gk.T,
        gv.T,
        go,
        g_table.T,
        g_router.T,
        grad_in,
        grad_out,
        g_one[0],
        g_two[0],
    )


def solution(mesh):
    placed = (
        P("exp", "tp"),
        P(None, "tp"),
        P(None, "tp"),
        P(None, "tp"),
        P("tp", None),
        P(None, "tp"),
        P("tp", None),
        P("exp", None, "tp"),
        P("exp", "tp", None),
        P("tp"),
        P("tp"),
        P("exp", None),
        P("exp", None),
        P(),
        P("exp", "tp"),
    )
    return jax.shard_map(
        local,
        mesh=mesh,
        in_specs=placed,
        out_specs=(
            P("exp", "tp"),
            P("exp", "tp"),
            P(None, "tp"),
            P(None, "tp"),
            P(None, "tp"),
            P("tp", None),
            P(None, "tp"),
            P("tp", None),
            P("exp", None, "tp"),
            P("exp", "tp", None),
            P("tp"),
            P("tp"),
        ),
        check_vma=False,
    )
```

```python
import math

import jax
import jax.numpy as jnp
from jax import lax
from jax.experimental import pallas as pl
from jax.experimental.pallas import tpu as pltpu
from jax.sharding import PartitionSpec as P

HD = 64
EPSILON = 1e-06
NEG_FILL = -1e30
HIGHEST = lax.Precision.HIGHEST
LANES = 128
f32 = jnp.float32
bf16 = jnp.bfloat16
VMEM = pl.BlockSpec(memory_space=pltpu.VMEM)
SMEM = pl.BlockSpec(memory_space=pltpu.SMEM)


class Far:
    def __init__(self, value):
        self.value = pltpu.with_memory_space_constraint(value, pltpu.HBM)


class Pin:
    def __init__(self, value):
        self.value = pltpu.with_memory_space_constraint(value, pltpu.VMEM)


class Loaded:
    def __init__(self, copy, held):
        self.copy, self.held = copy, held

    def wait(self):
        if self.copy is not None:
            self.copy.wait()
            self.copy = None

    def __getitem__(self, index):
        self.wait()
        return self.held[index]


def run(body, outs, args, name, us=1.0, scratch=(), limit=16):
    far = [isinstance(a, Far) for a in args]
    args = [a.value if isinstance(a, (Far, Pin)) else a for a in args]
    bufs = [pltpu.VMEM(a.shape, a.dtype) for a, f in zip(args, far) if f]
    n_in, n_out, n_own = len(args), len(outs), len(scratch)
    hbm = pl.BlockSpec(memory_space=pltpu.HBM)
    specs = [
        SMEM if a.shape == (1,) and a.dtype == jnp.int32 else hbm if f else VMEM
        for a, f in zip(args, far)
    ]
    moved = sum(a.size * a.dtype.itemsize for a in args)
    moved += sum(math.prod(o[0]) * jnp.dtype(o[1]).itemsize for o in outs)

    def wrapped(*refs):
        own = refs[n_in + n_out : n_in + n_out + n_own]
        held = refs[n_in + n_out + n_own :]
        given, at = [], 0
        for ref, f in zip(refs[:n_in], far):
            if f:
                copy = pltpu.make_async_copy(ref, held[at], held[-1].at[at])
                copy.start()
                given.append(Loaded(copy, held[at]))
                at += 1
            else:
                given.append(ref)
        body(*given, *refs[n_in : n_in + n_out], *own)
        for g in given:
            if isinstance(g, Loaded):
                g.wait()

    sems = [pltpu.SemaphoreType.DMA((len(bufs),))] if bufs else []
    return pl.pallas_call(
        wrapped,
        out_shape=[
            pltpu.VMEM(o[0], o[1]) if len(o) == 3 else jax.ShapeDtypeStruct(o[0], o[1])
            for o in outs
        ],
        in_specs=specs,
        out_specs=[VMEM] * n_out,
        scratch_shapes=[*scratch, *bufs, *sems],
        compiler_params=pltpu.CompilerParams(vmem_limit_bytes=limit * 2**20),
        cost_estimate=pl.CostEstimate(
            flops=int(us * 1.1e9), bytes_accessed=moved, transcendentals=0
        ),
        name=name,
    )(*args)


def swap(value, axis, mask):
    size = lax.axis_size(axis)
    return lax.ppermute(value, axis, [(i, i ^ mask) for i in range(size)])


def after(value, *others):
    return lax.optimization_barrier((value, *others))[0]


def mm(left, right):
    return jnp.dot(left, right, preferred_element_type=f32)


def mm_tn(left, right):
    return lax.dot_general(left, right, (((0,), (0,)), ((), ())), preferred_element_type=f32)


def mm_nt(left, right, precision=None):
    return lax.dot_general(
        left, right, (((1,), (1,)), ((), ())), precision=precision, preferred_element_type=f32
    )


def iota(shape, dim):
    return lax.broadcasted_iota(jnp.int32, shape, dim)


def absolute(pieces, me, place):
    picked = pieces[0]
    for rel in range(1, len(pieces)):
        picked = jnp.where((me ^ rel) == place, pieces[rel], picked)
    return picked


def split_low(value):
    high = value.astype(bf16)
    return high.astype(f32), value - high.astype(f32)


def two_lanes(value, count):
    high, low = split_low(value)
    lane = iota((value.shape[0], count), 1)
    return jnp.where(lane == 0, high, jnp.where(lane == 1, low, 0.0)).astype(bf16)


def gather_pieces(value):
    across = swap(value, "tp", 2)
    beside = swap(value, "tp", 1)
    return value, beside, across, swap(across, "tp", 1)


def scatter_sum(kept, passed, sent):
    came = swap(sent, "tp", 1)
    half = passed + came[1]
    return kept, came, swap(half, "tp", 2), half


def digits_of(count):
    digits, shift = [(0, 2)], 1
    while (1 << shift) < count:
        radix = min(4, count >> shift)
        digits.append((shift, radix))
        shift += radix.bit_length() - 1
    return digits


def rel_of(place, order):
    rel = 0
    for shift, radix in reversed(order):
        rel |= (place % radix) << shift
        place //= radix
    return rel


def trade(blocks, digit):
    shift, radix = digit
    return [swap(blocks[k], "exp", k << shift) for k in range(1, radix)]


def sum_blocks(kept, came):
    total = kept.astype(f32)
    for c in came:
        total = total + c.astype(f32)
    return total.astype(bf16)


def two_chains(a_blocks, b_blocks, order_a, order_b, tail):
    for at, (digit_a, digit_b) in enumerate(zip(order_a, order_b)):
        b_came = trade(b_blocks, digit_b)
        a_came = trade(a_blocks, digit_a)
        got = lax.optimization_barrier((*a_came, *b_came))
        a = sum_blocks(a_blocks[0], got[: len(a_came)])
        b = sum_blocks(b_blocks[0], got[len(a_came) :])
        few = b[b.shape[0] - tail :]
        if at + 1 < len(order_a):
            radix = order_a[at + 1][1]
            part = a.shape[0] // radix
            a_blocks = [a[k * part : (k + 1) * part] for k in range(radix)]
            radix = order_b[at + 1][1]
            part = (b.shape[0] - tail) // radix
            b_blocks = [
                jnp.concatenate([b[k * part : (k + 1) * part], few], axis=0) for k in range(radix)
            ]
    b = b[: b.shape[0] - tail]
    for at, (digit_a, digit_b) in enumerate(zip(order_a[::-1], order_b[::-1])):
        a_came = trade([a] * digit_a[1], digit_a)
        b_came = trade([b] * digit_b[1], digit_b)
        got = lax.optimization_barrier((*a_came, *b_came))
        a_blocks, b_blocks = [a, *got[: len(a_came)]], [b, *got[len(a_came) :]]
        if at + 1 < len(order_a):
            a, b = jnp.concatenate(a_blocks, axis=0), jnp.concatenate(b_blocks, axis=0)
    return a_blocks, b_blocks, few


def local(
    tokens,
    w_query,
    w_key,
    w_value,
    w_output,
    bias_table,
    w_router,
    w_in,
    w_out,
    gain_attn,
    gain_ffn,
    routes,
    segments,
    buckets,
    cotangent,
):
    length, quarter = tokens.shape
    ways = lax.axis_size("tp")
    owners = lax.axis_size("exp")
    width = quarter * ways
    here = w_query.shape[1]
    heads = here // HD
    experts = w_router.shape[1]
    bins = bias_table.shape[0]
    hidden_here = w_in.shape[2]
    capacity = max(2, length // owners * 9 // 8)
    per = -(-capacity // ways)
    while experts * per % LANES:
        per += 1
    rows = experts * per
    span = 2 * length
    extra = -(-(experts + 2) // 16) * 16
    few_rows = -(-(experts + 2 + heads) // 16) * 16
    me = lax.axis_index(("exp", "tp")).astype(jnp.int32)[None]
    order_a = digits_of(owners)
    order_b = order_a[1:] + order_a[:1]
    first_a, first_b = order_a[0][1], order_b[0][1]
    shift = ways.bit_length() - 1

    tok_t = tokens.T
    wq_t, wk_t, wv_t = w_query.T, w_key.T, w_value.T

    tok_pieces = gather_pieces(tok_t)

    def slot_body(
        me_ref, route_ref, cot_ref, router_ref, g1_ref, g2_ref, *outs
    ):
        drow_ref, drow_far, dcol_ref, cots_ref, d_ref = outs
        mine = me_ref[0] & (ways - 1)
        row = route_ref[...]
        above = iota((length, length), 0)
        along = iota((length, length), 1)
        col = jnp.sum(jnp.where(above == along, row, 0), axis=1, keepdims=True)
        same = col == row

        def dest(slot, expert):
            chunk = jnp.zeros_like(slot)
            for t in range(1, ways):
                chunk = chunk + (slot >= t * per).astype(jnp.int32)
            return (chunk ^ mine) * rows + expert * per + slot - chunk * per

        slot_row = jnp.sum(jnp.where(same & (above < along), 1, 0), axis=0, keepdims=True)
        slot_col = jnp.sum(jnp.where(same & (along < above), 1, 0), axis=1, keepdims=True)
        dest_row = dest(slot_row, row)
        drow_ref[...] = dest_row
        drow_far[...] = dest_row
        dcol_ref[...] = dest(slot_col, col)
        cot = cot_ref[...]
        line = iota((extra - experts, quarter), 0)
        gains = jnp.where(
            line == 0,
            g1_ref[...].astype(f32),
            jnp.where(line == 1, g2_ref[...].astype(f32), 0.0),
        )
        few = jnp.concatenate([router_ref[...].astype(f32), gains], axis=0).astype(bf16)
        for rel in range(ways):
            hot = (iota((rows, length), 0) + rel * rows == dest_row).astype(bf16)
            piece = mm_nt(hot, cot).astype(bf16)
            cots_ref[rel, 0:rows] = piece
            cots_ref[rel, rows : rows + extra] = few
            d_ref[:, rel * quarter : (rel + 1) * quarter] = piece

    dest_row, dest_far, dest_col, cots, d_send = run(
        slot_body,
        [
            ((1, length), jnp.int32),
            ((1, length), jnp.int32, True),
            ((length, 1), jnp.int32, True),
            ((ways, rows + extra, quarter), bf16),
            ((rows, width), bf16),
        ],
        (
            me,
            Far(routes.T),
            Far(cotangent.T),
            Far(w_router.T),
            gain_attn[None],
            gain_ffn[None],
        ),
        "slots",
        us=0.7,
    )
    cot_pieces = [cots[0]] + [swap(cots[rel], "tp", rel) for rel in range(1, ways)]

    def over_experts(value):
        blocks = value.reshape(experts, per, value.shape[1])
        moved = lax.all_to_all(blocks, "exp", split_axis=0, concat_axis=0, tiled=True)
        return moved.reshape(rows, value.shape[1])

    bucket_row = jnp.pad(buckets, (0, span - buckets.shape[0]), constant_values=-1)[None]

    def spread_row(few, line, count):
        pick = (iota((few.shape[0], count), 0) == line).astype(bf16)
        return mm_tn(few, pick)

    def attend_body(
        me_ref,
        t0,
        t1,
        t2,
        t3,
        c0,
        c1,
        c2,
        c3,
        wq_ref,
        wk_ref,
        wv_ref,
        wo_ref,
        table_ref,
        bucket_ref,
        seg_ref,
        dest_ref,
        x_ref,
        small_ref,
        small_far,
        r1_ref,
        n1_ref,
        q_ref,
        k_ref,
        v_ref,
        p_ref,
        attn_ref,
        kept_ref,
        passed_ref,
        sent_ref,
        xrow_ref,
    ):
        mine = me_ref[0] & (ways - 1)
        for rel, piece in enumerate((t0, t1, t2, t3)):
            at = pl.multiple_of((mine ^ rel) * quarter, quarter)
            x_ref[pl.ds(at, quarter), :] = piece[...]
        pieces = [c[rows : rows + extra] for c in (c0, c1, c2, c3)]
        small = jnp.concatenate([absolute(pieces, mine, t) for t in range(ways)], axis=1)
        small_ref[...] = small
        small_far[...] = small
        x_low = x_ref[...]
        x = x_low.astype(f32)
        r1 = lax.rsqrt(jnp.mean(x * x, axis=0, keepdims=True) + EPSILON)
        r1_ref[...] = r1
        n1 = (x * r1 * spread_row(small, experts, length)).astype(bf16)
        n1_ref[...] = n1
        q = mm(wq_ref[...], n1).astype(bf16)
        k = mm(wk_ref[...], n1).astype(bf16)
        v = mm(wv_ref[...], n1).astype(bf16)
        q_ref[...] = q
        k_ref[...] = k
        v_ref[...] = v
        hot = (iota((bins, span), 0) == bucket_ref[...]).astype(bf16)
        offsets = mm(table_ref[...], hot)
        above = iota((length, length), 0)
        along = iota((length, length), 1)
        seg_row = seg_ref[...]
        seg_col = jnp.sum(jnp.where(above == along, seg_row, 0), axis=1, keepdims=True)
        same = seg_col == seg_row
        for h in range(heads):
            part = slice(h * HD, (h + 1) * HD)
            spread = jnp.broadcast_to(offsets[h : h + 1], (length, span))
            bias = pltpu.roll(spread, length + 1, 1, stride=1, stride_axis=0)[:, :length]
            s = jnp.where(same, mm_tn(k[part], q[part]) + bias, NEG_FILL)
            e = jnp.exp(s - jnp.max(s, axis=0, keepdims=True))
            p = (e / jnp.sum(e, axis=0, keepdims=True)).astype(bf16)
            p_ref[h] = p
            attn_ref[part] = mm(v[part], p).astype(bf16)
        attn = attn_ref[...]
        dest = dest_ref[...]
        wo = wo_ref[...]
        for rel, out in enumerate((kept_ref, sent_ref.at[0], passed_ref, sent_ref.at[1])):
            hot = (iota((rows, length), 0) + rel * rows == dest).astype(bf16)
            out[...] = mm(mm_nt(hot, attn).astype(bf16), wo).astype(bf16)
            if rel == 0:
                xrow_ref[...] = mm_nt(hot, x_low).astype(bf16)

    x_full, small, small_far, r1, n1, q, k, v, probs, attn, *o_parts, x_rows = run(
        attend_body,
        [
            ((width, length), bf16, True),
            ((extra, width), bf16),
            ((extra, width), bf16, True),
            ((1, length), f32, True),
            ((width, length), bf16, True),
            ((here, length), bf16, True),
            ((here, length), bf16, True),
            ((here, length), bf16, True),
            ((heads, length, length), bf16, True),
            ((here, length), bf16, True),
            ((rows, width), bf16),
            ((rows, width), bf16),
            ((2, rows, width), bf16),
            ((rows, width), bf16),
        ],
        (
            me,
            *tok_pieces,
            *cot_pieces,
            wq_t,
            wk_t,
            wv_t,
            w_output,
            bias_table.T,
            bucket_row,
            segments,
            dest_row,
        ),
        "attend",
        us=4.0,
        limit=24,
    )
    o_kept, o_passed, o_sent = o_parts
    o_beside = swap(o_sent, "tp", 1)

    d_arrived = over_experts(d_send)
    o_half, d_arrived = lax.optimization_barrier((o_passed + o_beside[1], d_arrived))
    o_across = swap(o_half, "tp", 2)

    def route_body(
        me_ref,
        kept_ref,
        beside_ref,
        across_ref,
        xrow_ref,
        small_ref,
        c0,
        c1,
        c2,
        c3,
        h_ref,
        aux_ref,
        dout_ref,
        send_ref,
    ):
        mine = me_ref[0] & (ways - 1)
        o = kept_ref[...].astype(f32) + beside_ref[0].astype(f32) + across_ref[...].astype(f32)
        h = xrow_ref[...].astype(f32) + o
        h_ref[...] = h
        r2 = lax.rsqrt(jnp.mean(h * h, axis=-1, keepdims=True) + EPSILON)
        gain = small_ref[experts + 1 : experts + 2].astype(f32)
        n2 = h * r2 * gain
        logits = mm_nt(n2, small_ref[0:experts].astype(f32), HIGHEST)
        e = jnp.exp(logits - jnp.max(logits, axis=-1, keepdims=True))
        p = e / jnp.sum(e, axis=-1, keepdims=True)
        owner = iota((rows, experts), 0) - iota((rows, experts), 1) * per
        own = (owner >= 0) & (owner < per)
        g = jnp.sum(jnp.where(own, p, 0.0), axis=-1, keepdims=True)
        pieces = [c[0:rows] for c in (c0, c1, c2, c3)]
        dout_ref[...] = jnp.concatenate([absolute(pieces, mine, t) for t in range(ways)], axis=1)
        aux_ref[...] = jnp.zeros((rows, LANES), f32)
        aux_ref[:, 0:experts] = p
        aux_ref[:, LANES - 2 : LANES - 1] = r2
        aux_ref[:, LANES - 1 : LANES] = g
        send_ref[:, 0:width] = n2.astype(bf16)
        send_ref[:, width : width + LANES] = two_lanes(g, LANES)

    h_rows, aux, dout_rows, send = run(
        route_body,
        [
            ((rows, width), f32, True),
            ((rows, LANES), f32, True),
            ((rows, width), bf16, True),
            ((rows, width + LANES), bf16),
        ],
        (me, o_kept, o_beside, o_across, x_rows, small, *cot_pieces),
        "route",
        us=0.8,
    )
    d_pieces = gather_pieces(after(d_arrived, send))
    arrived, *d_pieces = lax.optimization_barrier((over_experts(send), *d_pieces))
    arrived = gather_pieces(arrived)

    def expert_body(me_ref, a0, a1, a2, a3, d0, d1, d2, d3, win_ref, wout_ref, *outs):
        u_ref, dy_ref, act_ref, dz_ref, kept_ref, passed_ref, sent_ref = outs
        mine = me_ref[0] & (ways - 1)
        douts = (d0, d1, d2, d3)
        for rel, a in enumerate((a0, a1, a2, a3)):
            part = slice(rel * rows, (rel + 1) * rows)
            u_ref[part] = a[:, 0:width]
            g = a[:, width : width + 1].astype(f32) + a[:, width + 1 : width + 2].astype(f32)
            pieces = []
            for src in range(ways):
                at = (rel ^ src) * quarter
                pieces.append(douts[src][:, at : at + quarter])
            dout = jnp.concatenate([absolute(pieces, mine, t) for t in range(ways)], axis=1)
            dy_ref[part] = (g * dout.astype(f32)).astype(bf16)
        u = u_ref[...]
        dy = dy_ref[...]
        z = mm(u, win_ref[0])
        c = math.sqrt(2.0 / math.pi)
        t = jnp.tanh(c * (z + 0.044715 * z * z * z))
        act = (0.5 * z * (1.0 + t)).astype(bf16)
        act_ref[...] = act
        slope = 0.5 * (1.0 + t) + 0.5 * z * (1.0 - t * t) * (c * (1.0 + 3 * 0.044715 * z * z))
        dact = mm_nt(dy, wout_ref[0])
        dot = jnp.sum(dact * act.astype(f32), axis=-1, keepdims=True)
        dz = (dact * slope).astype(bf16)
        dz_ref[...] = dz
        du = mm_nt(dz, win_ref[0]).astype(bf16)
        tail = two_lanes(dot, LANES)
        for rel, out in enumerate((kept_ref, sent_ref.at[0], passed_ref, sent_ref.at[1])):
            out[:, 0:width] = du[rel * rows : (rel + 1) * rows]
            out[:, width : width + LANES] = tail[rel * rows : (rel + 1) * rows]

    u_all, dy_all, act, dz, *du_parts = run(
        expert_body,
        [
            ((ways * rows, width), bf16, True),
            ((ways * rows, width), bf16, True),
            ((ways * rows, hidden_here), bf16, True),
            ((ways * rows, hidden_here), bf16, True),
            ((rows, width + LANES), bf16),
            ((rows, width + LANES), bf16),
            ((2, rows, width + LANES), bf16),
        ],
        (me, *arrived, *d_pieces, w_in, w_out),
        "expert",
        us=4.0,
        limit=24,
    )
    du_kept, du_beside, du_across, du_half = scatter_sum(*du_parts)
    du_sum = du_kept + du_beside[0] + du_across
    du_rows = over_experts(du_sum)

    def value_body(me_ref, act_ref, wout_ref, kept_ref, passed_ref, sent_ref):
        y = mm(act_ref[...], wout_ref[0]).astype(bf16)
        for rel, out in enumerate((kept_ref, sent_ref.at[0], passed_ref, sent_ref.at[1])):
            out[...] = y[rel * rows : (rel + 1) * rows]

    y_parts = run(
        value_body,
        [((rows, width), bf16), ((rows, width), bf16), ((2, rows, width), bf16)],
        (after(me, du_half), Pin(act), w_out),
        "value",
        us=0.8,
    )
    y_kept, y_passed, y_sent = y_parts
    y_beside = swap(y_sent, "tp", 1)
    y_across = swap(after(y_passed + y_beside[1], du_sum), "tp", 2)
    y_sum = y_kept + y_beside[0] + y_across

    def weights_body(me_ref, u_ref, dy_ref, act_ref, dz_ref, gin_ref, gout_ref):
        gin_ref[0] = mm_tn(u_ref[...], dz_ref[...]).astype(bf16)
        gout_ref[0] = mm_tn(act_ref[...], dy_ref[...]).astype(bf16)

    grad_in, grad_out = run(
        weights_body,
        [((1, width, hidden_here), bf16), ((1, hidden_here, width), bf16)],
        (after(me, du_sum), Pin(u_all), Pin(dy_all), Pin(act), Pin(dz)),
        "expert_weights",
        us=2.5,
    )
    y_rows = over_experts(y_sum)
    du_rows, grad_in, grad_out = lax.optimization_barrier((du_rows, grad_in, grad_out))

    def back_body(du_ref, h_ref, aux_ref, dout_ref, small_ref, do_ref, parts_ref):
        du = du_ref[:, 0:width].astype(f32)
        gg = du_ref[:, width : width + 1].astype(f32)
        gg = gg + du_ref[:, width + 1 : width + 2].astype(f32)
        h = h_ref[...]
        p = aux_ref[:, 0:experts]
        r2 = aux_ref[:, LANES - 2 : LANES - 1]
        gain = small_ref[experts + 1 : experts + 2].astype(f32)
        router = small_ref[0:experts].astype(f32)
        owner = iota((rows, experts), 0) - iota((rows, experts), 1) * per
        own = ((owner >= 0) & (owner < per)).astype(f32)
        dlogits = gg * (own - p)
        dn2 = du + lax.dot_general(
            dlogits, router, (((1,), (0,)), ((), ())), precision=HIGHEST, preferred_element_type=f32
        )
        hr = h * r2
        n2 = hr * gain
        inner = jnp.sum(dn2 * gain * h, axis=-1, keepdims=True)
        dh = dout_ref[...].astype(f32) + r2 * gain * dn2 - hr * (r2 * r2 / width) * inner
        do_ref[...] = dh.astype(bf16)
        parts_ref[...] = jnp.zeros((few_rows, width), f32)
        parts_ref[0:experts] = lax.dot_general(
            dlogits, n2, (((0,), (0,)), ((), ())), precision=HIGHEST, preferred_element_type=f32
        )
        parts_ref[experts : experts + 1] = jnp.sum(dn2 * hr, axis=0, keepdims=True)

    do_rows, few_parts = run(
        back_body,
        [((rows, width), bf16), ((few_rows, width), f32, True)],
        (du_rows, Pin(h_rows), Pin(aux), Pin(dout_rows), Pin(small_far)),
        "residual_back",
        us=2.0,
    )
    do_pieces = gather_pieces(do_rows)
    *do_pieces, y_rows = lax.optimization_barrier((*do_pieces, y_rows))

    a_rows = 4 * here * 2 // 3
    chunk_a = a_rows // owners
    chunk_b = (4 * here - a_rows) // owners
    a_part, b_part = a_rows // first_a, (4 * here - a_rows) // first_b

    def attend_back_body(
        me_ref,
        d0,
        d1,
        d2,
        d3,
        drow_ref,
        dcol_ref,
        wo_ref,
        attn_ref,
        q_ref,
        k_ref,
        v_ref,
        p_ref,
        n1_ref,
        wq_ref,
        wk_ref,
        wv_ref,
        x_ref,
        small_ref,
        few_ref,
        bucket_ref,
        own_ref,
        kept_ref,
        passed_ref,
        sent_ref,
        *others,
    ):
        a_outs, b_outs = others[:first_a], others[first_a : first_a + first_b]
        a_ref, b_ref, dq_ref, dk_ref, dv_ref, all_ref = others[first_a + first_b :]
        mine = me_ref[0] & (ways - 1)
        place = me_ref[0] >> shift
        stack = jnp.concatenate([d[...] for d in (d0, d1, d2, d3)], axis=0)
        hot_t = (iota((length, ways * rows), 1) == dcol_ref[...]).astype(bf16)
        do = mm(hot_t, stack).astype(bf16)
        own = stack[:, 0:quarter]
        for t in range(1, ways):
            own = jnp.where(mine == t, stack[:, t * quarter : (t + 1) * quarter], own)
        hot = (iota((ways * rows, length), 0) == drow_ref[...]).astype(bf16)
        own_ref[...] = mm_tn(own, hot).astype(bf16)
        wo = wo_ref[...]
        da = mm_nt(wo, do).astype(bf16)
        hot = (iota((bins, span), 0) == bucket_ref[...]).astype(f32)
        flip = (iota((length, length), 0) + iota((length, length), 1) == length - 1).astype(bf16)
        tables = []
        for h in range(heads):
            part = slice(h * HD, (h + 1) * HD)
            p_low = p_ref[h]
            p = p_low.astype(f32)
            dp = mm_tn(v_ref[part], da[part])
            dv_ref[part] = mm_nt(da[part], p_low).astype(bf16)
            inner = jnp.sum(p * dp, axis=0, keepdims=True)
            ds = (p * (dp - inner)).astype(bf16)
            dq_ref[part] = mm(k_ref[part], ds).astype(bf16)
            dk_ref[part] = mm_nt(q_ref[part], ds).astype(bf16)
            flipped = mm(flip, ds)
            flipped = jnp.concatenate([flipped, jnp.zeros_like(flipped)], axis=1)
            offsets = pltpu.roll(flipped, 0, 1, stride=1, stride_axis=0)
            offsets = jnp.sum(offsets, axis=0, keepdims=True)
            tables.append(mm_nt(offsets, hot, HIGHEST))
        n1 = n1_ref[...]
        gq = mm_nt(dq_ref[...], n1)
        gk = mm_nt(dk_ref[...], n1)
        gv = mm_nt(dv_ref[...], n1)
        back = gq * wq_ref[...].astype(f32) + gk * wk_ref[...].astype(f32)
        back = jnp.sum(back + gv * wv_ref[...].astype(f32), axis=0, keepdims=True)
        gain = small_ref[experts : experts + 1].astype(f32)
        gwo = mm(attn_ref[...], do)
        parts = [t.astype(bf16) for t in (gq, gk, gv, gwo)]
        for ref, chunk, start in ((a_ref, chunk_a, 0), (b_ref, chunk_b, a_rows)):
            for c in range(owners):
                low = start + c * chunk
                which, low = low // here, low % here
                ref[c] = parts[which][low : low + chunk]
        for order, ref, outs, chunk in (
            (order_a, a_ref, a_outs, chunk_a),
            (order_b, b_ref, b_outs, chunk_b),
        ):
            each = owners // len(outs)
            for at in range(owners):
                line = at % each
                outs[at // each][line * chunk : (line + 1) * chunk] = ref[rel_of(at, order) ^ place]
        few = few_ref[...]
        line = iota((few_rows, 1), 0)
        few = few + jnp.where(line == experts + 1, back / gain, 0.0)
        wide = jnp.concatenate(
            [jnp.concatenate([tables[h] * (mine == t).astype(f32) for t in range(ways)], axis=1)
             for h in range(heads)],
            axis=0,
        )
        pad = jnp.zeros((heads, width - ways * bins), f32)
        wide = jnp.concatenate([wide, pad], axis=1)
        for h in range(heads):
            few = few + jnp.where(line == experts + 2 + h, wide[h : h + 1], 0.0)
        few = few.astype(bf16)
        for out in b_outs:
            out[b_part : b_part + few_rows] = few
        dn1 = mm_tn(wq_ref[...], dq_ref[...])
        dn1 = dn1 + mm_tn(wk_ref[...], dk_ref[...])
        dn1 = dn1 + mm_tn(wv_ref[...], dv_ref[...])
        all_ref[...] = dn1.astype(bf16)
        gain = spread_row(small_ref[...], experts, length)
        dot = jnp.sum(dn1 * gain * x_ref[...].astype(f32), axis=0, keepdims=True)
        high, low = split_low(dot)
        line = iota((16, length), 0)
        tail = jnp.where(line == 0, high, jnp.where(line == 1, low, 0.0)).astype(bf16)
        for rel, out in enumerate((kept_ref, sent_ref.at[0], passed_ref, sent_ref.at[1])):
            at = pl.multiple_of((mine ^ rel) * quarter, quarter)
            out[0:quarter] = all_ref[pl.ds(at, quarter), :]
            out[quarter : quarter + 16] = tail

    dh_own, *others = run(
        attend_back_body,
        [
            ((quarter, length), bf16, True),
            ((quarter + 16, length), bf16),
            ((quarter + 16, length), bf16),
            ((2, quarter + 16, length), bf16),
            *[((a_part, width), bf16)] * first_a,
            *[((b_part + few_rows, width), bf16)] * first_b,
        ],
        (
            me,
            *do_pieces,
            Pin(dest_far),
            Pin(dest_col),
            Far(w_output),
            Pin(attn),
            Pin(q),
            Pin(k),
            Pin(v),
            Pin(probs),
            Pin(n1),
            Far(wq_t),
            Far(wk_t),
            Far(wv_t),
            Pin(x_full),
            Pin(small_far),
            Pin(few_parts),
            Far(bucket_row),
        ),
        "attend_back",
        us=6.0,
        scratch=[
            pltpu.VMEM((owners, chunk_a, width), bf16),
            pltpu.VMEM((owners, chunk_b, width), bf16),
            pltpu.VMEM((here, length), bf16),
            pltpu.VMEM((here, length), bf16),
            pltpu.VMEM((here, length), bf16),
            pltpu.VMEM((width, length), bf16),
        ],
        limit=32,
    )

    a_blocks, b_blocks, few = two_chains(
        others[3 : 3 + first_a], others[3 + first_a :], order_a, order_b, few_rows
    )

    *dn1_parts, none = scatter_sum(*others[:3])

    def tokens_body(
        me_ref, kept_ref, beside_ref, across_ref, dh_ref, tok_ref, r1_ref, small_ref, out_ref
    ):
        mine = me_ref[0] & (ways - 1)
        total = kept_ref[...].astype(f32) + beside_ref[0].astype(f32)
        total = total + across_ref[...].astype(f32)
        dn1 = total[0:quarter]
        dot = total[quarter : quarter + 1] + total[quarter + 1 : quarter + 2]
        one = r1_ref[...]
        small = small_ref[...]
        own = small[:, 0:quarter]
        for t in range(1, ways):
            own = jnp.where(mine == t, small[:, t * quarter : (t + 1) * quarter], own)
        gain = spread_row(own, experts, length)
        x = tok_ref[...].astype(f32)
        out_ref[...] = (
            dh_ref[...].astype(f32) + one * gain * dn1 - x * (one * one * one / width) * dot
        ).astype(bf16)

    (grad_tokens,) = run(
        tokens_body,
        [((quarter, length), bf16)],
        (me, *dn1_parts, Pin(dh_own), Far(tok_t), Pin(r1), Pin(small_far)),
        "tokens_back",
        us=0.5,
    )

    def out_rows_body(me_ref, h_ref, aux_ref, y_ref, o0, o1, o2, o3, all_ref):
        mine = me_ref[0] & (ways - 1)
        out = (h_ref[...] + aux_ref[:, LANES - 1 : LANES] * y_ref[...].astype(f32)).astype(bf16)
        eye = (iota((rows, rows), 0) == iota((rows, rows), 1)).astype(bf16)
        all_ref[...] = mm_tn(out, eye).astype(bf16)
        for rel, piece in enumerate((o0, o1, o2, o3)):
            at = pl.multiple_of((mine ^ rel) * quarter, quarter)
            piece[...] = all_ref[pl.ds(at, quarter), :]

    lo = run(
        out_rows_body,
        [((quarter, rows), bf16)] * ways,
        (me, Pin(h_rows), Pin(aux), y_rows),
        "layer_rows",
        us=0.5,
        scratch=[pltpu.VMEM((width, rows), bf16)],
    )
    lo = [lo[0]] + [swap(lo[rel], "tp", rel) for rel in range(1, ways)]

    def out_body(dest_ref, l0, l1, l2, l3, out_ref):
        dest = dest_ref[...]
        total = jnp.zeros((quarter, length), f32)
        for rel, piece in enumerate((l0, l1, l2, l3)):
            hot = (iota((rows, length), 0) + rel * rows == dest).astype(bf16)
            total = total + mm(piece[...], hot)
        out_ref[...] = total.astype(bf16)

    (layer_out,) = run(
        out_body, [((quarter, length), bf16)], (Pin(dest_far), *lo), "layer_out", us=0.5
    )

    few = few.astype(f32)
    few = few + swap(few, "tp", 1)
    few_other = swap(few, "tp", 2)

    def unpack_body(me_ref, few_ref, other_ref, *others):
        a_ins, b_ins = others[:first_a], others[first_a : first_a + first_b]
        *results, a_ref, b_ref = others[first_a + first_b :]
        gq_ref, gk_ref, gv_ref, go_ref, router_ref, g1_ref, g2_ref, table_ref = results
        mine = me_ref[0] & (ways - 1)
        place = me_ref[0] >> shift
        for order, ref, ins, chunk, start in (
            (order_a, a_ref, a_ins, chunk_a, 0),
            (order_b, b_ref, b_ins, chunk_b, a_rows),
        ):
            each = owners // len(ins)
            for at in range(owners):
                line = at % each
                ref[rel_of(at, order) ^ place] = ins[at // each][line * chunk : (line + 1) * chunk]
            for c in range(owners):
                low = start + c * chunk
                which, low = low // here, low % here
                (gq_ref, gk_ref, gv_ref, go_ref)[which][low : low + chunk] = ref[c]
        total = few_ref[...] + other_ref[...]
        own = total[:, 0:quarter]
        for t in range(1, ways):
            own = jnp.where(mine == t, total[:, t * quarter : (t + 1) * quarter], own)
        router_ref[...] = own[0:experts].astype(bf16)
        g2_ref[...] = own[experts : experts + 1].astype(bf16)
        g1_ref[...] = own[experts + 1 : experts + 2].astype(bf16)
        lines = total[experts + 2 : experts + 2 + heads]
        table = lines[:, 0:bins]
        for t in range(1, ways):
            table = jnp.where(mine == t, lines[:, t * bins : (t + 1) * bins], table)
        table_ref[...] = table.astype(bf16)

    gq, gk, gv, go, g_router, g_one, g_two, g_table = run(
        unpack_body,
        [
            ((here, width), bf16),
            ((here, width), bf16),
            ((here, width), bf16),
            ((here, width), bf16),
            ((experts, quarter), bf16),
            ((1, quarter), bf16),
            ((1, quarter), bf16),
            ((heads, bins), bf16),
        ],
        (me, few, few_other, *a_blocks, *b_blocks),
        "unpack",
        us=1.0,
        scratch=[
            pltpu.VMEM((owners, chunk_a, width), bf16),
            pltpu.VMEM((owners, chunk_b, width), bf16),
        ],
    )
    return (
        layer_out.T,
        grad_tokens.T,
        gq.T,
        gk.T,
        gv.T,
        go,
        g_table.T,
        g_router.T,
        grad_in,
        grad_out,
        g_one[0],
        g_two[0],
    )


def solution(mesh):
    placed = (
        P("exp", "tp"),
        P(None, "tp"),
        P(None, "tp"),
        P(None, "tp"),
        P("tp", None),
        P(None, "tp"),
        P("tp", None),
        P("exp", None, "tp"),
        P("exp", "tp", None),
        P("tp"),
        P("tp"),
        P("exp", None),
        P("exp", None),
        P(),
        P("exp", "tp"),
    )
    return jax.shard_map(
        local,
        mesh=mesh,
        in_specs=placed,
        out_specs=(
            P("exp", "tp"),
            P("exp", "tp"),
            P(None, "tp"),
            P(None, "tp"),
            P(None, "tp"),
            P("tp", None),
            P(None, "tp"),
            P("tp", None),
            P("exp", None, "tp"),
            P("exp", "tp", None),
            P("tp"),
            P("tp"),
        ),
        check_vma=False,
    )
```

```python
import math

import jax
import jax.numpy as jnp
from jax import lax
from jax.experimental import pallas as pl
from jax.experimental.pallas import tpu as pltpu
from jax.sharding import PartitionSpec as P

HD = 64
EPSILON = 1e-06
NEG_FILL = -1e30
HIGHEST = lax.Precision.HIGHEST
LANES = 128
f32 = jnp.float32
bf16 = jnp.bfloat16
VMEM = pl.BlockSpec(memory_space=pltpu.VMEM)
SMEM = pl.BlockSpec(memory_space=pltpu.SMEM)


class Far:
    def __init__(self, value):
        self.value = pltpu.with_memory_space_constraint(value, pltpu.HBM)


class Loaded:
    def __init__(self, copy, held):
        self.copy, self.held = copy, held

    def wait(self):
        if self.copy is not None:
            self.copy.wait()
            self.copy = None

    def __getitem__(self, index):
        self.wait()
        return self.held[index]


class Stored:
    def __init__(self, copy, held):
        self.copy, self.held, self.started = copy, held, False

    def __setitem__(self, index, value):
        self.held[index] = value

    def __getitem__(self, index):
        return self.held[index]

    def send(self):
        if not self.started:
            self.started = True
            self.copy.start()


def run(body, outs, args, name, us=1.0, scratch=(), limit=16):
    far_in = [isinstance(a, Far) for a in args]
    args = [a.value if isinstance(a, Far) else a for a in args]
    far_out = [len(o) == 3 for o in outs]
    bufs = [pltpu.VMEM(a.shape, a.dtype) for a, far in zip(args, far_in) if far]
    bufs += [pltpu.VMEM(o[0], o[1]) for o, far in zip(outs, far_out) if far]
    n_in, n_out, n_own = len(args), len(outs), len(scratch)
    hbm = pl.BlockSpec(memory_space=pltpu.HBM)
    specs = [
        SMEM if a.shape == (1,) and a.dtype == jnp.int32 else hbm if far else VMEM
        for a, far in zip(args, far_in)
    ]
    moved = sum(a.size * a.dtype.itemsize for a in args)
    moved += sum(math.prod(o[0]) * jnp.dtype(o[1]).itemsize for o in outs)

    def wrapped(*refs):
        ins, results = refs[:n_in], refs[n_in : n_in + n_out]
        own = refs[n_in + n_out : n_in + n_out + n_own]
        held = refs[n_in + n_out + n_own :]
        given, at = [], 0
        for ref, far in zip((*ins, *results), (*far_in, *far_out)):
            if not far:
                given.append(ref)
                continue
            if len(given) < n_in:
                copy = pltpu.make_async_copy(ref, held[at], held[-1].at[at])
                copy.start()
                given.append(Loaded(copy, held[at]))
            else:
                copy = pltpu.make_async_copy(held[at], ref, held[-1].at[at])
                given.append(Stored(copy, held[at]))
            at += 1
        body(*given, *own)
        for g in given:
            if isinstance(g, Stored):
                g.send()
        for g in given:
            if isinstance(g, Stored):
                g.copy.wait()
            elif isinstance(g, Loaded):
                g.wait()

    sems = [pltpu.SemaphoreType.DMA((len(bufs),))] if bufs else []
    return pl.pallas_call(
        wrapped,
        out_shape=[
            pltpu.HBM(o[0], o[1]) if len(o) == 3 else jax.ShapeDtypeStruct(o[0], o[1])
            for o in outs
        ],
        in_specs=specs,
        out_specs=[hbm if far else VMEM for far in far_out],
        scratch_shapes=[*scratch, *bufs, *sems],
        compiler_params=pltpu.CompilerParams(vmem_limit_bytes=limit * 2**20),
        cost_estimate=pl.CostEstimate(
            flops=int(us * 1.1e9), bytes_accessed=moved, transcendentals=0
        ),
        name=name,
    )(*args)


def fetch(token, values, name):
    values = [pltpu.with_memory_space_constraint(v, pltpu.HBM) for v in values]
    count = len(values)

    def body(token_ref, *refs):
        ins, outs, sems = refs[:count], refs[count : 2 * count], refs[-1]
        copies = [
            pltpu.make_async_copy(i, o, sems.at[n]) for n, (i, o) in enumerate(zip(ins, outs))
        ]
        for c in copies:
            c.start()
        for c in copies:
            c.wait()

    return pl.pallas_call(
        body,
        out_shape=[jax.ShapeDtypeStruct(v.shape, v.dtype) for v in values],
        in_specs=[SMEM] + [pl.BlockSpec(memory_space=pltpu.HBM)] * count,
        out_specs=[VMEM] * count,
        scratch_shapes=[pltpu.SemaphoreType.DMA((count,))],
        compiler_params=pltpu.CompilerParams(vmem_limit_bytes=16 * 2**20),
        name=name,
    )(token, *values)


def swap(value, axis, mask):
    size = lax.axis_size(axis)
    return lax.ppermute(value, axis, [(i, i ^ mask) for i in range(size)])


def after(value, *others):
    return lax.optimization_barrier((value, *others))[0]


def mm(left, right):
    return jnp.dot(left, right, preferred_element_type=f32)


def mm_tn(left, right):
    return lax.dot_general(left, right, (((0,), (0,)), ((), ())), preferred_element_type=f32)


def mm_nt(left, right, precision=None):
    return lax.dot_general(
        left, right, (((1,), (1,)), ((), ())), precision=precision, preferred_element_type=f32
    )


def iota(shape, dim):
    return lax.broadcasted_iota(jnp.int32, shape, dim)


def absolute(pieces, me, place):
    picked = pieces[0]
    for rel in range(1, len(pieces)):
        picked = jnp.where((me ^ rel) == place, pieces[rel], picked)
    return picked


def split_low(value):
    high = value.astype(bf16)
    return high.astype(f32), value - high.astype(f32)


def two_lanes(value, count):
    high, low = split_low(value)
    lane = iota((value.shape[0], count), 1)
    return jnp.where(lane == 0, high, jnp.where(lane == 1, low, 0.0)).astype(bf16)


def gather_pieces(value):
    across = swap(value, "tp", 2)
    beside = swap(value, "tp", 1)
    return value, beside, across, swap(across, "tp", 1)


def scatter_sum(kept, passed, sent):
    came = swap(sent, "tp", 1)
    half = passed + came[1]
    return kept, came, swap(half, "tp", 2), half


def digits_of(count):
    digits, shift = [(0, 2)], 1
    while (1 << shift) < count:
        radix = min(4, count >> shift)
        digits.append((shift, radix))
        shift += radix.bit_length() - 1
    return digits


def rel_of(place, order):
    rel = 0
    for shift, radix in reversed(order):
        rel |= (place % radix) << shift
        place //= radix
    return rel


def trade(blocks, digit):
    shift, radix = digit
    return [swap(blocks[k], "exp", k << shift) for k in range(1, radix)]


def sum_blocks(kept, came):
    total = kept.astype(f32)
    for c in came:
        total = total + c.astype(f32)
    return total.astype(bf16)


def two_chains(a_blocks, b_blocks, order_a, order_b, tail, beside):
    for at, (digit_a, digit_b) in enumerate(zip(order_a, order_b)):
        b_came = trade(b_blocks, digit_b)
        a_came = trade(a_blocks, digit_a)
        got = beside((*a_came, *b_came), b_blocks[0])
        a = sum_blocks(a_blocks[0], got[: len(a_came)])
        b = sum_blocks(b_blocks[0], got[len(a_came) :])
        few = b[b.shape[0] - tail :]
        if at + 1 < len(order_a):
            radix = order_a[at + 1][1]
            part = a.shape[0] // radix
            a_blocks = [a[k * part : (k + 1) * part] for k in range(radix)]
            radix = order_b[at + 1][1]
            part = (b.shape[0] - tail) // radix
            b_blocks = [
                jnp.concatenate([b[k * part : (k + 1) * part], few], axis=0) for k in range(radix)
            ]
    b = b[: b.shape[0] - tail]
    for at, (digit_a, digit_b) in enumerate(zip(order_a[::-1], order_b[::-1])):
        a_came = trade([a] * digit_a[1], digit_a)
        b_came = trade([b] * digit_b[1], digit_b)
        got = beside((*a_came, *b_came), few)
        a_blocks, b_blocks = [a, *got[: len(a_came)]], [b, *got[len(a_came) :]]
        if at + 1 < len(order_a):
            a, b = jnp.concatenate(a_blocks, axis=0), jnp.concatenate(b_blocks, axis=0)
    return a_blocks, b_blocks


def local(
    tokens,
    w_query,
    w_key,
    w_value,
    w_output,
    bias_table,
    w_router,
    w_in,
    w_out,
    gain_attn,
    gain_ffn,
    routes,
    segments,
    buckets,
    cotangent,
):
    length, quarter = tokens.shape
    ways = lax.axis_size("tp")
    owners = lax.axis_size("exp")
    width = quarter * ways
    here = w_query.shape[1]
    heads = here // HD
    experts = w_router.shape[1]
    bins = bias_table.shape[0]
    hidden_here = w_in.shape[2]
    capacity = max(2, length // owners * 9 // 8)
    per = -(-capacity // ways)
    while experts * per % LANES:
        per += 1
    rows = experts * per
    span = 2 * length
    extra = -(-(experts + 2) // 16) * 16
    few_rows = -(-(experts + 2 + heads) // 16) * 16
    me = lax.axis_index(("exp", "tp")).astype(jnp.int32)[None]
    order_a = digits_of(owners)
    order_b = order_a[1:] + order_a[:1]
    first_a, first_b = order_a[0][1], order_b[0][1]
    shift = ways.bit_length() - 1

    tok_t = tokens.T
    wq_t, wk_t, wv_t = w_query.T, w_key.T, w_value.T

    def slot_body(
        me_ref, route_ref, cot_ref, *outs
    ):
        drow_ref, cots_ref = outs
        mine = me_ref[0] & (ways - 1)
        row = route_ref[...]
        above = iota((length, length), 0)
        along = iota((length, length), 1)
        col = jnp.sum(jnp.where(above == along, row, 0), axis=1, keepdims=True)
        same = col == row

        def dest(slot, expert):
            chunk = jnp.zeros_like(slot)
            for t in range(1, ways):
                chunk = chunk + (slot >= t * per).astype(jnp.int32)
            return (chunk ^ mine) * rows + expert * per + slot - chunk * per

        slot_row = jnp.sum(jnp.where(same & (above < along), 1, 0), axis=0, keepdims=True)
        dest_row = dest(slot_row, row)
        drow_ref[...] = dest_row
        cot = cot_ref[...]
        for rel in range(ways):
            hot = (iota((rows, length), 0) + rel * rows == dest_row).astype(bf16)
            piece = mm_nt(hot, cot).astype(bf16)
            cots_ref[rel] = piece

    dest_row, cots = run(
        slot_body,
        [
            ((1, length), jnp.int32),
            ((ways, rows, quarter), bf16),
        ],
        (
            me,
            Far(routes.T),
            Far(cotangent.T),
        ),
        "slots",
        us=0.7,
    )
    def small_body(router_ref, g1_ref, g2_ref, small_ref):
        line = iota((extra - experts, quarter), 0)
        gains = jnp.where(
            line == 0,
            g1_ref[...].astype(f32)[None],
            jnp.where(line == 1, g2_ref[...].astype(f32)[None], 0.0),
        )
        small_ref[...] = jnp.concatenate([router_ref[...].astype(f32), gains], 0).astype(bf16)

    (small_own,) = run(
        small_body,
        [((extra, quarter), bf16)],
        (Far(w_router.T), Far(gain_attn), Far(gain_ffn)),
        "small",
        us=0.2,
    )
    small_pieces = [small_own] + [swap(small_own, "tp", rel) for rel in range(1, ways)]
    tok_across = swap(tok_t, "tp", 2)
    tok_across, *small_pieces = lax.optimization_barrier((tok_across, *small_pieces))
    tok_pieces = (tok_t, swap(tok_t, "tp", 1), tok_across, swap(tok_across, "tp", 1))

    def over_experts(value):
        blocks = value.reshape(experts, per, value.shape[1])
        moved = lax.all_to_all(blocks, "exp", split_axis=0, concat_axis=0, tiled=True)
        return moved.reshape(rows, value.shape[1])

    def bucket_hot(ref, held, dtype):
        held[...] = jnp.full((1, span), -1, jnp.int32)
        held[:, 0 : buckets.shape[0]] = ref[...][None]
        return (iota((bins, span), 0) == held[...]).astype(dtype)

    def spread_row(few, line, count):
        pick = (iota((few.shape[0], count), 0) == line).astype(bf16)
        return mm_tn(few, pick)

    def attend_body(
        me_ref,
        t0,
        t1,
        t2,
        t3,
        c0,
        c1,
        c2,
        c3,
        wq_ref,
        wk_ref,
        wv_ref,
        wo_ref,
        table_ref,
        bucket_ref,
        seg_ref,
        dest_ref,
        small_ref,
        small_far,
        dest_far,
        r1_ref,
        n1_ref,
        q_ref,
        k_ref,
        v_ref,
        p0_ref,
        p1_ref,
        p2_ref,
        attn_ref,
        kept_ref,
        passed_ref,
        sent_ref,
        xrow_ref,
        x_ref,
        bucket_held,
    ):
        p_refs = (p0_ref, p1_ref, p2_ref)
        mine = me_ref[0] & (ways - 1)
        for rel, piece in enumerate((t0, t1, t2, t3)):
            at = pl.multiple_of((mine ^ rel) * quarter, quarter)
            x_ref[pl.ds(at, quarter), :] = piece[...]
        pieces = [c[...] for c in (c0, c1, c2, c3)]
        small = jnp.concatenate([absolute(pieces, mine, t) for t in range(ways)], axis=1)
        small_ref[...] = small
        small_far[...] = small
        small_far.send()
        dest_far[...] = dest_ref[...]
        dest_far.send()
        x_low = x_ref[...]
        x = x_low.astype(f32)
        r1 = lax.rsqrt(jnp.mean(x * x, axis=0, keepdims=True) + EPSILON)
        r1_ref[...] = r1
        r1_ref.send()
        n1 = (x * r1 * spread_row(small, experts, length)).astype(bf16)
        n1_ref[...] = n1
        n1_ref.send()
        q = mm(wq_ref[...], n1).astype(bf16)
        k = mm(wk_ref[...], n1).astype(bf16)
        v = mm(wv_ref[...], n1).astype(bf16)
        q_ref[...] = q
        k_ref[...] = k
        v_ref[...] = v
        for ref in (q_ref, k_ref, v_ref):
            ref.send()
        hot = bucket_hot(bucket_ref, bucket_held, bf16)
        offsets = mm(table_ref[...], hot)
        above = iota((length, length), 0)
        along = iota((length, length), 1)
        seg_row = seg_ref[...]
        seg_col = jnp.sum(jnp.where(above == along, seg_row, 0), axis=1, keepdims=True)
        same = seg_col == seg_row
        for h in range(heads):
            part = slice(h * HD, (h + 1) * HD)
            spread = jnp.broadcast_to(offsets[h : h + 1], (length, span))
            bias = pltpu.roll(spread, length + 1, 1, stride=1, stride_axis=0)[:, :length]
            s = jnp.where(same, mm_tn(k[part], q[part]) + bias, NEG_FILL)
            e = jnp.exp(s - jnp.max(s, axis=0, keepdims=True))
            p = (e / jnp.sum(e, axis=0, keepdims=True)).astype(bf16)
            p_refs[h][...] = p
            p_refs[h].send()
            attn_ref[part] = mm(v[part], p).astype(bf16)
        attn = attn_ref[...]
        attn_ref.send()
        dest = dest_ref[...]
        wo = wo_ref[...]
        for rel, out in enumerate((kept_ref, sent_ref.at[0], passed_ref, sent_ref.at[1])):
            hot = (iota((rows, length), 0) + rel * rows == dest).astype(bf16)
            out[...] = mm(mm_nt(hot, attn).astype(bf16), wo).astype(bf16)
            if rel == 0:
                xrow_ref[...] = mm_nt(hot, x_low).astype(bf16)

    small, small_far, dest_far, r1, n1, q, k, v, p0, p1, p2, attn, *o_parts, x_rows = run(
        attend_body,
        [
            ((extra, width), bf16),
            ((extra, width), bf16, True),
            ((1, length), jnp.int32, True),
            ((1, length), f32, True),
            ((width, length), bf16, True),
            ((here, length), bf16, True),
            ((here, length), bf16, True),
            ((here, length), bf16, True),
            *[((length, length), bf16, True)] * heads,
            ((here, length), bf16, True),
            ((rows, width), bf16),
            ((rows, width), bf16),
            ((2, rows, width), bf16),
            ((rows, width), bf16),
        ],
        (
            me,
            *tok_pieces,
            *small_pieces,
            wq_t,
            wk_t,
            wv_t,
            w_output,
            bias_table.T,
            buckets,
            segments,
            dest_row,
        ),
        "attend",
        us=0.01,
        scratch=[pltpu.VMEM((width, length), bf16), pltpu.VMEM((1, span), jnp.int32)],
        limit=24,
    )
    o_kept, o_passed, o_sent = o_parts
    o_beside = swap(o_sent, "tp", 1)
    o_half = o_passed + o_beside[1]
    o_across = swap(o_half, "tp", 2)

    def join_body(me_ref, cots_ref, out_ref):
        for rel in range(ways):
            out_ref[:, rel * quarter : (rel + 1) * quarter] = cots_ref[rel]

    (d_send,) = run(join_body, [((rows, width), bf16)], (after(me, o_half), cots), "join", us=0.3)
    d_arrived = over_experts(d_send)

    def routed(kept_ref, beside_ref, across_ref, xrow_ref, small_ref):
        o = kept_ref[...].astype(f32) + beside_ref[0].astype(f32) + across_ref[...].astype(f32)
        h = xrow_ref[...].astype(f32) + o
        r2 = lax.rsqrt(jnp.mean(h * h, axis=-1, keepdims=True) + EPSILON)
        gain = small_ref[experts + 1 : experts + 2].astype(f32)
        n2 = h * r2 * gain
        logits = mm_nt(n2, small_ref[0:experts].astype(f32), HIGHEST)
        e = jnp.exp(logits - jnp.max(logits, axis=-1, keepdims=True))
        p = e / jnp.sum(e, axis=-1, keepdims=True)
        owner = iota((rows, experts), 0) - iota((rows, experts), 1) * per
        own = (owner >= 0) & (owner < per)
        g = jnp.sum(jnp.where(own, p, 0.0), axis=-1, keepdims=True)
        return h, r2, n2, p, g

    def route_body(kept_ref, beside_ref, across_ref, xrow_ref, small_ref, send_ref):
        h, r2, n2, p, g = routed(kept_ref, beside_ref, across_ref, xrow_ref, small_ref)
        send_ref[:, 0:width] = n2.astype(bf16)
        send_ref[:, width : width + LANES] = two_lanes(g, LANES)

    route_args = (o_kept, o_beside, o_across, x_rows, small)
    (send,) = run(
        route_body, [((rows, width + LANES), bf16)], route_args, "route", us=4
    )

    def state_body(
        me_ref, kept_ref, beside_ref, across_ref, xrow_ref, small_ref, c0, c1, c2, c3, *outs
    ):
        h_ref, aux_ref, dout_ref = outs
        mine = me_ref[0] & (ways - 1)
        pieces = [c[...] for c in (c0, c1, c2, c3)]
        dout_ref[...] = jnp.concatenate([absolute(pieces, mine, t) for t in range(ways)], axis=1)
        dout_ref.send()
        h, r2, n2, p, g = routed(kept_ref, beside_ref, across_ref, xrow_ref, small_ref)
        h_ref[...] = h
        h_ref.send()
        aux_ref[...] = jnp.zeros((rows, LANES), f32)
        aux_ref[:, 0:experts] = p
        aux_ref[:, LANES - 2 : LANES - 1] = r2
        aux_ref[:, LANES - 1 : LANES] = g

    later = after(cots, send)
    cot_pieces = [later[0]] + [swap(later[rel], "tp", rel) for rel in range(1, ways)]
    h_rows, aux, dout_rows = run(
        state_body,
        [
            ((rows, width), f32, True),
            ((rows, LANES), f32, True),
            ((rows, width), bf16, True),
        ],
        (after(me, send), *route_args, *cot_pieces),
        "state",
        us=0.01,
    )
    send, d_arrived = lax.optimization_barrier((send, d_arrived))
    d_pieces = gather_pieces(d_arrived)
    arrived, h_rows, aux, dout_rows, *d_pieces = lax.optimization_barrier(
        (over_experts(send), h_rows, aux, dout_rows, *d_pieces)
    )
    weights = fetch(after(me, arrived), [w_in, w_out], "expert_arguments")
    across, *weights = lax.optimization_barrier((swap(arrived, "tp", 2), *weights))
    arrived = (arrived, swap(arrived, "tp", 1), across, swap(across, "tp", 1))

    def expert_body(me_ref, a0, a1, a2, a3, d0, d1, d2, d3, win_ref, wout_ref, *outs):
        u_ref, dy_ref, act_ref, dz_ref, kept_ref, passed_ref, sent_ref = outs
        mine = me_ref[0] & (ways - 1)
        douts = (d0, d1, d2, d3)
        for rel, a in enumerate((a0, a1, a2, a3)):
            part = slice(rel * rows, (rel + 1) * rows)
            u_ref[part] = a[:, 0:width]
            g = a[:, width : width + 1].astype(f32) + a[:, width + 1 : width + 2].astype(f32)
            pieces = []
            for src in range(ways):
                at = (rel ^ src) * quarter
                pieces.append(douts[src][:, at : at + quarter])
            dout = jnp.concatenate([absolute(pieces, mine, t) for t in range(ways)], axis=1)
            dy_ref[part] = (g * dout.astype(f32)).astype(bf16)
        u_ref.send()
        dy_ref.send()
        u = u_ref[...]
        dy = dy_ref[...]
        z = mm(u, win_ref[0])
        c = math.sqrt(2.0 / math.pi)
        t = jnp.tanh(c * (z + 0.044715 * z * z * z))
        act = (0.5 * z * (1.0 + t)).astype(bf16)
        act_ref[...] = act
        act_ref.send()
        slope = 0.5 * (1.0 + t) + 0.5 * z * (1.0 - t * t) * (c * (1.0 + 3 * 0.044715 * z * z))
        dact = mm_nt(dy, wout_ref[0])
        dot = jnp.sum(dact * act.astype(f32), axis=-1, keepdims=True)
        dz = (dact * slope).astype(bf16)
        dz_ref[...] = dz
        dz_ref.send()
        du = mm_nt(dz, win_ref[0]).astype(bf16)
        tail = two_lanes(dot, LANES)
        for rel, out in enumerate((kept_ref, sent_ref.at[0], passed_ref, sent_ref.at[1])):
            out[:, 0:width] = du[rel * rows : (rel + 1) * rows]
            out[:, width : width + LANES] = tail[rel * rows : (rel + 1) * rows]

    u_all, dy_all, act, dz, *du_parts = run(
        expert_body,
        [
            ((ways * rows, width), bf16, True),
            ((ways * rows, width), bf16, True),
            ((ways * rows, hidden_here), bf16, True),
            ((ways * rows, hidden_here), bf16, True),
            ((rows, width + LANES), bf16),
            ((rows, width + LANES), bf16),
            ((2, rows, width + LANES), bf16),
        ],
        (me, *arrived, *d_pieces, *weights),
        "expert",
        us=4.0,
        limit=24,
    )
    du_kept, du_beside, du_across, du_half = scatter_sum(*du_parts)
    du_sum = du_kept + du_beside[0] + du_across
    du_rows = over_experts(du_sum)

    def value_body(me_ref, act_ref, wout_ref, kept_ref, passed_ref, sent_ref):
        y = mm(act_ref[...], wout_ref[0]).astype(bf16)
        for rel, out in enumerate((kept_ref, sent_ref.at[0], passed_ref, sent_ref.at[1])):
            out[...] = y[rel * rows : (rel + 1) * rows]

    y_parts = run(
        value_body,
        [((rows, width), bf16), ((rows, width), bf16), ((2, rows, width), bf16)],
        (after(me, du_half), Far(act), w_out),
        "value",
        us=0.8,
    )
    y_kept, y_passed, y_sent = y_parts
    y_beside = swap(y_sent, "tp", 1)
    y_across = swap(after(y_passed + y_beside[1], du_sum), "tp", 2)
    y_sum = y_kept + y_beside[0] + y_across

    y_rows = over_experts(y_sum)
    state = fetch(after(me, du_sum), [h_rows, aux, dout_rows, small_far, dest_far], "state_again")
    du_rows, _, *state = lax.optimization_barrier((du_rows, y_sum, *state))

    def back_body(
        du_ref, h_ref, aux_ref, dout_ref, small_ref, dest_ref, do_ref, parts_ref, drow_ref
    ):
        drow_ref[...] = dest_ref[...]
        du = du_ref[:, 0:width].astype(f32)
        gg = du_ref[:, width : width + 1].astype(f32)
        gg = gg + du_ref[:, width + 1 : width + 2].astype(f32)
        h = h_ref[...]
        p = aux_ref[:, 0:experts]
        r2 = aux_ref[:, LANES - 2 : LANES - 1]
        gain = small_ref[experts + 1 : experts + 2].astype(f32)
        router = small_ref[0:experts].astype(f32)
        owner = iota((rows, experts), 0) - iota((rows, experts), 1) * per
        own = ((owner >= 0) & (owner < per)).astype(f32)
        dlogits = gg * (own - p)
        dn2 = du + lax.dot_general(
            dlogits, router, (((1,), (0,)), ((), ())), precision=HIGHEST, preferred_element_type=f32
        )
        hr = h * r2
        n2 = hr * gain
        inner = jnp.sum(dn2 * gain * h, axis=-1, keepdims=True)
        dh = dout_ref[...].astype(f32) + r2 * gain * dn2 - hr * (r2 * r2 / width) * inner
        do_ref[...] = dh.astype(bf16)
        parts_ref[...] = jnp.zeros((few_rows, width), f32)
        parts_ref[0:experts] = lax.dot_general(
            dlogits, n2, (((0,), (0,)), ((), ())), precision=HIGHEST, preferred_element_type=f32
        )
        parts_ref[experts : experts + 1] = jnp.sum(dn2 * hr, axis=0, keepdims=True)

    do_rows, few_parts, dest_near = run(
        back_body,
        [((rows, width), bf16), ((few_rows, width), f32), ((1, length), jnp.int32)],
        (du_rows, *state),
        "residual_back",
        us=2.0,
    )
    do_across = swap(do_rows, "tp", 2)
    do_beside = swap(do_rows, "tp", 1)
    wanted = [w_output, attn, q, k, v, p0, p1, p2, n1, wq_t, wk_t, wv_t, small_far]
    fetched = fetch(after(me, do_rows), wanted, "attend_again")
    do_across, *fetched = lax.optimization_barrier((do_across, *fetched))
    do_pieces = (do_rows, do_beside, do_across, swap(do_across, "tp", 1))

    a_rows = 4 * here * 2 // 3
    chunk_a = a_rows // owners
    chunk_b = (4 * here - a_rows) // owners
    a_part, b_part = a_rows // first_a, (4 * here - a_rows) // first_b

    def attend_back_body(
        me_ref,
        d0,
        d1,
        d2,
        d3,
        drow_ref,
        wo_ref,
        attn_ref,
        q_ref,
        k_ref,
        v_ref,
        p0_ref,
        p1_ref,
        p2_ref,
        n1_ref,
        wq_ref,
        wk_ref,
        wv_ref,
        small_ref,
        few_ref,
        bucket_ref,
        own_ref,
        kept_ref,
        passed_ref,
        sent_ref,
        *others,
    ):
        a_outs, b_outs = others[:first_a], others[first_a : first_a + first_b]
        a_ref, b_ref, dq_ref, dk_ref, dv_ref, all_ref, bucket_held = others[first_a + first_b :]
        mine = me_ref[0] & (ways - 1)
        place = me_ref[0] >> shift
        stack = jnp.concatenate([d[...] for d in (d0, d1, d2, d3)], axis=0)
        drow = drow_ref[...]
        eye = iota((length, length), 0) == iota((length, length), 1)
        dcol = jnp.sum(jnp.where(eye, drow, 0), axis=1, keepdims=True)
        hot_t = (iota((length, ways * rows), 1) == dcol).astype(bf16)
        do = mm(hot_t, stack).astype(bf16)
        own = stack[:, 0:quarter]
        for t in range(1, ways):
            own = jnp.where(mine == t, stack[:, t * quarter : (t + 1) * quarter], own)
        hot = (iota((ways * rows, length), 0) == drow).astype(bf16)
        own_ref[...] = mm_tn(own, hot).astype(bf16)
        wo = wo_ref[...]
        da = mm_nt(wo, do).astype(bf16)
        hot = bucket_hot(bucket_ref, bucket_held, f32)
        flip = (iota((length, length), 0) + iota((length, length), 1) == length - 1).astype(bf16)
        tables = []
        for h in range(heads):
            part = slice(h * HD, (h + 1) * HD)
            p_low = (p0_ref, p1_ref, p2_ref)[h][...]
            p = p_low.astype(f32)
            dp = mm_tn(v_ref[part], da[part])
            dv_ref[part] = mm_nt(da[part], p_low).astype(bf16)
            inner = jnp.sum(p * dp, axis=0, keepdims=True)
            ds = (p * (dp - inner)).astype(bf16)
            dq_ref[part] = mm(k_ref[part], ds).astype(bf16)
            dk_ref[part] = mm_nt(q_ref[part], ds).astype(bf16)
            flipped = mm(flip, ds)
            flipped = jnp.concatenate([flipped, jnp.zeros_like(flipped)], axis=1)
            offsets = pltpu.roll(flipped, 0, 1, stride=1, stride_axis=0)
            offsets = jnp.sum(offsets, axis=0, keepdims=True)
            tables.append(mm_nt(offsets, hot, HIGHEST))
        n1 = n1_ref[...]
        gq = mm_nt(dq_ref[...], n1)
        gk = mm_nt(dk_ref[...], n1)
        gv = mm_nt(dv_ref[...], n1)
        back = gq * wq_ref[...].astype(f32) + gk * wk_ref[...].astype(f32)
        back = jnp.sum(back + gv * wv_ref[...].astype(f32), axis=0, keepdims=True)
        gain = small_ref[experts : experts + 1].astype(f32)
        gwo = mm(attn_ref[...], do)
        parts = [t.astype(bf16) for t in (gq, gk, gv, gwo)]
        for ref, chunk, start in ((a_ref, chunk_a, 0), (b_ref, chunk_b, a_rows)):
            for c in range(owners):
                low = start + c * chunk
                which, low = low // here, low % here
                ref[c] = parts[which][low : low + chunk]
        for order, ref, outs, chunk in (
            (order_a, a_ref, a_outs, chunk_a),
            (order_b, b_ref, b_outs, chunk_b),
        ):
            each = owners // len(outs)
            for at in range(owners):
                line = at % each
                outs[at // each][line * chunk : (line + 1) * chunk] = ref[rel_of(at, order) ^ place]
        few = few_ref[...]
        line = iota((few_rows, 1), 0)
        few = few + jnp.where(line == experts + 1, back / gain, 0.0)
        wide = jnp.concatenate(
            [jnp.concatenate([tables[h] * (mine == t).astype(f32) for t in range(ways)], axis=1)
             for h in range(heads)],
            axis=0,
        )
        pad = jnp.zeros((heads, width - ways * bins), f32)
        wide = jnp.concatenate([wide, pad], axis=1)
        for h in range(heads):
            few = few + jnp.where(line == experts + 2 + h, wide[h : h + 1], 0.0)
        few = few.astype(bf16)
        for out in b_outs:
            out[b_part : b_part + few_rows] = few
        dn1 = mm_tn(wq_ref[...], dq_ref[...])
        dn1 = dn1 + mm_tn(wk_ref[...], dk_ref[...])
        dn1 = dn1 + mm_tn(wv_ref[...], dv_ref[...])
        all_ref[...] = dn1.astype(bf16)
        dot = jnp.sum(dn1 * n1.astype(f32), axis=0, keepdims=True)
        high, low = split_low(dot)
        line = iota((16, length), 0)
        tail = jnp.where(line == 0, high, jnp.where(line == 1, low, 0.0)).astype(bf16)
        for rel, out in enumerate((kept_ref, sent_ref.at[0], passed_ref, sent_ref.at[1])):
            at = pl.multiple_of((mine ^ rel) * quarter, quarter)
            out[0:quarter] = all_ref[pl.ds(at, quarter), :]
            out[quarter : quarter + 16] = tail

    dh_own, *others = run(
        attend_back_body,
        [
            ((quarter, length), bf16),
            ((quarter + 16, length), bf16),
            ((quarter + 16, length), bf16),
            ((2, quarter + 16, length), bf16),
            *[((a_part, width), bf16)] * first_a,
            *[((b_part + few_rows, width), bf16)] * first_b,
        ],
        (
            me,
            *do_pieces,
            dest_near,
            *fetched,
            few_parts,
            buckets,
        ),
        "attend_back",
        us=0.01,
        scratch=[
            pltpu.VMEM((owners, chunk_a, width), bf16),
            pltpu.VMEM((owners, chunk_b, width), bf16),
            pltpu.VMEM((here, length), bf16),
            pltpu.VMEM((here, length), bf16),
            pltpu.VMEM((here, length), bf16),
            pltpu.VMEM((width, length), bf16),
            pltpu.VMEM((1, span), jnp.int32),
        ],
        limit=32,
    )

    y_rows, *others = lax.optimization_barrier((y_rows, *others))
    dn1_kept, dn1_passed, dn1_sent = others[:3]
    held = {}

    def tokens_body(
        me_ref, kept_ref, beside_ref, across_ref, dh_ref, tok_ref, r1_ref, small_ref, out_ref
    ):
        mine = me_ref[0] & (ways - 1)
        total = kept_ref[...].astype(f32) + beside_ref[0].astype(f32)
        total = total + across_ref[...].astype(f32)
        dn1 = total[0:quarter]
        dot = total[quarter : quarter + 1] + total[quarter + 1 : quarter + 2]
        one = r1_ref[...]
        small = small_ref[...]
        own = small[:, 0:quarter]
        for t in range(1, ways):
            own = jnp.where(mine == t, small[:, t * quarter : (t + 1) * quarter], own)
        gain = spread_row(own, experts, length)
        x = tok_ref[...].astype(f32)
        out_ref[...] = (
            dh_ref[...].astype(f32) + one * gain * dn1 - x * (one * one / width) * dot
        ).astype(bf16)

    def out_rows_body(me_ref, h_ref, aux_ref, y_ref, o0, o1, o2, o3, all_ref):
        mine = me_ref[0] & (ways - 1)
        out = (h_ref[...] + aux_ref[:, LANES - 1 : LANES] * y_ref[...].astype(f32)).astype(bf16)
        eye = (iota((rows, rows), 0) == iota((rows, rows), 1)).astype(bf16)
        all_ref[...] = mm_tn(out, eye).astype(bf16)
        for rel, piece in enumerate((o0, o1, o2, o3)):
            at = pl.multiple_of((mine ^ rel) * quarter, quarter)
            piece[...] = all_ref[pl.ds(at, quarter), :]

    def out_body(dest_ref, l0, l1, l2, l3, out_ref):
        dest = dest_ref[...]
        total = jnp.zeros((quarter, length), f32)
        for rel, piece in enumerate((l0, l1, l2, l3)):
            hot = (iota((rows, length), 0) + rel * rows == dest).astype(bf16)
            total = total + mm(piece[...], hot)
        out_ref[...] = total.astype(bf16)

    def weights_body(me_ref, u_ref, dy_ref, act_ref, dz_ref, gin_ref, gout_ref):
        gin_ref[0] = mm_tn(u_ref[...], dz_ref[...]).astype(bf16)
        gout_ref[0] = mm_tn(act_ref[...], dy_ref[...]).astype(bf16)

    def beside(came, block):
        phase = held.setdefault("phase", 0)
        held["phase"] += 1
        last = 2 * len(order_a) - 1
        extras = {}
        if phase == 0:
            extras["dn1_beside"] = swap(dn1_sent, "tp", 1)
            extras["grad_in"], extras["grad_out"] = run(
                weights_body,
                [((1, width, hidden_here), bf16), ((1, hidden_here, width), bf16)],
                (after(me, dn1_sent), Far(u_all), Far(dy_all), Far(act), Far(dz)),
                "expert_weights",
                us=12,
            )
        if phase == 1:
            half = dn1_passed + held["dn1_beside"][1]
            extras["dn1_across"] = swap(half, "tp", 2)
            lo = run(
                out_rows_body,
                [((quarter, rows), bf16)] * ways,
                (me, Far(h_rows), Far(aux), y_rows),
                "layer_rows",
                us=12,
                scratch=[pltpu.VMEM((width, rows), bf16)],
            )
            for rel in range(ways):
                extras["lo%d" % rel] = lo[rel]
        if phase == last - 1:
            few = block.astype(f32)
            extras["few"] = few + swap(few, "tp", 1)
            for rel in range(1, ways):
                extras["lo%d" % rel] = swap(held["lo%d" % rel], "tp", rel)
            (extras["grad_tokens"],) = run(
                tokens_body,
                [((quarter, length), bf16)],
                (
                    me,
                    dn1_kept,
                    held["dn1_beside"],
                    held["dn1_across"],
                    dh_own,
                    Far(tok_t),
                    Far(r1),
                    Far(small_far),
                ),
                "tokens_back",
                us=12,
            )
        if phase == last:
            extras["few_other"] = swap(held["few"], "tp", 2)
            (extras["layer_out"],) = run(
                out_body,
                [((quarter, length), bf16)],
                (Far(dest_far), *[held["lo%d" % rel] for rel in range(ways)]),
                "layer_out",
                us=12,
            )
        names = list(extras)
        got = lax.optimization_barrier((*came, *[extras[n] for n in names]))
        held.update(zip(names, got[len(came) :]))
        return got[: len(came)]

    a_blocks, b_blocks = two_chains(
        others[3 : 3 + first_a], others[3 + first_a :], order_a, order_b, few_rows, beside
    )
    layer_out, grad_tokens = held["layer_out"], held["grad_tokens"]
    grad_in, grad_out = held["grad_in"], held["grad_out"]

    def unpack_body(me_ref, few_ref, other_ref, *others):
        a_ins, b_ins = others[:first_a], others[first_a : first_a + first_b]
        *results, a_ref, b_ref = others[first_a + first_b :]
        gq_ref, gk_ref, gv_ref, go_ref, router_ref, g1_ref, g2_ref, table_ref = results
        mine = me_ref[0] & (ways - 1)
        place = me_ref[0] >> shift
        for order, ref, ins, chunk, start in (
            (order_a, a_ref, a_ins, chunk_a, 0),
            (order_b, b_ref, b_ins, chunk_b, a_rows),
        ):
            each = owners // len(ins)
            for at in range(owners):
                line = at % each
                ref[rel_of(at, order) ^ place] = ins[at // each][line * chunk : (line + 1) * chunk]
            for c in range(owners):
                low = start + c * chunk
                which, low = low // here, low % here
                (gq_ref, gk_ref, gv_ref, go_ref)[which][low : low + chunk] = ref[c]
        total = few_ref[...] + other_ref[...]
        own = total[:, 0:quarter]
        for t in range(1, ways):
            own = jnp.where(mine == t, total[:, t * quarter : (t + 1) * quarter], own)
        router_ref[...] = own[0:experts].astype(bf16)
        g2_ref[...] = own[experts].astype(bf16)
        g1_ref[...] = own[experts + 1].astype(bf16)
        lines = total[experts + 2 : experts + 2 + heads]
        table = lines[:, 0:bins]
        for t in range(1, ways):
            table = jnp.where(mine == t, lines[:, t * bins : (t + 1) * bins], table)
        table_ref[...] = table.astype(bf16)

    gq, gk, gv, go, g_router, g_one, g_two, g_table = run(
        unpack_body,
        [
            ((here, width), bf16),
            ((here, width), bf16),
            ((here, width), bf16),
            ((here, width), bf16),
            ((experts, quarter), bf16),
            ((quarter,), bf16),
            ((quarter,), bf16),
            ((heads, bins), bf16),
        ],
        (me, held["few"], held["few_other"], *a_blocks, *b_blocks),
        "unpack",
        us=1.0,
        scratch=[
            pltpu.VMEM((owners, chunk_a, width), bf16),
            pltpu.VMEM((owners, chunk_b, width), bf16),
        ],
    )
    return (
        layer_out.T,
        grad_tokens.T,
        gq.T,
        gk.T,
        gv.T,
        go,
        g_table.T,
        g_router.T,
        grad_in,
        grad_out,
        g_one,
        g_two,
    )


def solution(mesh):
    placed = (
        P("exp", "tp"),
        P(None, "tp"),
        P(None, "tp"),
        P(None, "tp"),
        P("tp", None),
        P(None, "tp"),
        P("tp", None),
        P("exp", None, "tp"),
        P("exp", "tp", None),
        P("tp"),
        P("tp"),
        P("exp", None),
        P("exp", None),
        P(),
        P("exp", "tp"),
    )
    return jax.shard_map(
        local,
        mesh=mesh,
        in_specs=placed,
        out_specs=(
            P("exp", "tp"),
            P("exp", "tp"),
            P(None, "tp"),
            P(None, "tp"),
            P(None, "tp"),
            P("tp", None),
            P(None, "tp"),
            P("tp", None),
            P("exp", None, "tp"),
            P("exp", "tp", None),
            P("tp"),
            P("tp"),
        ),
        check_vma=False,
    )
```

```python
import math

import jax
import jax.numpy as jnp
from jax import lax
from jax.experimental import pallas as pl
from jax.experimental.pallas import tpu as pltpu
from jax.sharding import PartitionSpec as P

HD = 64
EPSILON = 1e-06
NEG_FILL = -1e30
HIGHEST = lax.Precision.HIGHEST
LANES = 128
f32 = jnp.float32
bf16 = jnp.bfloat16
VMEM = pl.BlockSpec(memory_space=pltpu.VMEM)
SMEM = pl.BlockSpec(memory_space=pltpu.SMEM)


class Far:
    def __init__(self, value):
        self.value = pltpu.with_memory_space_constraint(value, pltpu.HBM)


class Loaded:
    def __init__(self, copy, held):
        self.copy, self.held = copy, held

    def wait(self):
        if self.copy is not None:
            self.copy.wait()
            self.copy = None

    def __getitem__(self, index):
        self.wait()
        return self.held[index]


class Stored:
    def __init__(self, copy, held):
        self.copy, self.held, self.started = copy, held, False

    def __setitem__(self, index, value):
        self.held[index] = value

    def __getitem__(self, index):
        return self.held[index]

    def send(self):
        if not self.started:
            self.started = True
            self.copy.start()


def run(body, outs, args, name, us=1.0, scratch=(), limit=16):
    far_in = [isinstance(a, Far) for a in args]
    args = [a.value if isinstance(a, Far) else a for a in args]
    far_out = [len(o) == 3 for o in outs]
    bufs = [pltpu.VMEM(a.shape, a.dtype) for a, far in zip(args, far_in) if far]
    bufs += [pltpu.VMEM(o[0], o[1]) for o, far in zip(outs, far_out) if far]
    n_in, n_out, n_own = len(args), len(outs), len(scratch)
    hbm = pl.BlockSpec(memory_space=pltpu.HBM)
    specs = [
        SMEM if a.shape == (1,) and a.dtype == jnp.int32 else hbm if far else VMEM
        for a, far in zip(args, far_in)
    ]
    moved = sum(a.size * a.dtype.itemsize for a in args)
    moved += sum(math.prod(o[0]) * jnp.dtype(o[1]).itemsize for o in outs)

    def wrapped(*refs):
        ins, results = refs[:n_in], refs[n_in : n_in + n_out]
        own = refs[n_in + n_out : n_in + n_out + n_own]
        held = refs[n_in + n_out + n_own :]
        given, at = [], 0
        for ref, far in zip((*ins, *results), (*far_in, *far_out)):
            if not far:
                given.append(ref)
                continue
            if len(given) < n_in:
                copy = pltpu.make_async_copy(ref, held[at], held[-1].at[at])
                copy.start()
                given.append(Loaded(copy, held[at]))
            else:
                copy = pltpu.make_async_copy(held[at], ref, held[-1].at[at])
                given.append(Stored(copy, held[at]))
            at += 1
        body(*given, *own)
        for g in given:
            if isinstance(g, Stored):
                g.send()
        for g in given:
            if isinstance(g, Stored):
                g.copy.wait()
            elif isinstance(g, Loaded):
                g.wait()

    sems = [pltpu.SemaphoreType.DMA((len(bufs),))] if bufs else []
    return pl.pallas_call(
        wrapped,
        out_shape=[
            pltpu.HBM(o[0], o[1]) if len(o) == 3 else jax.ShapeDtypeStruct(o[0], o[1])
            for o in outs
        ],
        in_specs=specs,
        out_specs=[hbm if far else VMEM for far in far_out],
        scratch_shapes=[*scratch, *bufs, *sems],
        compiler_params=pltpu.CompilerParams(vmem_limit_bytes=limit * 2**20),
        cost_estimate=pl.CostEstimate(
            flops=int(us * 1.1e9), bytes_accessed=moved, transcendentals=0
        ),
        name=name,
    )(*args)


def fetch(token, values, name):
    values = [pltpu.with_memory_space_constraint(v, pltpu.HBM) for v in values]
    count = len(values)

    def body(token_ref, *refs):
        ins, outs, sems = refs[:count], refs[count : 2 * count], refs[-1]
        copies = [
            pltpu.make_async_copy(i, o, sems.at[n]) for n, (i, o) in enumerate(zip(ins, outs))
        ]
        for c in copies:
            c.start()
        for c in copies:
            c.wait()

    return pl.pallas_call(
        body,
        out_shape=[jax.ShapeDtypeStruct(v.shape, v.dtype) for v in values],
        in_specs=[SMEM] + [pl.BlockSpec(memory_space=pltpu.HBM)] * count,
        out_specs=[VMEM] * count,
        scratch_shapes=[pltpu.SemaphoreType.DMA((count,))],
        compiler_params=pltpu.CompilerParams(vmem_limit_bytes=16 * 2**20),
        name=name,
    )(token, *values)


def swap(value, axis, mask):
    size = lax.axis_size(axis)
    return lax.ppermute(value, axis, [(i, i ^ mask) for i in range(size)])


def after(value, *others):
    return lax.optimization_barrier((value, *others))[0]


def mm(left, right):
    return jnp.dot(left, right, preferred_element_type=f32)


def mm_tn(left, right):
    return lax.dot_general(left, right, (((0,), (0,)), ((), ())), preferred_element_type=f32)


def mm_nt(left, right, precision=None):
    return lax.dot_general(
        left, right, (((1,), (1,)), ((), ())), precision=precision, preferred_element_type=f32
    )


def iota(shape, dim):
    return lax.broadcasted_iota(jnp.int32, shape, dim)


def absolute(pieces, me, place):
    picked = pieces[0]
    for rel in range(1, len(pieces)):
        picked = jnp.where((me ^ rel) == place, pieces[rel], picked)
    return picked


def split_low(value):
    high = value.astype(bf16)
    return high.astype(f32), value - high.astype(f32)


def two_lanes(value, count):
    high, low = split_low(value)
    lane = iota((value.shape[0], count), 1)
    return jnp.where(lane == 0, high, jnp.where(lane == 1, low, 0.0)).astype(bf16)


def gather_pieces(value):
    across = swap(value, "tp", 2)
    beside = swap(value, "tp", 1)
    return value, beside, across, swap(across, "tp", 1)


def scatter_sum(kept, passed, sent):
    came = swap(sent, "tp", 1)
    half = passed + came[1]
    return kept, came, swap(half, "tp", 2), half


def digits_of(count):
    digits, shift = [(0, 2)], 1
    while (1 << shift) < count:
        radix = min(4, count >> shift)
        digits.append((shift, radix))
        shift += radix.bit_length() - 1
    return digits


def rel_of(place, order):
    rel = 0
    for shift, radix in reversed(order):
        rel |= (place % radix) << shift
        place //= radix
    return rel


def trade(blocks, digit):
    shift, radix = digit
    return [swap(blocks[k], "exp", k << shift) for k in range(1, radix)]


def sum_blocks(kept, came):
    total = kept.astype(f32)
    for c in came:
        total = total + c.astype(f32)
    return total.astype(bf16)


def two_chains(a_blocks, b_blocks, order_a, order_b, tail, beside):
    for at, (digit_a, digit_b) in enumerate(zip(order_a, order_b)):
        b_came = trade(b_blocks, digit_b)
        a_came = trade(a_blocks, digit_a)
        got = beside((*b_came, *a_came), b_blocks[0])
        got = (*got[len(b_came) :], *got[: len(b_came)])
        a = sum_blocks(a_blocks[0], got[: len(a_came)])
        b = sum_blocks(b_blocks[0], got[len(a_came) :])
        few = b[b.shape[0] - tail :]
        if at + 1 < len(order_a):
            radix = order_a[at + 1][1]
            part = a.shape[0] // radix
            a_blocks = [a[k * part : (k + 1) * part] for k in range(radix)]
            radix = order_b[at + 1][1]
            part = (b.shape[0] - tail) // radix
            b_blocks = [
                jnp.concatenate([b[k * part : (k + 1) * part], few], axis=0) for k in range(radix)
            ]
    b = b[: b.shape[0] - tail]
    last = len(order_a) - 1
    early = []
    for at, (digit_a, digit_b) in enumerate(zip(order_a[::-1], order_b[::-1])):
        b_came = trade([b] * digit_b[1], digit_b)
        a_came = trade([rest if at == last else a] * digit_a[1], digit_a)
        ahead = trade([a] * order_a[0][1], order_a[0]) if at == last - 1 else []
        got = beside((*ahead, *b_came, *a_came), few)
        early += got[: len(ahead)]
        b_blocks = [b, *got[len(ahead) : len(ahead) + len(b_came)]]
        a_blocks = got[len(ahead) + len(b_came) :]
        if at == last - 1:
            own, rest = a, jnp.concatenate(a_blocks, axis=0)
        elif at < last:
            a = jnp.concatenate([a, *a_blocks], axis=0)
        if at < last:
            b = jnp.concatenate(b_blocks, axis=0)
    return [own, rest, *early, *a_blocks], b_blocks


def local(
    tokens,
    w_query,
    w_key,
    w_value,
    w_output,
    bias_table,
    w_router,
    w_in,
    w_out,
    gain_attn,
    gain_ffn,
    routes,
    segments,
    buckets,
    cotangent,
):
    length, quarter = tokens.shape
    ways = lax.axis_size("tp")
    owners = lax.axis_size("exp")
    width = quarter * ways
    here = w_query.shape[1]
    heads = here // HD
    experts = w_router.shape[1]
    bins = bias_table.shape[0]
    hidden_here = w_in.shape[2]
    capacity = max(2, length // owners * 9 // 8)
    per = -(-capacity // ways)
    while experts * per % LANES:
        per += 1
    rows = experts * per
    span = 2 * length
    tiles = length // LANES
    extra = -(-(experts + 2) // 16) * 16
    few_rows = -(-(experts + 2 + heads) // 16) * 16
    me = lax.axis_index(("exp", "tp")).astype(jnp.int32)[None]
    order_a = digits_of(owners)
    order_b = order_a[1:] + order_a[:1]
    first_a, first_b = order_a[0][1], order_b[0][1]
    shift = ways.bit_length() - 1

    tok_t = tokens.T
    wq_t, wk_t, wv_t = w_query.T, w_key.T, w_value.T

    def slot_body(
        me_ref, route_ref, cot_ref, *outs
    ):
        drow_ref, cots_ref = outs
        mine = me_ref[0] & (ways - 1)
        row = route_ref[...]
        above = iota((length, length), 0)
        along = iota((length, length), 1)
        col = jnp.sum(jnp.where(above == along, row, 0), axis=1, keepdims=True)
        same = col == row

        def dest(slot, expert):
            chunk = jnp.zeros_like(slot)
            for t in range(1, ways):
                chunk = chunk + (slot >= t * per).astype(jnp.int32)
            return (chunk ^ mine) * rows + expert * per + slot - chunk * per

        slot_row = jnp.sum(jnp.where(same & (above < along), 1, 0), axis=0, keepdims=True)
        dest_row = dest(slot_row, row)
        drow_ref[...] = dest_row
        cot = cot_ref[...]
        for rel in range(ways):
            hot = (iota((rows, length), 0) + rel * rows == dest_row).astype(bf16)
            piece = mm_nt(hot, cot).astype(bf16)
            cots_ref[rel] = piece

    dest_row, cots = run(
        slot_body,
        [
            ((1, length), jnp.int32),
            ((ways, rows, quarter), bf16),
        ],
        (
            me,
            Far(routes.T),
            Far(cotangent.T),
        ),
        "slots",
        us=0.7,
    )
    def small_body(router_ref, g1_ref, g2_ref, small_ref):
        line = iota((extra - experts, quarter), 0)
        gains = jnp.where(
            line == 0,
            g1_ref[...].astype(f32)[None],
            jnp.where(line == 1, g2_ref[...].astype(f32)[None], 0.0),
        )
        small_ref[...] = jnp.concatenate([router_ref[...].astype(f32), gains], 0).astype(bf16)

    (small_own,) = run(
        small_body,
        [((extra, quarter), bf16)],
        (Far(w_router.T), Far(gain_attn), Far(gain_ffn)),
        "small",
        us=0.2,
    )
    small_pieces = [small_own] + [swap(small_own, "tp", rel) for rel in range(1, ways)]
    tok_across = swap(tok_t, "tp", 2)
    tok_across, *small_pieces = lax.optimization_barrier((tok_across, *small_pieces))
    tok_pieces = (tok_t, swap(tok_t, "tp", 1), tok_across, swap(tok_across, "tp", 1))

    def over_experts(value):
        blocks = value.reshape(experts, per, value.shape[1])
        moved = lax.all_to_all(blocks, "exp", split_axis=0, concat_axis=0, tiled=True)
        return moved.reshape(rows, value.shape[1])

    def bucket_hot(ref, held, dtype):
        held[...] = jnp.full((1, span), -1, jnp.int32)
        held[:, 0 : buckets.shape[0]] = ref[...][None]
        return (iota((bins, span), 0) == held[...]).astype(dtype)

    def spread_row(few, line, count):
        pick = (iota((few.shape[0], count), 0) == line).astype(bf16)
        return mm_tn(few, pick)

    def attend_body(
        me_ref,
        t0,
        t1,
        t2,
        t3,
        c0,
        c1,
        c2,
        c3,
        wq_ref,
        wk_ref,
        wv_ref,
        wo_ref,
        table_ref,
        bucket_ref,
        seg_ref,
        dest_ref,
        small_ref,
        small_far,
        dest_far,
        r1_ref,
        n1_ref,
        q_ref,
        k_ref,
        v_ref,
        p0_ref,
        p1_ref,
        p2_ref,
        attn_ref,
        kept_ref,
        passed_ref,
        sent_ref,
        xrow_ref,
        x_ref,
        bucket_held,
    ):
        p_refs = (p0_ref, p1_ref, p2_ref)
        mine = me_ref[0] & (ways - 1)
        for rel, piece in enumerate((t0, t1, t2, t3)):
            at = pl.multiple_of((mine ^ rel) * quarter, quarter)
            x_ref[pl.ds(at, quarter), :] = piece[...]
        pieces = [c[...] for c in (c0, c1, c2, c3)]
        small = jnp.concatenate([absolute(pieces, mine, t) for t in range(ways)], axis=1)
        small_ref[...] = small
        small_far[...] = small
        small_far.send()
        dest_far[...] = dest_ref[...]
        dest_far.send()
        x_low = x_ref[...]
        x = x_low.astype(f32)
        r1 = lax.rsqrt(jnp.mean(x * x, axis=0, keepdims=True) + EPSILON)
        r1_ref[...] = r1
        r1_ref.send()
        n1 = (x * r1 * spread_row(small, experts, length)).astype(bf16)
        n1_ref[...] = n1
        n1_ref.send()
        q = mm(wq_ref[...], n1).astype(bf16)
        k = mm(wk_ref[...], n1).astype(bf16)
        v = mm(wv_ref[...], n1).astype(bf16)
        q_ref[...] = q
        k_ref[...] = k
        v_ref[...] = v
        for ref in (q_ref, k_ref, v_ref):
            ref.send()
        hot = bucket_hot(bucket_ref, bucket_held, bf16)
        offsets = mm(table_ref[...], hot)
        above = iota((length, length), 0)
        along = iota((length, length), 1)
        seg_row = seg_ref[...]
        seg_col = jnp.sum(jnp.where(above == along, seg_row, 0), axis=1, keepdims=True)
        same = seg_col == seg_row
        for h in range(heads):
            part = slice(h * HD, (h + 1) * HD)
            diagonals = []
            for d in range(2 * tiles - 1):
                window = offsets[h : h + 1, d * LANES : (d + 2) * LANES]
                spread = jnp.broadcast_to(window, (LANES, 2 * LANES))
                turned = pltpu.roll(spread, LANES + 1, 1, stride=1, stride_axis=0)
                diagonals.append(turned[:, :LANES])
            bias = jnp.concatenate(
                [
                    jnp.concatenate([diagonals[bi - bj + tiles - 1] for bi in range(tiles)], axis=1)
                    for bj in range(tiles)
                ],
                axis=0,
            )
            s = jnp.where(same, mm_tn(k[part], q[part]) + bias, NEG_FILL)
            e = jnp.exp(s - jnp.max(s, axis=0, keepdims=True))
            p = (e * (1.0 / jnp.sum(e, axis=0, keepdims=True))).astype(bf16)
            p_refs[h][...] = p
            p_refs[h].send()
            attn_ref[part] = mm(v[part], p).astype(bf16)
        attn = attn_ref[...]
        attn_ref.send()
        dest = dest_ref[...]
        wo = wo_ref[...]
        for rel, out in enumerate((kept_ref, sent_ref.at[0], passed_ref, sent_ref.at[1])):
            hot = (iota((rows, length), 0) + rel * rows == dest).astype(bf16)
            out[...] = mm(mm_nt(hot, attn).astype(bf16), wo).astype(bf16)
            if rel == 0:
                xrow_ref[...] = mm_nt(hot, x_low).astype(bf16)

    small, small_far, dest_far, r1, n1, q, k, v, p0, p1, p2, attn, *o_parts, x_rows = run(
        attend_body,
        [
            ((extra, width), bf16),
            ((extra, width), bf16, True),
            ((1, length), jnp.int32, True),
            ((1, length), f32, True),
            ((width, length), bf16, True),
            ((here, length), bf16, True),
            ((here, length), bf16, True),
            ((here, length), bf16, True),
            *[((length, length), bf16, True)] * heads,
            ((here, length), bf16, True),
            ((rows, width), bf16),
            ((rows, width), bf16),
            ((2, rows, width), bf16),
            ((rows, width), bf16),
        ],
        (
            me,
            *tok_pieces,
            *small_pieces,
            wq_t,
            wk_t,
            wv_t,
            w_output,
            bias_table.T,
            buckets,
            segments,
            dest_row,
        ),
        "attend",
        us=0.01,
        scratch=[pltpu.VMEM((width, length), bf16), pltpu.VMEM((1, span), jnp.int32)],
        limit=24,
    )
    o_kept, o_passed, o_sent = o_parts
    o_beside = swap(o_sent, "tp", 1)
    o_half = o_passed + o_beside[1]
    o_across = swap(o_half, "tp", 2)

    def join_body(me_ref, cots_ref, out_ref):
        for rel in range(ways):
            out_ref[:, rel * quarter : (rel + 1) * quarter] = cots_ref[rel]

    (d_send,) = run(join_body, [((rows, width), bf16)], (after(me, o_half), cots), "join", us=0.3)
    d_arrived = over_experts(d_send)

    def routed(kept_ref, beside_ref, across_ref, xrow_ref, small_ref):
        o = kept_ref[...].astype(f32) + beside_ref[0].astype(f32) + across_ref[...].astype(f32)
        h = xrow_ref[...].astype(f32) + o
        r2 = lax.rsqrt(jnp.mean(h * h, axis=-1, keepdims=True) + EPSILON)
        gain = small_ref[experts + 1 : experts + 2].astype(f32)
        n2 = h * r2 * gain
        logits = mm_nt(n2, small_ref[0:experts].astype(f32), HIGHEST)
        e = jnp.exp(logits - jnp.max(logits, axis=-1, keepdims=True))
        p = e / jnp.sum(e, axis=-1, keepdims=True)
        owner = iota((rows, experts), 0) - iota((rows, experts), 1) * per
        own = (owner >= 0) & (owner < per)
        g = jnp.sum(jnp.where(own, p, 0.0), axis=-1, keepdims=True)
        return h, r2, n2, p, g

    def route_body(kept_ref, beside_ref, across_ref, xrow_ref, small_ref, send_ref):
        h, r2, n2, p, g = routed(kept_ref, beside_ref, across_ref, xrow_ref, small_ref)
        send_ref[:, 0:width] = n2.astype(bf16)
        send_ref[:, width : width + LANES] = two_lanes(g, LANES)

    route_args = (o_kept, o_beside, o_across, x_rows, small)
    (send,) = run(
        route_body, [((rows, width + LANES), bf16)], route_args, "route", us=4
    )

    def state_body(
        me_ref, kept_ref, beside_ref, across_ref, xrow_ref, small_ref, c0, c1, c2, c3, *outs
    ):
        h_ref, aux_ref, dout_ref = outs
        mine = me_ref[0] & (ways - 1)
        pieces = [c[...] for c in (c0, c1, c2, c3)]
        dout_ref[...] = jnp.concatenate([absolute(pieces, mine, t) for t in range(ways)], axis=1)
        dout_ref.send()
        h, r2, n2, p, g = routed(kept_ref, beside_ref, across_ref, xrow_ref, small_ref)
        h_ref[...] = h
        h_ref.send()
        aux_ref[...] = jnp.zeros((rows, LANES), f32)
        aux_ref[:, 0:experts] = p
        aux_ref[:, LANES - 2 : LANES - 1] = r2
        aux_ref[:, LANES - 1 : LANES] = g

    later = after(cots, send)
    cot_pieces = [later[0]] + [swap(later[rel], "tp", rel) for rel in range(1, ways)]
    h_rows, aux, dout_rows = run(
        state_body,
        [
            ((rows, width), f32, True),
            ((rows, LANES), f32, True),
            ((rows, width), bf16, True),
        ],
        (after(me, send), *route_args, *cot_pieces),
        "state",
        us=0.01,
    )
    send, d_arrived = lax.optimization_barrier((send, d_arrived))
    d_pieces = gather_pieces(d_arrived)
    arrived, h_rows, aux, dout_rows, *d_pieces = lax.optimization_barrier(
        (over_experts(send), h_rows, aux, dout_rows, *d_pieces)
    )
    weights = fetch(after(me, arrived), [w_in, w_out], "expert_arguments")

    def dout_body(me_ref, d0, d1, d2, d3, out_ref):
        mine = me_ref[0] & (ways - 1)
        came = (d0, d1, d2, d3)
        for rel in range(ways):
            pieces = []
            for src in range(ways):
                at = (rel ^ src) * quarter
                pieces.append(came[src][:, at : at + quarter])
            dout = jnp.concatenate([absolute(pieces, mine, t) for t in range(ways)], axis=1)
            out_ref[rel * rows : (rel + 1) * rows] = dout

    (douts,) = run(
        dout_body,
        [((ways * rows, width), bf16)],
        (after(me, arrived), *d_pieces),
        "douts",
        us=0.01,
    )
    across, douts, *weights = lax.optimization_barrier(
        (swap(arrived, "tp", 2), douts, *weights)
    )
    arrived = (arrived, swap(arrived, "tp", 1), across, swap(across, "tp", 1))

    def expert_body(a0, a1, a2, a3, dout_ref, win_ref, wout_ref, *outs):
        u_ref, dy_ref, act_ref, dz_ref, kept_ref, passed_ref, sent_ref = outs
        for rel, a in enumerate((a0, a1, a2, a3)):
            part = slice(rel * rows, (rel + 1) * rows)
            u_ref[part] = a[:, 0:width]
            g = a[:, width : width + 1].astype(f32) + a[:, width + 1 : width + 2].astype(f32)
            dy_ref[part] = (g * dout_ref[part].astype(f32)).astype(bf16)
        u_ref.send()
        dy_ref.send()
        u = u_ref[...]
        dy = dy_ref[...]
        z = mm(u, win_ref[0])
        c = math.sqrt(2.0 / math.pi)
        z2 = z * z
        t = jnp.tanh(z * (c + (0.044715 * c) * z2))
        half = 0.5 + 0.5 * t
        wide_act = z * half
        act = wide_act.astype(bf16)
        act_ref[...] = act
        act_ref.send()
        slope = half + wide_act * (1.0 - t) * (c + (3 * 0.044715 * c) * z2)
        dact = mm_nt(dy, wout_ref[0])
        dot = jnp.sum(dact * act.astype(f32), axis=-1, keepdims=True)
        dz = (dact * slope).astype(bf16)
        dz_ref[...] = dz
        dz_ref.send()
        du = mm_nt(dz, win_ref[0]).astype(bf16)
        tail = two_lanes(dot, LANES)
        for rel, out in enumerate((kept_ref, sent_ref.at[0], passed_ref, sent_ref.at[1])):
            out[:, 0:width] = du[rel * rows : (rel + 1) * rows]
            out[:, width : width + LANES] = tail[rel * rows : (rel + 1) * rows]

    u_all, dy_all, act, dz, *du_parts = run(
        expert_body,
        [
            ((ways * rows, width), bf16, True),
            ((ways * rows, width), bf16, True),
            ((ways * rows, hidden_here), bf16, True),
            ((ways * rows, hidden_here), bf16, True),
            ((rows, width + LANES), bf16),
            ((rows, width + LANES), bf16),
            ((2, rows, width + LANES), bf16),
        ],
        (*arrived, douts, *weights),
        "expert",
        us=4.0,
        limit=24,
    )
    du_kept, du_beside, du_across, du_half = scatter_sum(*du_parts)
    du_sum = du_kept + du_beside[0] + du_across
    du_rows = over_experts(du_sum)

    def value_body(me_ref, act_ref, wout_ref, kept_ref, passed_ref, sent_ref):
        y = mm(act_ref[...], wout_ref[0]).astype(bf16)
        for rel, out in enumerate((kept_ref, sent_ref.at[0], passed_ref, sent_ref.at[1])):
            out[...] = y[rel * rows : (rel + 1) * rows]

    y_parts = run(
        value_body,
        [((rows, width), bf16), ((rows, width), bf16), ((2, rows, width), bf16)],
        (after(me, du_half), Far(act), w_out),
        "value",
        us=0.8,
    )
    y_kept, y_passed, y_sent = y_parts
    y_beside = swap(y_sent, "tp", 1)
    y_across = swap(after(y_passed + y_beside[1], du_sum), "tp", 2)
    y_sum = y_kept + y_beside[0] + y_across

    y_rows = over_experts(y_sum)
    state = fetch(after(me, du_sum), [h_rows, aux, dout_rows, small_far, dest_far], "state_again")
    du_rows, _, *state = lax.optimization_barrier((du_rows, y_sum, *state))

    def back_body(
        du_ref, h_ref, aux_ref, dout_ref, small_ref, dest_ref, do_ref, parts_ref, drow_ref
    ):
        drow_ref[...] = dest_ref[...]
        du = du_ref[:, 0:width].astype(f32)
        gg = du_ref[:, width : width + 1].astype(f32)
        gg = gg + du_ref[:, width + 1 : width + 2].astype(f32)
        h = h_ref[...]
        p = aux_ref[:, 0:experts]
        r2 = aux_ref[:, LANES - 2 : LANES - 1]
        gain = small_ref[experts + 1 : experts + 2].astype(f32)
        router = small_ref[0:experts].astype(f32)
        owner = iota((rows, experts), 0) - iota((rows, experts), 1) * per
        own = ((owner >= 0) & (owner < per)).astype(f32)
        dlogits = gg * (own - p)
        dn2 = du + lax.dot_general(
            dlogits, router, (((1,), (0,)), ((), ())), precision=HIGHEST, preferred_element_type=f32
        )
        hr = h * r2
        n2 = hr * gain
        inner = jnp.sum(dn2 * gain * h, axis=-1, keepdims=True)
        dh = dout_ref[...].astype(f32) + r2 * gain * dn2 - hr * (r2 * r2 / width) * inner
        do_ref[...] = dh.astype(bf16)
        parts_ref[...] = jnp.zeros((few_rows, width), f32)
        parts_ref[0:experts] = lax.dot_general(
            dlogits, n2, (((0,), (0,)), ((), ())), precision=HIGHEST, preferred_element_type=f32
        )
        parts_ref[experts : experts + 1] = jnp.sum(dn2 * hr, axis=0, keepdims=True)

    do_rows, few_parts, dest_near = run(
        back_body,
        [((rows, width), bf16), ((few_rows, width), f32), ((1, length), jnp.int32)],
        (du_rows, *state),
        "residual_back",
        us=2.0,
    )
    do_across = swap(do_rows, "tp", 2)
    do_beside = swap(do_rows, "tp", 1)
    wanted = [w_output, attn, q, k, v, p0, p1, p2, n1, wq_t, wk_t, wv_t, small_far]
    fetched = fetch(after(me, do_rows), wanted, "attend_again")
    do_across, *fetched = lax.optimization_barrier((do_across, *fetched))
    do_pieces = (do_rows, do_beside, do_across, swap(do_across, "tp", 1))

    a_rows = 4 * here * 2 // 3
    chunk_a = a_rows // owners
    chunk_b = (4 * here - a_rows) // owners
    a_part, b_part = a_rows // first_a, (4 * here - a_rows) // first_b

    def attend_back_body(
        me_ref,
        d0,
        d1,
        d2,
        d3,
        drow_ref,
        wo_ref,
        attn_ref,
        q_ref,
        k_ref,
        v_ref,
        p0_ref,
        p1_ref,
        p2_ref,
        n1_ref,
        wq_ref,
        wk_ref,
        wv_ref,
        small_ref,
        few_ref,
        bucket_ref,
        own_ref,
        kept_ref,
        passed_ref,
        sent_ref,
        *others,
    ):
        a_outs, b_outs = others[:first_a], others[first_a : first_a + first_b]
        a_ref, b_ref, dq_ref, dk_ref, dv_ref, all_ref, bucket_held = others[first_a + first_b :]
        mine = me_ref[0] & (ways - 1)
        place = me_ref[0] >> shift
        stack = jnp.concatenate([d[...] for d in (d0, d1, d2, d3)], axis=0)
        drow = drow_ref[...]
        eye = iota((length, length), 0) == iota((length, length), 1)
        dcol = jnp.sum(jnp.where(eye, drow, 0), axis=1, keepdims=True)
        hot_t = (iota((length, ways * rows), 1) == dcol).astype(bf16)
        do = mm(hot_t, stack).astype(bf16)
        own = stack[:, 0:quarter]
        for t in range(1, ways):
            own = jnp.where(mine == t, stack[:, t * quarter : (t + 1) * quarter], own)
        hot = (iota((ways * rows, length), 0) == drow).astype(bf16)
        own_ref[...] = mm_tn(own, hot).astype(bf16)
        wo = wo_ref[...]
        da = mm_nt(wo, do).astype(bf16)
        hot = bucket_hot(bucket_ref, bucket_held, f32)
        flip = (iota((LANES, LANES), 0) + iota((LANES, LANES), 1) == LANES - 1).astype(bf16)
        tables = []
        for h in range(heads):
            part = slice(h * HD, (h + 1) * HD)
            p_low = (p0_ref, p1_ref, p2_ref)[h][...]
            p = p_low.astype(f32)
            dp = mm_tn(v_ref[part], da[part])
            dv_ref[part] = mm_nt(da[part], p_low).astype(bf16)
            inner = jnp.sum(p * dp, axis=0, keepdims=True)
            ds = (p * (dp - inner)).astype(bf16)
            dq_ref[part] = mm(k_ref[part], ds).astype(bf16)
            dk_ref[part] = mm_nt(q_ref[part], ds).astype(bf16)
            rows_of = [mm(flip, ds[bj * LANES : (bj + 1) * LANES]) for bj in range(tiles)]
            offsets = jnp.zeros((1, span), f32)
            for d in range(2 * tiles - 1):
                block = jnp.zeros((LANES, LANES), f32)
                for bj in range(tiles):
                    bi = bj + d - tiles + 1
                    if 0 <= bi < tiles:
                        block = block + rows_of[bj][:, bi * LANES : (bi + 1) * LANES]
                block = jnp.concatenate([block, jnp.zeros_like(block)], axis=1)
                block = pltpu.roll(block, 0, 1, stride=1, stride_axis=0)
                block = [jnp.sum(block, axis=0, keepdims=True)]
                if d:
                    block = [jnp.zeros((1, d * LANES), f32), *block]
                if d < 2 * tiles - 2:
                    block = [*block, jnp.zeros((1, span - (d + 2) * LANES), f32)]
                offsets = offsets + jnp.concatenate(block, axis=1)
            tables.append(mm_nt(offsets, hot, HIGHEST))
        n1 = n1_ref[...]
        gq = mm_nt(dq_ref[...], n1)
        gk = mm_nt(dk_ref[...], n1)
        gv = mm_nt(dv_ref[...], n1)
        back = gq * wq_ref[...].astype(f32) + gk * wk_ref[...].astype(f32)
        back = jnp.sum(back + gv * wv_ref[...].astype(f32), axis=0, keepdims=True)
        gain = small_ref[experts : experts + 1].astype(f32)
        gwo = mm(attn_ref[...], do)
        parts = [t.astype(bf16) for t in (gq, gk, gv, gwo)]
        for ref, chunk, start in ((a_ref, chunk_a, 0), (b_ref, chunk_b, a_rows)):
            for c in range(owners):
                low = start + c * chunk
                which, low = low // here, low % here
                ref[c] = parts[which][low : low + chunk]
        for order, ref, outs, chunk in (
            (order_a, a_ref, a_outs, chunk_a),
            (order_b, b_ref, b_outs, chunk_b),
        ):
            each = owners // len(outs)
            for at in range(owners):
                line = at % each
                outs[at // each][line * chunk : (line + 1) * chunk] = ref[rel_of(at, order) ^ place]
        few = few_ref[...]
        line = iota((few_rows, 1), 0)
        few = few + jnp.where(line == experts + 1, back / gain, 0.0)
        wide = jnp.concatenate(
            [jnp.concatenate([tables[h] * (mine == t).astype(f32) for t in range(ways)], axis=1)
             for h in range(heads)],
            axis=0,
        )
        pad = jnp.zeros((heads, width - ways * bins), f32)
        wide = jnp.concatenate([wide, pad], axis=1)
        for h in range(heads):
            few = few + jnp.where(line == experts + 2 + h, wide[h : h + 1], 0.0)
        few = few.astype(bf16)
        for out in b_outs:
            out[b_part : b_part + few_rows] = few
        dn1 = mm_tn(wq_ref[...], dq_ref[...])
        dn1 = dn1 + mm_tn(wk_ref[...], dk_ref[...])
        dn1 = dn1 + mm_tn(wv_ref[...], dv_ref[...])
        all_ref[...] = dn1.astype(bf16)
        dot = jnp.sum(dn1 * n1.astype(f32), axis=0, keepdims=True)
        high, low = split_low(dot)
        line = iota((16, length), 0)
        tail = jnp.where(line == 0, high, jnp.where(line == 1, low, 0.0)).astype(bf16)
        for rel, out in enumerate((kept_ref, sent_ref.at[0], passed_ref, sent_ref.at[1])):
            at = pl.multiple_of((mine ^ rel) * quarter, quarter)
            out[0:quarter] = all_ref[pl.ds(at, quarter), :]
            out[quarter : quarter + 16] = tail

    dh_own, *others = run(
        attend_back_body,
        [
            ((quarter, length), bf16),
            ((quarter + 16, length), bf16),
            ((quarter + 16, length), bf16),
            ((2, quarter + 16, length), bf16),
            *[((a_part, width), bf16)] * first_a,
            *[((b_part + few_rows, width), bf16)] * first_b,
        ],
        (
            me,
            *do_pieces,
            dest_near,
            *fetched,
            few_parts,
            buckets,
        ),
        "attend_back",
        us=0.01,
        scratch=[
            pltpu.VMEM((owners, chunk_a, width), bf16),
            pltpu.VMEM((owners, chunk_b, width), bf16),
            pltpu.VMEM((here, length), bf16),
            pltpu.VMEM((here, length), bf16),
            pltpu.VMEM((here, length), bf16),
            pltpu.VMEM((width, length), bf16),
            pltpu.VMEM((1, span), jnp.int32),
        ],
        limit=32,
    )

    y_rows, *others = lax.optimization_barrier((y_rows, *others))
    dn1_kept, dn1_passed, dn1_sent = others[:3]
    held = {}

    def tokens_body(
        me_ref, kept_ref, beside_ref, across_ref, dh_ref, tok_ref, r1_ref, small_ref, out_ref
    ):
        mine = me_ref[0] & (ways - 1)
        total = kept_ref[...].astype(f32) + beside_ref[0].astype(f32)
        total = total + across_ref[...].astype(f32)
        dn1 = total[0:quarter]
        dot = total[quarter : quarter + 1] + total[quarter + 1 : quarter + 2]
        one = r1_ref[...]
        small = small_ref[...]
        own = small[:, 0:quarter]
        for t in range(1, ways):
            own = jnp.where(mine == t, small[:, t * quarter : (t + 1) * quarter], own)
        gain = spread_row(own, experts, length)
        x = tok_ref[...].astype(f32)
        out_ref[...] = (
            dh_ref[...].astype(f32) + one * gain * dn1 - x * (one * one / width) * dot
        ).astype(bf16)

    def out_rows_body(me_ref, h_ref, aux_ref, y_ref, o0, o1, o2, o3, all_ref):
        mine = me_ref[0] & (ways - 1)
        out = (h_ref[...] + aux_ref[:, LANES - 1 : LANES] * y_ref[...].astype(f32)).astype(bf16)
        eye = (iota((rows, rows), 0) == iota((rows, rows), 1)).astype(bf16)
        all_ref[...] = mm_tn(out, eye).astype(bf16)
        for rel, piece in enumerate((o0, o1, o2, o3)):
            at = pl.multiple_of((mine ^ rel) * quarter, quarter)
            piece[...] = all_ref[pl.ds(at, quarter), :]

    def out_body(dest_ref, l0, l1, l2, l3, out_ref):
        dest = dest_ref[...]
        total = jnp.zeros((quarter, length), f32)
        for rel, piece in enumerate((l0, l1, l2, l3)):
            hot = (iota((rows, length), 0) + rel * rows == dest).astype(bf16)
            total = total + mm(piece[...], hot)
        out_ref[...] = total.astype(bf16)

    def weights_body(me_ref, u_ref, dy_ref, act_ref, dz_ref, gin_ref, gout_ref):
        gin_ref[0] = mm_tn(u_ref[...], dz_ref[...]).astype(bf16)
        gout_ref[0] = mm_tn(act_ref[...], dy_ref[...]).astype(bf16)

    def beside(came, block):
        phase = held.setdefault("phase", 0)
        held["phase"] += 1
        last = 2 * len(order_a) - 1
        extras = {}
        if phase == 0:
            extras["dn1_beside"] = swap(dn1_sent, "tp", 1)
            extras["grad_in"], extras["grad_out"] = run(
                weights_body,
                [((1, width, hidden_here), bf16), ((1, hidden_here, width), bf16)],
                (after(me, dn1_sent), Far(u_all), Far(dy_all), Far(act), Far(dz)),
                "expert_weights",
                us=12,
            )
        if phase == 1:
            half = dn1_passed + held["dn1_beside"][1]
            extras["dn1_across"] = swap(half, "tp", 2)
            lo = run(
                out_rows_body,
                [((quarter, rows), bf16)] * ways,
                (me, Far(h_rows), Far(aux), y_rows),
                "layer_rows",
                us=12,
                scratch=[pltpu.VMEM((width, rows), bf16)],
            )
            for rel in range(ways):
                extras["lo%d" % rel] = lo[rel]
        if phase == last - 1:
            few = block.astype(f32)
            extras["few"] = few + swap(few, "tp", 1)
            for rel in range(1, ways):
                extras["lo%d" % rel] = swap(held["lo%d" % rel], "tp", rel)
        if phase == last:
            extras["few_other"] = swap(held["few"], "tp", 2)
            (extras["layer_out"],) = run(
                out_body,
                [((quarter, length), bf16)],
                (Far(dest_far), *[held["lo%d" % rel] for rel in range(ways)]),
                "layer_out",
                us=12,
            )
            (extras["grad_tokens"],) = run(
                tokens_body,
                [((quarter, length), bf16)],
                (
                    after(me, held["few"]),
                    dn1_kept,
                    held["dn1_beside"],
                    held["dn1_across"],
                    dh_own,
                    Far(tok_t),
                    Far(r1),
                    Far(small_far),
                ),
                "tokens_back",
                us=12,
            )
        names = list(extras)
        got = lax.optimization_barrier((*[extras[n] for n in names], *came))
        held.update(zip(names, got))
        return got[len(names) :]

    a_blocks, b_blocks = two_chains(
        others[3 : 3 + first_a], others[3 + first_a :], order_a, order_b, few_rows, beside
    )
    layer_out, grad_tokens = held["layer_out"], held["grad_tokens"]
    grad_in, grad_out = held["grad_in"], held["grad_out"]

    def unpack_body(me_ref, few_ref, other_ref, *others):
        a_ins, b_ins = others[: len(a_blocks)], others[len(a_blocks) :][:first_b]
        *results, a_ref, b_ref = others[len(a_blocks) + first_b :]
        gq_ref, gk_ref, gv_ref, go_ref, router_ref, g1_ref, g2_ref, table_ref = results
        mine = me_ref[0] & (ways - 1)
        place = me_ref[0] >> shift
        for order, ref, ins, chunk, start in (
            (order_a, a_ref, a_ins, chunk_a, 0),
            (order_b, b_ref, b_ins, chunk_b, a_rows),
        ):
            at = 0
            for piece in ins:
                for line in range(piece.shape[0] // chunk):
                    low = line * chunk
                    ref[rel_of(at, order) ^ place] = piece[low : low + chunk]
                    at += 1
            for c in range(owners):
                low = start + c * chunk
                which, low = low // here, low % here
                (gq_ref, gk_ref, gv_ref, go_ref)[which][low : low + chunk] = ref[c]
        total = few_ref[...] + other_ref[...]
        own = total[:, 0:quarter]
        for t in range(1, ways):
            own = jnp.where(mine == t, total[:, t * quarter : (t + 1) * quarter], own)
        router_ref[...] = own[0:experts].astype(bf16)
        g2_ref[...] = own[experts].astype(bf16)
        g1_ref[...] = own[experts + 1].astype(bf16)
        lines = total[experts + 2 : experts + 2 + heads]
        table = lines[:, 0:bins]
        for t in range(1, ways):
            table = jnp.where(mine == t, lines[:, t * bins : (t + 1) * bins], table)
        table_ref[...] = table.astype(bf16)

    gq, gk, gv, go, g_router, g_one, g_two, g_table = run(
        unpack_body,
        [
            ((here, width), bf16),
            ((here, width), bf16),
            ((here, width), bf16),
            ((here, width), bf16),
            ((experts, quarter), bf16),
            ((quarter,), bf16),
            ((quarter,), bf16),
            ((heads, bins), bf16),
        ],
        (me, held["few"], held["few_other"], *a_blocks, *b_blocks),
        "unpack",
        us=1.0,
        scratch=[
            pltpu.VMEM((owners, chunk_a, width), bf16),
            pltpu.VMEM((owners, chunk_b, width), bf16),
        ],
    )
    return (
        layer_out.T,
        grad_tokens.T,
        gq.T,
        gk.T,
        gv.T,
        go,
        g_table.T,
        g_router.T,
        grad_in,
        grad_out,
        g_one,
        g_two,
    )


def solution(mesh):
    placed = (
        P("exp", "tp"),
        P(None, "tp"),
        P(None, "tp"),
        P(None, "tp"),
        P("tp", None),
        P(None, "tp"),
        P("tp", None),
        P("exp", None, "tp"),
        P("exp", "tp", None),
        P("tp"),
        P("tp"),
        P("exp", None),
        P("exp", None),
        P(),
        P("exp", "tp"),
    )
    return jax.shard_map(
        local,
        mesh=mesh,
        in_specs=placed,
        out_specs=(
            P("exp", "tp"),
            P("exp", "tp"),
            P(None, "tp"),
            P(None, "tp"),
            P(None, "tp"),
            P("tp", None),
            P(None, "tp"),
            P("tp", None),
            P("exp", None, "tp"),
            P("exp", "tp", None),
            P("tp"),
            P("tp"),
        ),
        check_vma=False,
    )
```

```python
import math

import jax
import jax.numpy as jnp
from jax import lax
from jax.experimental import pallas as pl
from jax.experimental.pallas import tpu as pltpu
from jax.sharding import PartitionSpec as P

HD = 64
EPSILON = 1e-06
NEG_FILL = -1e30
HIGHEST = lax.Precision.HIGHEST
LANES = 128
f32 = jnp.float32
bf16 = jnp.bfloat16
VMEM = pl.BlockSpec(memory_space=pltpu.VMEM)
SMEM = pl.BlockSpec(memory_space=pltpu.SMEM)


class Far:
    def __init__(self, value):
        self.value = pltpu.with_memory_space_constraint(value, pltpu.HBM)


class Loaded:
    def __init__(self, copy, held):
        self.copy, self.held = copy, held

    def wait(self):
        if self.copy is not None:
            self.copy.wait()
            self.copy = None

    def __getitem__(self, index):
        self.wait()
        return self.held[index]


class Stored:
    def __init__(self, copy, held):
        self.copy, self.held, self.started = copy, held, False

    def __setitem__(self, index, value):
        self.held[index] = value

    def __getitem__(self, index):
        return self.held[index]

    def send(self):
        if not self.started:
            self.started = True
            self.copy.start()


def run(body, outs, args, name, us=1.0, scratch=(), limit=16):
    far_in = [isinstance(a, Far) for a in args]
    args = [a.value if isinstance(a, Far) else a for a in args]
    far_out = [len(o) == 3 for o in outs]
    bufs = [pltpu.VMEM(a.shape, a.dtype) for a, far in zip(args, far_in) if far]
    bufs += [pltpu.VMEM(o[0], o[1]) for o, far in zip(outs, far_out) if far]
    n_in, n_out, n_own = len(args), len(outs), len(scratch)
    hbm = pl.BlockSpec(memory_space=pltpu.HBM)
    specs = [
        SMEM if a.shape == (1,) and a.dtype == jnp.int32 else hbm if far else VMEM
        for a, far in zip(args, far_in)
    ]
    moved = sum(a.size * a.dtype.itemsize for a in args)
    moved += sum(math.prod(o[0]) * jnp.dtype(o[1]).itemsize for o in outs)

    def wrapped(*refs):
        ins, results = refs[:n_in], refs[n_in : n_in + n_out]
        own = refs[n_in + n_out : n_in + n_out + n_own]
        held = refs[n_in + n_out + n_own :]
        given, at = [], 0
        for ref, far in zip((*ins, *results), (*far_in, *far_out)):
            if not far:
                given.append(ref)
                continue
            if len(given) < n_in:
                copy = pltpu.make_async_copy(ref, held[at], held[-1].at[at])
                copy.start()
                given.append(Loaded(copy, held[at]))
            else:
                copy = pltpu.make_async_copy(held[at], ref, held[-1].at[at])
                given.append(Stored(copy, held[at]))
            at += 1
        body(*given, *own)
        for g in given:
            if isinstance(g, Stored):
                g.send()
        for g in given:
            if isinstance(g, Stored):
                g.copy.wait()
            elif isinstance(g, Loaded):
                g.wait()

    sems = [pltpu.SemaphoreType.DMA((len(bufs),))] if bufs else []
    return pl.pallas_call(
        wrapped,
        out_shape=[
            pltpu.HBM(o[0], o[1]) if len(o) == 3 else jax.ShapeDtypeStruct(o[0], o[1])
            for o in outs
        ],
        in_specs=specs,
        out_specs=[hbm if far else VMEM for far in far_out],
        scratch_shapes=[*scratch, *bufs, *sems],
        compiler_params=pltpu.CompilerParams(vmem_limit_bytes=limit * 2**20),
        cost_estimate=pl.CostEstimate(
            flops=int(us * 1.1e9), bytes_accessed=moved, transcendentals=0
        ),
        name=name,
    )(*args)


def fetch(token, values, name):
    values = [pltpu.with_memory_space_constraint(v, pltpu.HBM) for v in values]
    count = len(values)

    def body(token_ref, *refs):
        ins, outs, sems = refs[:count], refs[count : 2 * count], refs[-1]
        copies = [
            pltpu.make_async_copy(i, o, sems.at[n]) for n, (i, o) in enumerate(zip(ins, outs))
        ]
        for c in copies:
            c.start()
        for c in copies:
            c.wait()

    return pl.pallas_call(
        body,
        out_shape=[jax.ShapeDtypeStruct(v.shape, v.dtype) for v in values],
        in_specs=[SMEM] + [pl.BlockSpec(memory_space=pltpu.HBM)] * count,
        out_specs=[VMEM] * count,
        scratch_shapes=[pltpu.SemaphoreType.DMA((count,))],
        compiler_params=pltpu.CompilerParams(vmem_limit_bytes=16 * 2**20),
        name=name,
    )(token, *values)


def store(values, name):
    count = len(values)

    def body(*refs):
        ins, outs, sems = refs[:count], refs[count : 2 * count], refs[-1]
        copies = [
            pltpu.make_async_copy(i, o, sems.at[n]) for n, (i, o) in enumerate(zip(ins, outs))
        ]
        for c in copies:
            c.start()
        for c in copies:
            c.wait()

    return pl.pallas_call(
        body,
        out_shape=[pltpu.HBM(v.shape, v.dtype) for v in values],
        in_specs=[VMEM] * count,
        out_specs=[pl.BlockSpec(memory_space=pltpu.HBM)] * count,
        scratch_shapes=[pltpu.SemaphoreType.DMA((count,))],
        compiler_params=pltpu.CompilerParams(vmem_limit_bytes=16 * 2**20),
        name=name,
    )(*values)


def swap(value, axis, mask):
    size = lax.axis_size(axis)
    return lax.ppermute(value, axis, [(i, i ^ mask) for i in range(size)])


def after(value, *others):
    return lax.optimization_barrier((value, *others))[0]


def mm(left, right):
    return jnp.dot(left, right, preferred_element_type=f32)


def mm_tn(left, right):
    return lax.dot_general(left, right, (((0,), (0,)), ((), ())), preferred_element_type=f32)


def mm_nt(left, right, precision=None):
    return lax.dot_general(
        left, right, (((1,), (1,)), ((), ())), precision=precision, preferred_element_type=f32
    )


def iota(shape, dim):
    return lax.broadcasted_iota(jnp.int32, shape, dim)


def absolute(pieces, me, place):
    picked = pieces[0]
    for rel in range(1, len(pieces)):
        picked = jnp.where((me ^ rel) == place, pieces[rel], picked)
    return picked


def split_low(value):
    high = value.astype(bf16)
    return high.astype(f32), value - high.astype(f32)


def two_lanes(value, count):
    high, low = split_low(value)
    lane = iota((value.shape[0], count), 1)
    return jnp.where(lane == 0, high, jnp.where(lane == 1, low, 0.0)).astype(bf16)


def gather_pieces(value):
    across = swap(value, "tp", 2)
    beside = swap(value, "tp", 1)
    return value, beside, across, swap(across, "tp", 1)


def scatter_sum(kept, passed, sent):
    came = swap(sent, "tp", 1)
    half = passed + came[1]
    return kept, came, swap(half, "tp", 2), half


def digits_of(count):
    digits, shift = [(0, 2)], 1
    while (1 << shift) < count:
        radix = min(4, count >> shift)
        digits.append((shift, radix))
        shift += radix.bit_length() - 1
    return digits


def rel_of(place, order):
    rel = 0
    for shift, radix in reversed(order):
        rel |= (place % radix) << shift
        place //= radix
    return rel


def trade(blocks, digit):
    shift, radix = digit
    return [swap(blocks[k], "exp", k << shift) for k in range(1, radix)]


def sum_blocks(kept, came):
    total = kept.astype(f32)
    for c in came:
        total = total + c.astype(f32)
    return total.astype(bf16)


def two_chains(a_blocks, b_blocks, order_a, order_b, tail, beside):
    for at, (digit_a, digit_b) in enumerate(zip(order_a, order_b)):
        b_came = trade(b_blocks, digit_b)
        a_came = trade(a_blocks, digit_a)
        got = beside((*b_came, *a_came), b_blocks[0])
        got = (*got[len(b_came) :], *got[: len(b_came)])
        a = sum_blocks(a_blocks[0], got[: len(a_came)])
        b = sum_blocks(b_blocks[0], got[len(a_came) :])
        few = b[b.shape[0] - tail :]
        if at + 1 < len(order_a):
            radix = order_a[at + 1][1]
            part = a.shape[0] // radix
            a_blocks = [a[k * part : (k + 1) * part] for k in range(radix)]
            radix = order_b[at + 1][1]
            part = (b.shape[0] - tail) // radix
            b_blocks = [
                jnp.concatenate([b[k * part : (k + 1) * part], few], axis=0) for k in range(radix)
            ]
    b = b[: b.shape[0] - tail]
    last = len(order_a) - 1
    early = []
    for at, (digit_a, digit_b) in enumerate(zip(order_a[::-1], order_b[::-1])):
        b_came = trade([b] * digit_b[1], digit_b)
        a_came = trade([rest if at == last else a] * digit_a[1], digit_a)
        ahead = trade([a] * order_a[0][1], order_a[0]) if at == last - 1 else []
        got = beside((*ahead, *b_came, *a_came), few)
        early += got[: len(ahead)]
        b_blocks = [b, *got[len(ahead) : len(ahead) + len(b_came)]]
        a_blocks = got[len(ahead) + len(b_came) :]
        if at == last - 1:
            own, rest = a, jnp.concatenate(a_blocks, axis=0)
        elif at < last:
            a = jnp.concatenate([a, *a_blocks], axis=0)
        if at < last:
            b = jnp.concatenate(b_blocks, axis=0)
    return [own, rest, *early, *a_blocks], b_blocks


def local(
    tokens,
    w_query,
    w_key,
    w_value,
    w_output,
    bias_table,
    w_router,
    w_in,
    w_out,
    gain_attn,
    gain_ffn,
    routes,
    segments,
    buckets,
    cotangent,
):
    length, quarter = tokens.shape
    ways = lax.axis_size("tp")
    owners = lax.axis_size("exp")
    width = quarter * ways
    here = w_query.shape[1]
    heads = here // HD
    experts = w_router.shape[1]
    bins = bias_table.shape[0]
    hidden_here = w_in.shape[2]
    capacity = max(2, length // owners * 9 // 8)
    per = -(-capacity // ways)
    while experts * per % LANES:
        per += 1
    rows = experts * per
    span = 2 * length
    tiles = length // LANES
    extra = -(-(experts + 2) // 16) * 16
    few_rows = -(-(experts + 2 + heads) // 16) * 16
    me = lax.axis_index(("exp", "tp")).astype(jnp.int32)[None]
    order_a = digits_of(owners)
    order_b = order_a[1:] + order_a[:1]
    first_a, first_b = order_a[0][1], order_b[0][1]
    shift = ways.bit_length() - 1

    tok_t = tokens.T
    wq_t, wk_t, wv_t = w_query.T, w_key.T, w_value.T

    def slot_body(
        me_ref, route_ref, cot_ref, *outs
    ):
        drow_ref, cots_ref = outs
        mine = me_ref[0] & (ways - 1)
        row = route_ref[...]
        above = iota((length, length), 0)
        along = iota((length, length), 1)
        col = jnp.sum(jnp.where(above == along, row, 0), axis=1, keepdims=True)
        same = col == row

        def dest(slot, expert):
            chunk = jnp.zeros_like(slot)
            for t in range(1, ways):
                chunk = chunk + (slot >= t * per).astype(jnp.int32)
            return (chunk ^ mine) * rows + expert * per + slot - chunk * per

        slot_row = jnp.sum(jnp.where(same & (above < along), 1, 0), axis=0, keepdims=True)
        dest_row = dest(slot_row, row)
        drow_ref[...] = dest_row
        cot = cot_ref[...]
        for rel in range(ways):
            hot = (iota((rows, length), 0) + rel * rows == dest_row).astype(bf16)
            piece = mm_nt(hot, cot).astype(bf16)
            cots_ref[rel] = piece

    dest_row, cots = run(
        slot_body,
        [
            ((1, length), jnp.int32),
            ((ways, rows, quarter), bf16),
        ],
        (
            me,
            Far(routes.T),
            Far(cotangent.T),
        ),
        "slots",
        us=0.7,
    )
    def small_body(router_ref, g1_ref, g2_ref, small_ref):
        line = iota((extra - experts, quarter), 0)
        gains = jnp.where(
            line == 0,
            g1_ref[...].astype(f32)[None],
            jnp.where(line == 1, g2_ref[...].astype(f32)[None], 0.0),
        )
        small_ref[...] = jnp.concatenate([router_ref[...].astype(f32), gains], 0).astype(bf16)

    (small_own,) = run(
        small_body,
        [((extra, quarter), bf16)],
        (Far(w_router.T), Far(gain_attn), Far(gain_ffn)),
        "small",
        us=0.2,
    )
    small_pieces = [small_own] + [swap(small_own, "tp", rel) for rel in range(1, ways)]
    tok_across = swap(tok_t, "tp", 2)
    tok_across, dest_row, *small_pieces = lax.optimization_barrier(
        (tok_across, dest_row, *small_pieces)
    )
    tok_pieces = (tok_t, swap(tok_t, "tp", 1), tok_across, swap(tok_across, "tp", 1))

    def over_experts(value):
        blocks = value.reshape(experts, per, value.shape[1])
        moved = lax.all_to_all(blocks, "exp", split_axis=0, concat_axis=0, tiled=True)
        return moved.reshape(rows, value.shape[1])

    def bucket_hot(ref, held, dtype):
        held[...] = jnp.full((1, span), -1, jnp.int32)
        held[:, 0 : buckets.shape[0]] = ref[...][None]
        return (iota((bins, span), 0) == held[...]).astype(dtype)

    def spread_row(few, line, count):
        pick = (iota((few.shape[0], count), 0) == line).astype(bf16)
        return mm_tn(few, pick)

    def attend_body(
        me_ref,
        t0,
        t1,
        t2,
        t3,
        c0,
        c1,
        c2,
        c3,
        wq_ref,
        wk_ref,
        wv_ref,
        wo_ref,
        table_ref,
        bucket_ref,
        seg_ref,
        dest_ref,
        small_ref,
        dest_far,
        r1_ref,
        n1_ref,
        q_ref,
        k_ref,
        v_ref,
        p0_ref,
        p1_ref,
        p2_ref,
        attn_ref,
        kept_ref,
        passed_ref,
        sent_ref,
        xrow_ref,
        x_ref,
        bucket_held,
    ):
        p_refs = (p0_ref, p1_ref, p2_ref)
        mine = me_ref[0] & (ways - 1)
        for rel, piece in enumerate((t0, t1, t2, t3)):
            at = pl.multiple_of((mine ^ rel) * quarter, quarter)
            x_ref[pl.ds(at, quarter), :] = piece[...]
        pieces = [c[...] for c in (c0, c1, c2, c3)]
        small = jnp.concatenate([absolute(pieces, mine, t) for t in range(ways)], axis=1)
        small_ref[...] = small
        dest_far[...] = dest_ref[...]
        x_low = x_ref[...]
        x = x_low.astype(f32)
        r1 = lax.rsqrt(jnp.mean(x * x, axis=0, keepdims=True) + EPSILON)
        r1_ref[...] = r1
        n1 = (x * r1 * spread_row(small, experts, length)).astype(bf16)
        n1_ref[...] = n1
        q = mm(wq_ref[...], n1).astype(bf16)
        k = mm(wk_ref[...], n1).astype(bf16)
        v = mm(wv_ref[...], n1).astype(bf16)
        q_ref[...] = q
        k_ref[...] = k
        v_ref[...] = v
        hot = bucket_hot(bucket_ref, bucket_held, bf16)
        offsets = mm(table_ref[...], hot)
        above = iota((length, length), 0)
        along = iota((length, length), 1)
        seg_row = seg_ref[...]
        seg_col = jnp.sum(jnp.where(above == along, seg_row, 0), axis=1, keepdims=True)
        same = seg_col == seg_row
        for h in range(heads):
            part = slice(h * HD, (h + 1) * HD)
            diagonals = []
            for d in range(2 * tiles - 1):
                window = offsets[h : h + 1, d * LANES : (d + 2) * LANES]
                spread = jnp.broadcast_to(window, (LANES, 2 * LANES))
                turned = pltpu.roll(spread, LANES + 1, 1, stride=1, stride_axis=0)
                diagonals.append(turned[:, :LANES])
            bias = jnp.concatenate(
                [
                    jnp.concatenate([diagonals[bi - bj + tiles - 1] for bi in range(tiles)], axis=1)
                    for bj in range(tiles)
                ],
                axis=0,
            )
            s = jnp.where(same, mm_tn(k[part], q[part]) + bias, NEG_FILL)
            e = jnp.exp(s - jnp.max(s, axis=0, keepdims=True))
            p = (e * (1.0 / jnp.sum(e, axis=0, keepdims=True))).astype(bf16)
            p_refs[h][...] = p
            attn_ref[part] = mm(v[part], p).astype(bf16)
        attn = attn_ref[...]
        dest = dest_ref[...]
        wo = wo_ref[...]
        for rel, out in enumerate((kept_ref, sent_ref.at[0], passed_ref, sent_ref.at[1])):
            hot = (iota((rows, length), 0) + rel * rows == dest).astype(bf16)
            out[...] = mm(mm_nt(hot, attn).astype(bf16), wo).astype(bf16)
            if rel == 0:
                xrow_ref[...] = mm_nt(hot, x_low).astype(bf16)

    small, *long_lived, o_kept, o_passed, o_sent, x_rows = run(
        attend_body,
        [
            ((extra, width), bf16),
            ((1, length), jnp.int32),
            ((1, length), f32),
            ((width, length), bf16),
            ((here, length), bf16),
            ((here, length), bf16),
            ((here, length), bf16),
            *[((length, length), bf16)] * heads,
            ((here, length), bf16),
            ((rows, width), bf16),
            ((rows, width), bf16),
            ((2, rows, width), bf16),
            ((rows, width), bf16),
        ],
        (
            me,
            *tok_pieces,
            *small_pieces,
            wq_t,
            wk_t,
            wv_t,
            w_output,
            bias_table.T,
            buckets,
            segments,
            dest_row,
        ),
        "attend",
        us=0.01,
        scratch=[pltpu.VMEM((width, length), bf16), pltpu.VMEM((1, span), jnp.int32)],
        limit=24,
    )
    dest_far, r1, n1, q, k, v, p0, p1, p2, attn, small_far = store(
        [*long_lived, small], "attend_store"
    )
    o_beside = swap(o_sent, "tp", 1)
    o_half, n1 = lax.optimization_barrier((o_passed + o_beside[1], n1))
    o_across = swap(o_half, "tp", 2)

    def join_body(me_ref, cots_ref, out_ref):
        for rel in range(ways):
            out_ref[:, rel * quarter : (rel + 1) * quarter] = cots_ref[rel]

    (d_send,) = run(join_body, [((rows, width), bf16)], (after(me, o_half), cots), "join", us=0.3)
    d_arrived = over_experts(d_send)

    def routed(kept_ref, beside_ref, across_ref, xrow_ref, small_ref):
        o = kept_ref[...].astype(f32) + beside_ref[0].astype(f32) + across_ref[...].astype(f32)
        h = xrow_ref[...].astype(f32) + o
        r2 = lax.rsqrt(jnp.mean(h * h, axis=-1, keepdims=True) + EPSILON)
        gain = small_ref[experts + 1 : experts + 2].astype(f32)
        scaled = h * gain
        n2 = scaled * r2
        logits = r2 * mm_nt(scaled, small_ref[0:experts].astype(f32), HIGHEST)
        e = jnp.exp(logits - jnp.max(logits, axis=-1, keepdims=True))
        p = e / jnp.sum(e, axis=-1, keepdims=True)
        owner = iota((rows, experts), 0) - iota((rows, experts), 1) * per
        own = (owner >= 0) & (owner < per)
        g = jnp.sum(jnp.where(own, p, 0.0), axis=-1, keepdims=True)
        return h, r2, n2, p, g

    def route_body(kept_ref, beside_ref, across_ref, xrow_ref, small_ref, send_ref):
        h, r2, n2, p, g = routed(kept_ref, beside_ref, across_ref, xrow_ref, small_ref)
        send_ref[:, 0:width] = n2.astype(bf16)
        send_ref[:, width : width + LANES] = two_lanes(g, LANES)

    route_args = (o_kept, o_beside, o_across, x_rows, small)
    (send,) = run(
        route_body, [((rows, width + LANES), bf16)], route_args, "route", us=4
    )

    def state_body(
        me_ref, kept_ref, beside_ref, across_ref, xrow_ref, small_ref, c0, c1, c2, c3, *outs
    ):
        h_ref, aux_ref, dout_ref = outs
        mine = me_ref[0] & (ways - 1)
        pieces = [c[...] for c in (c0, c1, c2, c3)]
        dout_ref[...] = jnp.concatenate([absolute(pieces, mine, t) for t in range(ways)], axis=1)
        dout_ref.send()
        h, r2, n2, p, g = routed(kept_ref, beside_ref, across_ref, xrow_ref, small_ref)
        h_ref[...] = h
        h_ref.send()
        aux_ref[...] = jnp.zeros((rows, LANES), f32)
        aux_ref[:, 0:experts] = p
        aux_ref[:, LANES - 2 : LANES - 1] = r2
        aux_ref[:, LANES - 1 : LANES] = g

    later = after(cots, send)
    cot_pieces = [later[0]] + [swap(later[rel], "tp", rel) for rel in range(1, ways)]
    h_rows, aux, dout_rows = run(
        state_body,
        [
            ((rows, width), f32, True),
            ((rows, LANES), f32, True),
            ((rows, width), bf16, True),
        ],
        (after(me, send), *route_args, *cot_pieces),
        "state",
        us=0.01,
    )
    send, d_arrived = lax.optimization_barrier((send, d_arrived))
    d_pieces = gather_pieces(d_arrived)
    arrived, h_rows, aux, dout_rows, *d_pieces = lax.optimization_barrier(
        (over_experts(send), h_rows, aux, dout_rows, *d_pieces)
    )
    weights = fetch(after(me, arrived), [w_in, w_out], "expert_arguments")

    def dout_body(me_ref, d0, d1, d2, d3, *outs):
        mine = me_ref[0] & (ways - 1)
        came = (d0, d1, d2, d3)
        for rel in range(ways):
            pieces = []
            for src in range(ways):
                at = (rel ^ src) * quarter
                pieces.append(came[src][:, at : at + quarter])
            dout = jnp.concatenate([absolute(pieces, mine, t) for t in range(ways)], axis=1)
            outs[rel // 2][rel % 2 * rows : (rel % 2 + 1) * rows] = dout

    near_douts, far_douts = run(
        dout_body,
        [((2 * rows, width), bf16), ((2 * rows, width), bf16)],
        (after(me, arrived), *d_pieces),
        "douts",
        us=0.01,
    )
    across, beside = swap(arrived, "tp", 2), swap(arrived, "tp", 1)

    def expert_body(a0, a1, dout_ref, win_ref, wout_ref, *outs):
        u_ref, dy_ref, act_ref, dz_ref, kept_ref, sent_ref = outs
        for at, a in enumerate((a0, a1)):
            part = slice(at * rows, (at + 1) * rows)
            u_ref[part] = a[:, 0:width]
            g = a[:, width : width + 1].astype(f32) + a[:, width + 1 : width + 2].astype(f32)
            dy_ref[part] = (g * dout_ref[part].astype(f32)).astype(bf16)
        u = u_ref[...]
        dy = dy_ref[...]
        z = mm(u, win_ref[0])
        c = math.sqrt(2.0 / math.pi)
        z2 = z * z
        t = jnp.tanh(z * (c + (0.044715 * c) * z2))
        half = 0.5 + 0.5 * t
        wide_act = z * half
        act = wide_act.astype(bf16)
        act_ref[...] = act
        slope = half + wide_act * (1.0 - t) * (c + (3 * 0.044715 * c) * z2)
        dact = mm_nt(dy, wout_ref[0])
        dot = jnp.sum(dact * act.astype(f32), axis=-1, keepdims=True)
        dz = (dact * slope).astype(bf16)
        dz_ref[...] = dz
        du = mm_nt(dz, win_ref[0]).astype(bf16)
        tail = two_lanes(dot, LANES)
        for at, out in enumerate((kept_ref, sent_ref)):
            out[:, 0:width] = du[at * rows : (at + 1) * rows]
            out[:, width : width + LANES] = tail[at * rows : (at + 1) * rows]

    def expert(pieces, dout, name):
        return run(
            expert_body,
            [
                ((2 * rows, width), bf16),
                ((2 * rows, width), bf16),
                ((2 * rows, hidden_here), bf16),
                ((2 * rows, hidden_here), bf16),
                ((rows, width + LANES), bf16),
                ((rows, width + LANES), bf16),
            ],
            (*pieces, dout, *weights),
            name,
            us=0.01,
            limit=24,
        )

    *near, du_kept, du_sent = expert((arrived, beside), near_douts, "expert_near")
    du_beside = swap(du_sent, "tp", 1)
    across, du_kept, du_beside, *near = lax.optimization_barrier(
        (across, du_kept, du_beside, *near)
    )
    *wide, du_passed, du_sent = expert(
        (across, swap(across, "tp", 1)), far_douts, "expert_far"
    )
    du_half = du_passed + swap(du_sent, "tp", 1)
    du_across = swap(du_half, "tp", 2)
    stored = store([*near, *wide], "expert_store")
    du_across, *stored = lax.optimization_barrier((du_across, *stored))
    du_sum = du_kept + du_beside + du_across
    du_rows = over_experts(du_sum)

    def value_body(me_ref, near_ref, far_ref, wout_ref, kept_ref, passed_ref, sent_ref):
        act = jnp.concatenate([near_ref[...], far_ref[...]], axis=0)
        y = mm(act, wout_ref[0]).astype(bf16)
        for rel, out in enumerate((kept_ref, sent_ref.at[0], passed_ref, sent_ref.at[1])):
            out[...] = y[rel * rows : (rel + 1) * rows]

    y_parts = run(
        value_body,
        [((rows, width), bf16), ((rows, width), bf16), ((2, rows, width), bf16)],
        (after(me, du_half), near[2], wide[2], w_out),
        "value",
        us=0.8,
    )
    y_kept, y_passed, y_sent = y_parts
    y_beside = swap(y_sent, "tp", 1)
    y_across = swap(after(y_passed + y_beside[1], du_sum), "tp", 2)
    y_sum = y_kept + y_beside[0] + y_across

    y_rows = over_experts(y_sum)
    state = fetch(after(me, du_sum), [h_rows, aux, dout_rows, small_far, dest_far], "state_again")
    du_rows, _, *state = lax.optimization_barrier((du_rows, y_sum, *state))

    def back_body(
        du_ref, h_ref, aux_ref, dout_ref, small_ref, dest_ref, do_ref, parts_ref, drow_ref
    ):
        drow_ref[...] = dest_ref[...]
        du = du_ref[:, 0:width].astype(f32)
        gg = du_ref[:, width : width + 1].astype(f32)
        gg = gg + du_ref[:, width + 1 : width + 2].astype(f32)
        h = h_ref[...]
        p = aux_ref[:, 0:experts]
        r2 = aux_ref[:, LANES - 2 : LANES - 1]
        gain = small_ref[experts + 1 : experts + 2].astype(f32)
        router = small_ref[0:experts].astype(f32)
        owner = iota((rows, experts), 0) - iota((rows, experts), 1) * per
        own = ((owner >= 0) & (owner < per)).astype(f32)
        dlogits = gg * (own - p)
        dn2 = du + lax.dot_general(
            dlogits, router, (((1,), (0,)), ((), ())), precision=HIGHEST, preferred_element_type=f32
        )
        hr = h * r2
        n2 = hr * gain
        inner = jnp.sum(dn2 * gain * h, axis=-1, keepdims=True)
        dh = dout_ref[...].astype(f32) + r2 * gain * dn2 - hr * (r2 * r2 / width) * inner
        do_ref[...] = dh.astype(bf16)
        parts_ref[...] = jnp.zeros((few_rows, width), f32)
        parts_ref[0:experts] = lax.dot_general(
            dlogits, n2, (((0,), (0,)), ((), ())), precision=HIGHEST, preferred_element_type=f32
        )
        parts_ref[experts : experts + 1] = jnp.sum(dn2 * hr, axis=0, keepdims=True)

    do_rows, few_parts, dest_near = run(
        back_body,
        [((rows, width), bf16), ((few_rows, width), f32), ((1, length), jnp.int32)],
        (du_rows, *state),
        "residual_back",
        us=2.0,
    )
    do_across = swap(do_rows, "tp", 2)
    do_beside = swap(do_rows, "tp", 1)
    wanted = [w_output, attn, q, k, v, p0, p1, p2, n1, wq_t, wk_t, wv_t, small_far]
    fetched = fetch(after(me, do_rows), wanted, "attend_again")
    do_across, *fetched = lax.optimization_barrier((do_across, *fetched))
    do_pieces = (do_rows, do_beside, do_across, swap(do_across, "tp", 1))

    a_rows = 4 * here * 2 // 3
    chunk_a = a_rows // owners
    chunk_b = (4 * here - a_rows) // owners
    a_part, b_part = a_rows // first_a, (4 * here - a_rows) // first_b

    def attend_back_body(
        me_ref,
        d0,
        d1,
        d2,
        d3,
        drow_ref,
        wo_ref,
        attn_ref,
        q_ref,
        k_ref,
        v_ref,
        p0_ref,
        p1_ref,
        p2_ref,
        n1_ref,
        wq_ref,
        wk_ref,
        wv_ref,
        small_ref,
        few_ref,
        bucket_ref,
        own_ref,
        kept_ref,
        passed_ref,
        sent_ref,
        *others,
    ):
        a_outs, b_outs = others[:first_a], others[first_a : first_a + first_b]
        a_ref, b_ref, dq_ref, dk_ref, dv_ref, all_ref, bucket_held = others[first_a + first_b :]
        mine = me_ref[0] & (ways - 1)
        place = me_ref[0] >> shift
        stack = jnp.concatenate([d[...] for d in (d0, d1, d2, d3)], axis=0)
        drow = drow_ref[...]
        eye = iota((length, length), 0) == iota((length, length), 1)
        dcol = jnp.sum(jnp.where(eye, drow, 0), axis=1, keepdims=True)
        hot_t = (iota((length, ways * rows), 1) == dcol).astype(bf16)
        do = mm(hot_t, stack).astype(bf16)
        own = stack[:, 0:quarter]
        for t in range(1, ways):
            own = jnp.where(mine == t, stack[:, t * quarter : (t + 1) * quarter], own)
        hot = (iota((ways * rows, length), 0) == drow).astype(bf16)
        own_ref[...] = mm_tn(own, hot).astype(bf16)
        wo = wo_ref[...]
        da = mm_nt(wo, do).astype(bf16)
        hot = bucket_hot(bucket_ref, bucket_held, f32)
        flip = (iota((LANES, LANES), 0) + iota((LANES, LANES), 1) == LANES - 1).astype(bf16)
        tables = []
        for h in range(heads):
            part = slice(h * HD, (h + 1) * HD)
            p_low = (p0_ref, p1_ref, p2_ref)[h][...]
            p = p_low.astype(f32)
            dp = mm_tn(v_ref[part], da[part])
            dv_ref[part] = mm_nt(da[part], p_low).astype(bf16)
            inner = jnp.sum(p * dp, axis=0, keepdims=True)
            ds = (p * (dp - inner)).astype(bf16)
            dq_ref[part] = mm(k_ref[part], ds).astype(bf16)
            dk_ref[part] = mm_nt(q_ref[part], ds).astype(bf16)
            rows_of = [mm(flip, ds[bj * LANES : (bj + 1) * LANES]) for bj in range(tiles)]
            offsets = jnp.zeros((1, span), f32)
            for d in range(2 * tiles - 1):
                block = jnp.zeros((LANES, LANES), f32)
                for bj in range(tiles):
                    bi = bj + d - tiles + 1
                    if 0 <= bi < tiles:
                        block = block + rows_of[bj][:, bi * LANES : (bi + 1) * LANES]
                block = jnp.concatenate([block, jnp.zeros_like(block)], axis=1)
                block = pltpu.roll(block, 0, 1, stride=1, stride_axis=0)
                block = [jnp.sum(block, axis=0, keepdims=True)]
                if d:
                    block = [jnp.zeros((1, d * LANES), f32), *block]
                if d < 2 * tiles - 2:
                    block = [*block, jnp.zeros((1, span - (d + 2) * LANES), f32)]
                offsets = offsets + jnp.concatenate(block, axis=1)
            tables.append(mm_nt(offsets, hot, HIGHEST))
        n1 = n1_ref[...]
        gq = mm_nt(dq_ref[...], n1)
        gk = mm_nt(dk_ref[...], n1)
        gv = mm_nt(dv_ref[...], n1)
        back = gq * wq_ref[...].astype(f32) + gk * wk_ref[...].astype(f32)
        back = jnp.sum(back + gv * wv_ref[...].astype(f32), axis=0, keepdims=True)
        gain = small_ref[experts : experts + 1].astype(f32)
        gwo = mm(attn_ref[...], do)
        parts = [t.astype(bf16) for t in (gq, gk, gv, gwo)]
        for ref, chunk, start in ((a_ref, chunk_a, 0), (b_ref, chunk_b, a_rows)):
            for c in range(owners):
                low = start + c * chunk
                which, low = low // here, low % here
                ref[c] = parts[which][low : low + chunk]
        for order, ref, outs, chunk in (
            (order_a, a_ref, a_outs, chunk_a),
            (order_b, b_ref, b_outs, chunk_b),
        ):
            each = owners // len(outs)
            for at in range(owners):
                line = at % each
                outs[at // each][line * chunk : (line + 1) * chunk] = ref[rel_of(at, order) ^ place]
        few = few_ref[...]
        line = iota((few_rows, 1), 0)
        few = few + jnp.where(line == experts + 1, back / gain, 0.0)
        wide = jnp.concatenate(
            [jnp.concatenate([tables[h] * (mine == t).astype(f32) for t in range(ways)], axis=1)
             for h in range(heads)],
            axis=0,
        )
        pad = jnp.zeros((heads, width - ways * bins), f32)
        wide = jnp.concatenate([wide, pad], axis=1)
        for h in range(heads):
            few = few + jnp.where(line == experts + 2 + h, wide[h : h + 1], 0.0)
        few = few.astype(bf16)
        for out in b_outs:
            out[b_part : b_part + few_rows] = few
        dn1 = mm_tn(wq_ref[...], dq_ref[...])
        dn1 = dn1 + mm_tn(wk_ref[...], dk_ref[...])
        dn1 = dn1 + mm_tn(wv_ref[...], dv_ref[...])
        all_ref[...] = dn1.astype(bf16)
        dot = jnp.sum(dn1 * n1.astype(f32), axis=0, keepdims=True)
        high, low = split_low(dot)
        line = iota((16, length), 0)
        tail = jnp.where(line == 0, high, jnp.where(line == 1, low, 0.0)).astype(bf16)
        for rel, out in enumerate((kept_ref, sent_ref.at[0], passed_ref, sent_ref.at[1])):
            at = pl.multiple_of((mine ^ rel) * quarter, quarter)
            out[0:quarter] = all_ref[pl.ds(at, quarter), :]
            out[quarter : quarter + 16] = tail

    dh_own, *others = run(
        attend_back_body,
        [
            ((quarter, length), bf16),
            ((quarter + 16, length), bf16),
            ((quarter + 16, length), bf16),
            ((2, quarter + 16, length), bf16),
            *[((a_part, width), bf16)] * first_a,
            *[((b_part + few_rows, width), bf16)] * first_b,
        ],
        (
            me,
            *do_pieces,
            dest_near,
            *fetched,
            few_parts,
            buckets,
        ),
        "attend_back",
        us=0.01,
        scratch=[
            pltpu.VMEM((owners, chunk_a, width), bf16),
            pltpu.VMEM((owners, chunk_b, width), bf16),
            pltpu.VMEM((here, length), bf16),
            pltpu.VMEM((here, length), bf16),
            pltpu.VMEM((here, length), bf16),
            pltpu.VMEM((width, length), bf16),
            pltpu.VMEM((1, span), jnp.int32),
        ],
        limit=32,
    )

    y_rows, *others = lax.optimization_barrier((y_rows, *others))
    dn1_kept, dn1_passed, dn1_sent = others[:3]
    held = {}

    def tokens_body(
        me_ref, kept_ref, beside_ref, across_ref, dh_ref, tok_ref, r1_ref, small_ref, out_ref
    ):
        mine = me_ref[0] & (ways - 1)
        total = kept_ref[...].astype(f32) + beside_ref[0].astype(f32)
        total = total + across_ref[...].astype(f32)
        dn1 = total[0:quarter]
        dot = total[quarter : quarter + 1] + total[quarter + 1 : quarter + 2]
        one = r1_ref[...]
        small = small_ref[...]
        own = small[:, 0:quarter]
        for t in range(1, ways):
            own = jnp.where(mine == t, small[:, t * quarter : (t + 1) * quarter], own)
        gain = spread_row(own, experts, length)
        x = tok_ref[...].astype(f32)
        out_ref[...] = (
            dh_ref[...].astype(f32) + one * gain * dn1 - x * (one * one / width) * dot
        ).astype(bf16)

    def out_rows_body(me_ref, h_ref, aux_ref, y_ref, o0, o1, o2, o3, all_ref):
        mine = me_ref[0] & (ways - 1)
        out = (h_ref[...] + aux_ref[:, LANES - 1 : LANES] * y_ref[...].astype(f32)).astype(bf16)
        eye = (iota((rows, rows), 0) == iota((rows, rows), 1)).astype(bf16)
        all_ref[...] = mm_tn(out, eye).astype(bf16)
        for rel, piece in enumerate((o0, o1, o2, o3)):
            at = pl.multiple_of((mine ^ rel) * quarter, quarter)
            piece[...] = all_ref[pl.ds(at, quarter), :]

    def out_body(dest_ref, l0, l1, l2, l3, out_ref):
        dest = dest_ref[...]
        total = jnp.zeros((quarter, length), f32)
        for rel, piece in enumerate((l0, l1, l2, l3)):
            hot = (iota((rows, length), 0) + rel * rows == dest).astype(bf16)
            total = total + mm(piece[...], hot)
        out_ref[...] = total.astype(bf16)

    def weights_body(me_ref, u0, dy0, act0, dz0, u1, dy1, act1, dz1, gin_ref, gout_ref):
        gin = mm_tn(u0[...], dz0[...]) + mm_tn(u1[...], dz1[...])
        gin_ref[0] = gin.astype(bf16)
        gout = mm_tn(act0[...], dy0[...]) + mm_tn(act1[...], dy1[...])
        gout_ref[0] = gout.astype(bf16)

    def beside(came, block):
        phase = held.setdefault("phase", 0)
        held["phase"] += 1
        last = 2 * len(order_a) - 1
        extras = {}
        if phase == 0:
            extras["dn1_beside"] = swap(dn1_sent, "tp", 1)
            extras["grad_in"], extras["grad_out"] = run(
                weights_body,
                [((1, width, hidden_here), bf16), ((1, hidden_here, width), bf16)],
                (after(me, dn1_sent), *[Far(v) for v in stored]),
                "expert_weights",
                us=12,
            )
        if phase == 1:
            half = dn1_passed + held["dn1_beside"][1]
            extras["dn1_across"] = swap(half, "tp", 2)
            lo = run(
                out_rows_body,
                [((quarter, rows), bf16)] * ways,
                (me, Far(h_rows), Far(aux), y_rows),
                "layer_rows",
                us=12,
                scratch=[pltpu.VMEM((width, rows), bf16)],
            )
            for rel in range(ways):
                extras["lo%d" % rel] = lo[rel]
        if phase == last - 1:
            few = block.astype(f32)
            extras["few"] = few + swap(few, "tp", 1)
            for rel in range(1, ways):
                extras["lo%d" % rel] = swap(held["lo%d" % rel], "tp", rel)
        if phase == last:
            extras["few_other"] = swap(held["few"], "tp", 2)
            (extras["layer_out"],) = run(
                out_body,
                [((quarter, length), bf16)],
                (Far(dest_far), *[held["lo%d" % rel] for rel in range(ways)]),
                "layer_out",
                us=12,
            )
            (extras["grad_tokens"],) = run(
                tokens_body,
                [((quarter, length), bf16)],
                (
                    after(me, held["few"]),
                    dn1_kept,
                    held["dn1_beside"],
                    held["dn1_across"],
                    dh_own,
                    Far(tok_t),
                    Far(r1),
                    Far(small_far),
                ),
                "tokens_back",
                us=12,
            )
        names = list(extras)
        got = lax.optimization_barrier((*[extras[n] for n in names], *came))
        held.update(zip(names, got))
        return got[len(names) :]

    a_blocks, b_blocks = two_chains(
        others[3 : 3 + first_a], others[3 + first_a :], order_a, order_b, few_rows, beside
    )
    layer_out, grad_tokens = held["layer_out"], held["grad_tokens"]
    grad_in, grad_out = held["grad_in"], held["grad_out"]

    def unpack_body(me_ref, few_ref, other_ref, *others):
        a_ins, b_ins = others[: len(a_blocks)], others[len(a_blocks) :][:first_b]
        *results, a_ref, b_ref = others[len(a_blocks) + first_b :]
        gq_ref, gk_ref, gv_ref, go_ref, router_ref, g1_ref, g2_ref, table_ref = results
        mine = me_ref[0] & (ways - 1)
        place = me_ref[0] >> shift
        for order, ref, ins, chunk, start in (
            (order_a, a_ref, a_ins, chunk_a, 0),
            (order_b, b_ref, b_ins, chunk_b, a_rows),
        ):
            at = 0
            for piece in ins:
                for line in range(piece.shape[0] // chunk):
                    low = line * chunk
                    ref[rel_of(at, order) ^ place] = piece[low : low + chunk]
                    at += 1
            for c in range(owners):
                low = start + c * chunk
                which, low = low // here, low % here
                (gq_ref, gk_ref, gv_ref, go_ref)[which][low : low + chunk] = ref[c]
        total = few_ref[...] + other_ref[...]
        own = total[:, 0:quarter]
        for t in range(1, ways):
            own = jnp.where(mine == t, total[:, t * quarter : (t + 1) * quarter], own)
        router_ref[...] = own[0:experts].astype(bf16)
        g2_ref[...] = own[experts].astype(bf16)
        g1_ref[...] = own[experts + 1].astype(bf16)
        lines = total[experts + 2 : experts + 2 + heads]
        table = lines[:, 0:bins]
        for t in range(1, ways):
            table = jnp.where(mine == t, lines[:, t * bins : (t + 1) * bins], table)
        table_ref[...] = table.astype(bf16)

    gq, gk, gv, go, g_router, g_one, g_two, g_table = run(
        unpack_body,
        [
            ((here, width), bf16),
            ((here, width), bf16),
            ((here, width), bf16),
            ((here, width), bf16),
            ((experts, quarter), bf16),
            ((quarter,), bf16),
            ((quarter,), bf16),
            ((heads, bins), bf16),
        ],
        (me, held["few"], held["few_other"], *a_blocks, *b_blocks),
        "unpack",
        us=1.0,
        scratch=[
            pltpu.VMEM((owners, chunk_a, width), bf16),
            pltpu.VMEM((owners, chunk_b, width), bf16),
        ],
    )
    return (
        layer_out.T,
        grad_tokens.T,
        gq.T,
        gk.T,
        gv.T,
        go,
        g_table.T,
        g_router.T,
        grad_in,
        grad_out,
        g_one,
        g_two,
    )


def solution(mesh):
    placed = (
        P("exp", "tp"),
        P(None, "tp"),
        P(None, "tp"),
        P(None, "tp"),
        P("tp", None),
        P(None, "tp"),
        P("tp", None),
        P("exp", None, "tp"),
        P("exp", "tp", None),
        P("tp"),
        P("tp"),
        P("exp", None),
        P("exp", None),
        P(),
        P("exp", "tp"),
    )
    return jax.shard_map(
        local,
        mesh=mesh,
        in_specs=placed,
        out_specs=(
            P("exp", "tp"),
            P("exp", "tp"),
            P(None, "tp"),
            P(None, "tp"),
            P(None, "tp"),
            P("tp", None),
            P(None, "tp"),
            P("tp", None),
            P("exp", None, "tp"),
            P("exp", "tp", None),
            P("tp"),
            P("tp"),
        ),
        check_vma=False,
    )
```

```python
import math

import jax
import jax.numpy as jnp
from jax import lax
from jax.experimental import pallas as pl
from jax.experimental.pallas import tpu as pltpu
from jax.sharding import PartitionSpec as P

HD = 64
EPSILON = 1e-06
NEG_FILL = -1e30
HIGHEST = lax.Precision.HIGHEST
LANES = 128
f32 = jnp.float32
bf16 = jnp.bfloat16
VMEM = pl.BlockSpec(memory_space=pltpu.VMEM)
SMEM = pl.BlockSpec(memory_space=pltpu.SMEM)


class Far:
    def __init__(self, value):
        self.value = pltpu.with_memory_space_constraint(value, pltpu.HBM)


class Loaded:
    def __init__(self, copy, held):
        self.copy, self.held = copy, held

    def wait(self):
        if self.copy is not None:
            self.copy.wait()
            self.copy = None

    def __getitem__(self, index):
        self.wait()
        return self.held[index]


class Stored:
    def __init__(self, copy, held):
        self.copy, self.held, self.started = copy, held, False

    def __setitem__(self, index, value):
        self.held[index] = value

    def __getitem__(self, index):
        return self.held[index]

    def send(self):
        if not self.started:
            self.started = True
            self.copy.start()


def run(body, outs, args, name, us=1.0, scratch=(), limit=16):
    far_in = [isinstance(a, Far) for a in args]
    args = [a.value if isinstance(a, Far) else a for a in args]
    far_out = [len(o) == 3 for o in outs]
    bufs = [pltpu.VMEM(a.shape, a.dtype) for a, far in zip(args, far_in) if far]
    bufs += [pltpu.VMEM(o[0], o[1]) for o, far in zip(outs, far_out) if far]
    n_in, n_out, n_own = len(args), len(outs), len(scratch)
    hbm = pl.BlockSpec(memory_space=pltpu.HBM)
    specs = [
        SMEM if a.shape == (1,) and a.dtype == jnp.int32 else hbm if far else VMEM
        for a, far in zip(args, far_in)
    ]
    moved = sum(a.size * a.dtype.itemsize for a in args)
    moved += sum(math.prod(o[0]) * jnp.dtype(o[1]).itemsize for o in outs)

    def wrapped(*refs):
        ins, results = refs[:n_in], refs[n_in : n_in + n_out]
        own = refs[n_in + n_out : n_in + n_out + n_own]
        held = refs[n_in + n_out + n_own :]
        given, at = [], 0
        for ref, far in zip((*ins, *results), (*far_in, *far_out)):
            if not far:
                given.append(ref)
                continue
            if len(given) < n_in:
                copy = pltpu.make_async_copy(ref, held[at], held[-1].at[at])
                copy.start()
                given.append(Loaded(copy, held[at]))
            else:
                copy = pltpu.make_async_copy(held[at], ref, held[-1].at[at])
                given.append(Stored(copy, held[at]))
            at += 1
        body(*given, *own)
        for g in given:
            if isinstance(g, Stored):
                g.send()
        for g in given:
            if isinstance(g, Stored):
                g.copy.wait()
            elif isinstance(g, Loaded):
                g.wait()

    sems = [pltpu.SemaphoreType.DMA((len(bufs),))] if bufs else []
    return pl.pallas_call(
        wrapped,
        out_shape=[
            pltpu.HBM(o[0], o[1]) if len(o) == 3 else jax.ShapeDtypeStruct(o[0], o[1])
            for o in outs
        ],
        in_specs=specs,
        out_specs=[hbm if far else VMEM for far in far_out],
        scratch_shapes=[*scratch, *bufs, *sems],
        compiler_params=pltpu.CompilerParams(vmem_limit_bytes=limit * 2**20),
        cost_estimate=pl.CostEstimate(
            flops=int(us * 1.1e9), bytes_accessed=moved, transcendentals=0
        ),
        name=name,
    )(*args)


def fetch(token, values, name):
    values = [pltpu.with_memory_space_constraint(v, pltpu.HBM) for v in values]
    count = len(values)

    def body(token_ref, *refs):
        ins, outs, sems = refs[:count], refs[count : 2 * count], refs[-1]
        copies = [
            pltpu.make_async_copy(i, o, sems.at[n]) for n, (i, o) in enumerate(zip(ins, outs))
        ]
        for c in copies:
            c.start()
        for c in copies:
            c.wait()

    return pl.pallas_call(
        body,
        out_shape=[jax.ShapeDtypeStruct(v.shape, v.dtype) for v in values],
        in_specs=[SMEM] + [pl.BlockSpec(memory_space=pltpu.HBM)] * count,
        out_specs=[VMEM] * count,
        scratch_shapes=[pltpu.SemaphoreType.DMA((count,))],
        compiler_params=pltpu.CompilerParams(vmem_limit_bytes=16 * 2**20),
        name=name,
    )(token, *values)


def store(values, name):
    count = len(values)

    def body(*refs):
        ins, outs, sems = refs[:count], refs[count : 2 * count], refs[-1]
        copies = [
            pltpu.make_async_copy(i, o, sems.at[n]) for n, (i, o) in enumerate(zip(ins, outs))
        ]
        for c in copies:
            c.start()
        for c in copies:
            c.wait()

    return pl.pallas_call(
        body,
        out_shape=[pltpu.HBM(v.shape, v.dtype) for v in values],
        in_specs=[VMEM] * count,
        out_specs=[pl.BlockSpec(memory_space=pltpu.HBM)] * count,
        scratch_shapes=[pltpu.SemaphoreType.DMA((count,))],
        compiler_params=pltpu.CompilerParams(vmem_limit_bytes=16 * 2**20),
        name=name,
    )(*values)


def swap(value, axis, mask):
    size = lax.axis_size(axis)
    return lax.ppermute(value, axis, [(i, i ^ mask) for i in range(size)])


def after(value, *others):
    return lax.optimization_barrier((value, *others))[0]


def mm(left, right):
    return jnp.dot(left, right, preferred_element_type=f32)


def mm_tn(left, right):
    return lax.dot_general(left, right, (((0,), (0,)), ((), ())), preferred_element_type=f32)


def mm_nt(left, right, precision=None):
    return lax.dot_general(
        left, right, (((1,), (1,)), ((), ())), precision=precision, preferred_element_type=f32
    )


def iota(shape, dim):
    return lax.broadcasted_iota(jnp.int32, shape, dim)


def absolute(pieces, me, place):
    picked = pieces[0]
    for rel in range(1, len(pieces)):
        picked = jnp.where((me ^ rel) == place, pieces[rel], picked)
    return picked


def split_low(value):
    high = value.astype(bf16)
    return high.astype(f32), value - high.astype(f32)


def two_lanes(value, count):
    high, low = split_low(value)
    lane = iota((value.shape[0], count), 1)
    return jnp.where(lane == 0, high, jnp.where(lane == 1, low, 0.0)).astype(bf16)


def gather_pieces(value):
    across = swap(value, "tp", 2)
    beside = swap(value, "tp", 1)
    return value, beside, across, swap(across, "tp", 1)


def scatter_sum(kept, passed, sent):
    came = swap(sent, "tp", 1)
    half = passed + came[1]
    return kept, came, swap(half, "tp", 2), half


def digits_of(count):
    digits, shift = [(0, 2)], 1
    while (1 << shift) < count:
        radix = min(4, count >> shift)
        digits.append((shift, radix))
        shift += radix.bit_length() - 1
    return digits


def rel_of(place, order):
    rel = 0
    for shift, radix in reversed(order):
        rel |= (place % radix) << shift
        place //= radix
    return rel


def trade(blocks, digit):
    shift, radix = digit
    return [swap(blocks[k], "exp", k << shift) for k in range(1, radix)]


def sum_blocks(kept, came):
    total = kept.astype(f32)
    for c in came:
        total = total + c.astype(f32)
    return total.astype(bf16)


def two_chains(a_blocks, b_blocks, order_a, order_b, tail, beside):
    for at, (digit_a, digit_b) in enumerate(zip(order_a, order_b)):
        b_came = trade(b_blocks, digit_b)
        a_came = trade(a_blocks, digit_a)
        got = beside((*b_came, *a_came), b_blocks[0])
        got = (*got[len(b_came) :], *got[: len(b_came)])
        a = sum_blocks(a_blocks[0], got[: len(a_came)])
        b = sum_blocks(b_blocks[0], got[len(a_came) :])
        few = b[b.shape[0] - tail :]
        if at + 1 < len(order_a):
            radix = order_a[at + 1][1]
            part = a.shape[0] // radix
            a_blocks = [a[k * part : (k + 1) * part] for k in range(radix)]
            radix = order_b[at + 1][1]
            part = (b.shape[0] - tail) // radix
            b_blocks = [
                jnp.concatenate([b[k * part : (k + 1) * part], few], axis=0) for k in range(radix)
            ]
    b = b[: b.shape[0] - tail]
    last = len(order_a) - 1
    early = []
    for at, (digit_a, digit_b) in enumerate(zip(order_a[::-1], order_b[::-1])):
        b_came = trade([b] * digit_b[1], digit_b)
        a_came = trade([rest if at == last else a] * digit_a[1], digit_a)
        ahead = trade([a] * order_a[0][1], order_a[0]) if at == last - 1 else []
        got = beside((*ahead, *b_came, *a_came), few)
        early += got[: len(ahead)]
        b_blocks = [b, *got[len(ahead) : len(ahead) + len(b_came)]]
        a_blocks = got[len(ahead) + len(b_came) :]
        if at == last - 1:
            own, rest = a, jnp.concatenate(a_blocks, axis=0)
        elif at < last:
            a = jnp.concatenate([a, *a_blocks], axis=0)
        if at < last:
            b = jnp.concatenate(b_blocks, axis=0)
    return [own, rest, *early, *a_blocks], b_blocks


def local(
    tokens,
    w_query,
    w_key,
    w_value,
    w_output,
    bias_table,
    w_router,
    w_in,
    w_out,
    gain_attn,
    gain_ffn,
    routes,
    segments,
    buckets,
    cotangent,
):
    length, quarter = tokens.shape
    ways = lax.axis_size("tp")
    owners = lax.axis_size("exp")
    width = quarter * ways
    here = w_query.shape[1]
    heads = here // HD
    experts = w_router.shape[1]
    bins = bias_table.shape[0]
    hidden_here = w_in.shape[2]
    capacity = max(2, length // owners * 9 // 8)
    per = -(-capacity // ways)
    while experts * per % LANES:
        per += 1
    rows = experts * per
    span = 2 * length
    tiles = length // LANES
    extra = -(-(experts + 2) // 16) * 16
    few_rows = -(-(experts + 2 + heads) // 16) * 16
    me = lax.axis_index(("exp", "tp")).astype(jnp.int32)[None]
    order_a = digits_of(owners)
    order_b = order_a[1:] + order_a[:1]
    first_a, first_b = order_a[0][1], order_b[0][1]
    shift = ways.bit_length() - 1

    tok_t = tokens.T
    wq_t, wk_t, wv_t = w_query.T, w_key.T, w_value.T

    def slot_body(
        me_ref, route_ref, cot_ref, *outs
    ):
        drow_ref, cots_ref = outs
        mine = me_ref[0] & (ways - 1)
        row = route_ref[...]
        above = iota((length, length), 0)
        along = iota((length, length), 1)
        col = jnp.sum(jnp.where(above == along, row, 0), axis=1, keepdims=True)
        same = col == row

        def dest(slot, expert):
            chunk = jnp.zeros_like(slot)
            for t in range(1, ways):
                chunk = chunk + (slot >= t * per).astype(jnp.int32)
            return (chunk ^ mine) * rows + expert * per + slot - chunk * per

        slot_row = jnp.sum(jnp.where(same & (above < along), 1, 0), axis=0, keepdims=True)
        dest_row = dest(slot_row, row)
        drow_ref[...] = dest_row
        cot = cot_ref[...]
        for rel in range(ways):
            hot = (iota((rows, length), 0) + rel * rows == dest_row).astype(bf16)
            piece = mm_nt(hot, cot).astype(bf16)
            cots_ref[rel] = piece

    dest_row, cots = run(
        slot_body,
        [
            ((1, length), jnp.int32),
            ((ways, rows, quarter), bf16),
        ],
        (
            me,
            Far(routes.T),
            Far(cotangent.T),
        ),
        "slots",
        us=0.7,
    )
    def small_body(router_ref, g1_ref, g2_ref, small_ref):
        line = iota((extra - experts, quarter), 0)
        gains = jnp.where(
            line == 0,
            g1_ref[...].astype(f32)[None],
            jnp.where(line == 1, g2_ref[...].astype(f32)[None], 0.0),
        )
        small_ref[...] = jnp.concatenate([router_ref[...].astype(f32), gains], 0).astype(bf16)

    (small_own,) = run(
        small_body,
        [((extra, quarter), bf16)],
        (Far(w_router.T), Far(gain_attn), Far(gain_ffn)),
        "small",
        us=0.2,
    )
    small_pieces = [small_own] + [swap(small_own, "tp", rel) for rel in range(1, ways)]
    tok_across = swap(tok_t, "tp", 2)
    tok_across, dest_row, *small_pieces = lax.optimization_barrier(
        (tok_across, dest_row, *small_pieces)
    )
    tok_pieces = (tok_t, swap(tok_t, "tp", 1), tok_across, swap(tok_across, "tp", 1))

    def over_experts(value):
        blocks = value.reshape(experts, per, value.shape[1])
        moved = lax.all_to_all(blocks, "exp", split_axis=0, concat_axis=0, tiled=True)
        return moved.reshape(rows, value.shape[1])

    def bucket_hot(ref, held, dtype):
        held[...] = jnp.full((1, span), -1, jnp.int32)
        held[:, 0 : buckets.shape[0]] = ref[...][None]
        return (iota((bins, span), 0) == held[...]).astype(dtype)

    def spread_row(few, line, count):
        pick = (iota((few.shape[0], count), 0) == line).astype(bf16)
        return mm_tn(few, pick)

    def attend_body(
        me_ref,
        t0,
        t1,
        t2,
        t3,
        c0,
        c1,
        c2,
        c3,
        wq_ref,
        wk_ref,
        wv_ref,
        wo_ref,
        table_ref,
        bucket_ref,
        seg_ref,
        dest_ref,
        small_ref,
        dest_far,
        r1_ref,
        n1_ref,
        q_ref,
        k_ref,
        v_ref,
        p0_ref,
        p1_ref,
        p2_ref,
        attn_ref,
        kept_ref,
        passed_ref,
        sent_ref,
        xrow_ref,
        x_ref,
        bucket_held,
    ):
        p_refs = (p0_ref, p1_ref, p2_ref)
        mine = me_ref[0] & (ways - 1)
        for rel, piece in enumerate((t0, t1, t2, t3)):
            at = pl.multiple_of((mine ^ rel) * quarter, quarter)
            x_ref[pl.ds(at, quarter), :] = piece[...]
        pieces = [c[...] for c in (c0, c1, c2, c3)]
        small = jnp.concatenate([absolute(pieces, mine, t) for t in range(ways)], axis=1)
        small_ref[...] = small
        dest_far[...] = dest_ref[...]
        x_low = x_ref[...]
        x = x_low.astype(f32)
        r1 = lax.rsqrt(jnp.mean(x * x, axis=0, keepdims=True) + EPSILON)
        r1_ref[...] = r1
        n1 = (x * r1 * spread_row(small, experts, length)).astype(bf16)
        n1_ref[...] = n1
        q = mm(wq_ref[...], n1).astype(bf16)
        k = mm(wk_ref[...], n1).astype(bf16)
        v = mm(wv_ref[...], n1).astype(bf16)
        q_ref[...] = q
        k_ref[...] = k
        v_ref[...] = v
        hot = bucket_hot(bucket_ref, bucket_held, bf16)
        offsets = mm(table_ref[...], hot)
        above = iota((length, length), 0)
        along = iota((length, length), 1)
        seg_row = seg_ref[...]
        seg_col = jnp.sum(jnp.where(above == along, seg_row, 0), axis=1, keepdims=True)
        same = seg_col == seg_row
        for h in range(heads):
            part = slice(h * HD, (h + 1) * HD)
            diagonals = []
            for d in range(2 * tiles - 1):
                window = offsets[h : h + 1, d * LANES : (d + 2) * LANES]
                spread = jnp.broadcast_to(window, (LANES, 2 * LANES))
                turned = pltpu.roll(spread, LANES + 1, 1, stride=1, stride_axis=0)
                diagonals.append(turned[:, :LANES])
            bias = jnp.concatenate(
                [
                    jnp.concatenate([diagonals[bi - bj + tiles - 1] for bi in range(tiles)], axis=1)
                    for bj in range(tiles)
                ],
                axis=0,
            )
            s = jnp.where(same, mm_tn(k[part], q[part]) + bias, NEG_FILL)
            e = jnp.exp(s - jnp.max(s, axis=0, keepdims=True))
            p = (e * (1.0 / jnp.sum(e, axis=0, keepdims=True))).astype(bf16)
            p_refs[h][...] = p
            attn_ref[part] = mm(v[part], p).astype(bf16)
        attn = attn_ref[...]
        dest = dest_ref[...]
        wo = wo_ref[...]
        for rel, out in enumerate((kept_ref, sent_ref.at[0], passed_ref, sent_ref.at[1])):
            hot = (iota((rows, length), 0) + rel * rows == dest).astype(bf16)
            out[...] = mm(mm_nt(hot, attn).astype(bf16), wo).astype(bf16)
            if rel == 0:
                xrow_ref[...] = mm_nt(hot, x_low).astype(bf16)

    small, *long_lived, o_kept, o_passed, o_sent, x_rows = run(
        attend_body,
        [
            ((extra, width), bf16),
            ((1, length), jnp.int32),
            ((1, length), f32),
            ((width, length), bf16),
            ((here, length), bf16),
            ((here, length), bf16),
            ((here, length), bf16),
            *[((length, length), bf16)] * heads,
            ((here, length), bf16),
            ((rows, width), bf16),
            ((rows, width), bf16),
            ((2, rows, width), bf16),
            ((rows, width), bf16),
        ],
        (
            me,
            *tok_pieces,
            *small_pieces,
            wq_t,
            wk_t,
            wv_t,
            w_output,
            bias_table.T,
            buckets,
            segments,
            dest_row,
        ),
        "attend",
        us=0.01,
        scratch=[pltpu.VMEM((width, length), bf16), pltpu.VMEM((1, span), jnp.int32)],
        limit=24,
    )
    dest_far, r1, n1, q, k, v, p0, p1, p2, attn, small_far = store(
        [*long_lived, small], "attend_store"
    )
    o_beside = swap(o_sent, "tp", 1)
    o_half, n1 = lax.optimization_barrier((o_passed + o_beside[1], n1))
    o_across = swap(o_half, "tp", 2)

    def join_body(me_ref, cots_ref, out_ref):
        for rel in range(ways):
            out_ref[:, rel * quarter : (rel + 1) * quarter] = cots_ref[rel]

    (d_send,) = run(join_body, [((rows, width), bf16)], (after(me, o_sent), cots), "join", us=0.3)
    d_arrived = over_experts(d_send)

    def routed(kept_ref, beside_ref, across_ref, xrow_ref, small_ref):
        o = kept_ref[...].astype(f32) + beside_ref[0].astype(f32) + across_ref[...].astype(f32)
        h = xrow_ref[...].astype(f32) + o
        r2 = lax.rsqrt(jnp.mean(h * h, axis=-1, keepdims=True) + EPSILON)
        gain = small_ref[experts + 1 : experts + 2].astype(f32)
        scaled = h * gain
        n2 = scaled * r2
        logits = r2 * mm_nt(scaled, small_ref[0:experts].astype(f32), HIGHEST)
        e = jnp.exp(logits - jnp.max(logits, axis=-1, keepdims=True))
        p = e / jnp.sum(e, axis=-1, keepdims=True)
        owner = iota((rows, experts), 0) - iota((rows, experts), 1) * per
        own = (owner >= 0) & (owner < per)
        g = jnp.sum(jnp.where(own, p, 0.0), axis=-1, keepdims=True)
        return h, r2, n2, p, g

    def route_body(kept_ref, beside_ref, across_ref, xrow_ref, small_ref, send_ref):
        h, r2, n2, p, g = routed(kept_ref, beside_ref, across_ref, xrow_ref, small_ref)
        send_ref[:, 0:width] = n2.astype(bf16)
        send_ref[:, width : width + LANES] = two_lanes(g, LANES)

    route_args = (o_kept, o_beside, o_across, x_rows, small)
    (send,) = run(
        route_body, [((rows, width + LANES), bf16)], route_args, "route", us=4
    )

    def state_body(
        me_ref, kept_ref, beside_ref, across_ref, xrow_ref, small_ref, c0, c1, c2, c3, *outs
    ):
        h_ref, aux_ref, dout_ref = outs
        mine = me_ref[0] & (ways - 1)
        pieces = [c[...] for c in (c0, c1, c2, c3)]
        dout_ref[...] = jnp.concatenate([absolute(pieces, mine, t) for t in range(ways)], axis=1)
        dout_ref.send()
        h, r2, n2, p, g = routed(kept_ref, beside_ref, across_ref, xrow_ref, small_ref)
        h_ref[...] = h
        h_ref.send()
        aux_ref[...] = jnp.zeros((rows, LANES), f32)
        aux_ref[:, 0:experts] = p
        aux_ref[:, LANES - 2 : LANES - 1] = r2
        aux_ref[:, LANES - 1 : LANES] = g

    later = after(cots, send)
    cot_pieces = [later[0]] + [swap(later[rel], "tp", rel) for rel in range(1, ways)]
    h_rows, aux, dout_rows = run(
        state_body,
        [
            ((rows, width), f32, True),
            ((rows, LANES), f32, True),
            ((rows, width), bf16, True),
        ],
        (after(me, send), *route_args, *cot_pieces),
        "state",
        us=1,
    )
    send, d_arrived = lax.optimization_barrier((send, d_arrived))
    d_pieces = gather_pieces(d_arrived)
    arrived, h_rows, aux, dout_rows, *d_pieces = lax.optimization_barrier(
        (over_experts(send), h_rows, aux, dout_rows, *d_pieces)
    )
    weights = fetch(after(me, arrived), [w_in, w_out], "expert_arguments")

    def dout_body(me_ref, d0, d1, d2, d3, *outs):
        mine = me_ref[0] & (ways - 1)
        came = (d0, d1, d2, d3)
        for rel in range(ways):
            pieces = []
            for src in range(ways):
                at = (rel ^ src) * quarter
                pieces.append(came[src][:, at : at + quarter])
            dout = jnp.concatenate([absolute(pieces, mine, t) for t in range(ways)], axis=1)
            outs[rel // 2][rel % 2 * rows : (rel % 2 + 1) * rows] = dout

    near_douts, far_douts = run(
        dout_body,
        [((2 * rows, width), bf16), ((2 * rows, width), bf16)],
        (after(me, arrived), *d_pieces),
        "douts",
        us=0.01,
    )
    across, beside = swap(arrived, "tp", 2), swap(arrived, "tp", 1)

    def expert_body(a0, a1, dout_ref, win_ref, wout_ref, *outs):
        u_ref, dy_ref, act_ref, dz_ref, kept_ref, sent_ref = outs
        for at, a in enumerate((a0, a1)):
            part = slice(at * rows, (at + 1) * rows)
            u_ref[part] = a[:, 0:width]
            g = a[:, width : width + 1].astype(f32) + a[:, width + 1 : width + 2].astype(f32)
            dy_ref[part] = (g * dout_ref[part].astype(f32)).astype(bf16)
        u = u_ref[...]
        dy = dy_ref[...]
        z = mm(u, win_ref[0])
        c = math.sqrt(2.0 / math.pi)
        z2 = z * z
        t = jnp.tanh(z * (c + (0.044715 * c) * z2))
        half = 0.5 + 0.5 * t
        wide_act = z * half
        act = wide_act.astype(bf16)
        act_ref[...] = act
        slope = half + wide_act * (1.0 - t) * (c + (3 * 0.044715 * c) * z2)
        dact = mm_nt(dy, wout_ref[0])
        dot = jnp.sum(dact * act.astype(f32), axis=-1, keepdims=True)
        dz = (dact * slope).astype(bf16)
        dz_ref[...] = dz
        du = mm_nt(dz, win_ref[0]).astype(bf16)
        tail = two_lanes(dot, LANES)
        for at, out in enumerate((kept_ref, sent_ref)):
            out[:, 0:width] = du[at * rows : (at + 1) * rows]
            out[:, width : width + LANES] = tail[at * rows : (at + 1) * rows]

    def expert(pieces, dout, name):
        return run(
            expert_body,
            [
                ((2 * rows, width), bf16),
                ((2 * rows, width), bf16),
                ((2 * rows, hidden_here), bf16),
                ((2 * rows, hidden_here), bf16),
                ((rows, width + LANES), bf16),
                ((rows, width + LANES), bf16),
            ],
            (*pieces, dout, *weights),
            name,
            us=0.01,
            limit=24,
        )

    *near, du_kept, du_sent = expert((arrived, beside), near_douts, "expert_near")
    du_beside = swap(du_sent, "tp", 1)
    across, du_kept, du_beside, *near = lax.optimization_barrier(
        (across, du_kept, du_beside, *near)
    )
    *wide, du_passed, du_sent = expert(
        (across, swap(across, "tp", 1)), far_douts, "expert_far"
    )
    du_half = du_passed + swap(du_sent, "tp", 1)
    du_across = swap(du_half, "tp", 2)
    stored = store([*near, *wide], "expert_store")
    du_across, *stored = lax.optimization_barrier((du_across, *stored))
    du_sum = du_kept + du_beside + du_across
    du_rows = over_experts(du_sum)

    def value_body(me_ref, near_ref, far_ref, wout_ref, kept_ref, passed_ref, sent_ref):
        act = jnp.concatenate([near_ref[...], far_ref[...]], axis=0)
        y = mm(act, wout_ref[0]).astype(bf16)
        for rel, out in enumerate((kept_ref, sent_ref.at[0], passed_ref, sent_ref.at[1])):
            out[...] = y[rel * rows : (rel + 1) * rows]

    y_parts = run(
        value_body,
        [((rows, width), bf16), ((rows, width), bf16), ((2, rows, width), bf16)],
        (after(me, du_half), near[2], wide[2], w_out),
        "value",
        us=0.01,
    )
    y_kept, y_passed, y_sent = y_parts
    y_beside = swap(y_sent, "tp", 1)
    y_across = swap(after(y_passed + y_beside[1], du_sum), "tp", 2)
    y_sum = y_kept + y_beside[0] + y_across

    y_rows = over_experts(y_sum)
    state = fetch(after(me, du_sum), [h_rows, aux, dout_rows, small_far, dest_far], "state_again")
    du_rows, _, *state = lax.optimization_barrier((du_rows, y_sum, *state))

    def back_body(
        du_ref, h_ref, aux_ref, dout_ref, small_ref, dest_ref, do_ref, parts_ref, drow_ref
    ):
        drow_ref[...] = dest_ref[...]
        du = du_ref[:, 0:width].astype(f32)
        gg = du_ref[:, width : width + 1].astype(f32)
        gg = gg + du_ref[:, width + 1 : width + 2].astype(f32)
        h = h_ref[...]
        p = aux_ref[:, 0:experts]
        r2 = aux_ref[:, LANES - 2 : LANES - 1]
        gain = small_ref[experts + 1 : experts + 2].astype(f32)
        router = small_ref[0:experts].astype(f32)
        owner = iota((rows, experts), 0) - iota((rows, experts), 1) * per
        own = ((owner >= 0) & (owner < per)).astype(f32)
        dlogits = gg * (own - p)
        dn2 = du + lax.dot_general(
            dlogits, router, (((1,), (0,)), ((), ())), precision=HIGHEST, preferred_element_type=f32
        )
        hr = h * r2
        n2 = hr * gain
        inner = jnp.sum(dn2 * gain * h, axis=-1, keepdims=True)
        dh = dout_ref[...].astype(f32) + r2 * gain * dn2 - hr * (r2 * r2 / width) * inner
        do_ref[...] = dh.astype(bf16)
        parts_ref[...] = jnp.zeros((few_rows, width), f32)
        parts_ref[0:experts] = lax.dot_general(
            dlogits, n2, (((0,), (0,)), ((), ())), precision=HIGHEST, preferred_element_type=f32
        )
        parts_ref[experts : experts + 1] = jnp.sum(dn2 * hr, axis=0, keepdims=True)

    do_rows, few_parts, dest_near = run(
        back_body,
        [((rows, width), bf16), ((few_rows, width), f32), ((1, length), jnp.int32)],
        (du_rows, *state),
        "residual_back",
        us=2.0,
    )
    do_across = swap(do_rows, "tp", 2)
    do_beside = swap(do_rows, "tp", 1)
    wanted = [w_output, attn, q, k, v, p0, p1, p2, n1, wq_t, wk_t, wv_t, small_far]
    fetched = fetch(after(me, do_rows), wanted, "attend_again")
    do_across, *fetched = lax.optimization_barrier((do_across, *fetched))
    do_pieces = (do_rows, do_beside, do_across, swap(do_across, "tp", 1))

    a_rows = 4 * here * 2 // 3
    chunk_a = a_rows // owners
    chunk_b = (4 * here - a_rows) // owners
    a_part, b_part = a_rows // first_a, (4 * here - a_rows) // first_b

    def attend_back_body(
        me_ref,
        d0,
        d1,
        d2,
        d3,
        drow_ref,
        wo_ref,
        attn_ref,
        q_ref,
        k_ref,
        v_ref,
        p0_ref,
        p1_ref,
        p2_ref,
        n1_ref,
        wq_ref,
        wk_ref,
        wv_ref,
        small_ref,
        few_ref,
        bucket_ref,
        own_ref,
        kept_ref,
        passed_ref,
        sent_ref,
        *others,
    ):
        a_outs, b_outs = others[:first_a], others[first_a : first_a + first_b]
        a_ref, b_ref, dq_ref, dk_ref, dv_ref, all_ref, bucket_held = others[first_a + first_b :]
        mine = me_ref[0] & (ways - 1)
        place = me_ref[0] >> shift
        stack = jnp.concatenate([d[...] for d in (d0, d1, d2, d3)], axis=0)
        drow = drow_ref[...]
        eye = iota((length, length), 0) == iota((length, length), 1)
        dcol = jnp.sum(jnp.where(eye, drow, 0), axis=1, keepdims=True)
        hot_t = (iota((length, ways * rows), 1) == dcol).astype(bf16)
        do = mm(hot_t, stack).astype(bf16)
        own = stack[:, 0:quarter]
        for t in range(1, ways):
            own = jnp.where(mine == t, stack[:, t * quarter : (t + 1) * quarter], own)
        hot = (iota((ways * rows, length), 0) == drow).astype(bf16)
        own_ref[...] = mm_tn(own, hot).astype(bf16)
        wo = wo_ref[...]
        da = mm_nt(wo, do).astype(bf16)
        hot = bucket_hot(bucket_ref, bucket_held, f32)
        flip = (iota((LANES, LANES), 0) + iota((LANES, LANES), 1) == LANES - 1).astype(bf16)
        tables = []
        for h in range(heads):
            part = slice(h * HD, (h + 1) * HD)
            p_low = (p0_ref, p1_ref, p2_ref)[h][...]
            p = p_low.astype(f32)
            dp = mm_tn(v_ref[part], da[part])
            dv_ref[part] = mm_nt(da[part], p_low).astype(bf16)
            inner = jnp.sum(p * dp, axis=0, keepdims=True)
            ds = (p * (dp - inner)).astype(bf16)
            dq_ref[part] = mm(k_ref[part], ds).astype(bf16)
            dk_ref[part] = mm_nt(q_ref[part], ds).astype(bf16)
            rows_of = [mm(flip, ds[bj * LANES : (bj + 1) * LANES]) for bj in range(tiles)]
            offsets = jnp.zeros((1, span), f32)
            for d in range(2 * tiles - 1):
                block = jnp.zeros((LANES, LANES), f32)
                for bj in range(tiles):
                    bi = bj + d - tiles + 1
                    if 0 <= bi < tiles:
                        block = block + rows_of[bj][:, bi * LANES : (bi + 1) * LANES]
                block = jnp.concatenate([block, jnp.zeros_like(block)], axis=1)
                block = pltpu.roll(block, 0, 1, stride=1, stride_axis=0)
                block = [jnp.sum(block, axis=0, keepdims=True)]
                if d:
                    block = [jnp.zeros((1, d * LANES), f32), *block]
                if d < 2 * tiles - 2:
                    block = [*block, jnp.zeros((1, span - (d + 2) * LANES), f32)]
                offsets = offsets + jnp.concatenate(block, axis=1)
            tables.append(mm_nt(offsets, hot, HIGHEST))
        n1 = n1_ref[...]
        gq = mm_nt(dq_ref[...], n1)
        gk = mm_nt(dk_ref[...], n1)
        gv = mm_nt(dv_ref[...], n1)
        back = gq * wq_ref[...].astype(f32) + gk * wk_ref[...].astype(f32)
        back = jnp.sum(back + gv * wv_ref[...].astype(f32), axis=0, keepdims=True)
        gain = small_ref[experts : experts + 1].astype(f32)
        gwo = mm(attn_ref[...], do)
        parts = [t.astype(bf16) for t in (gq, gk, gv, gwo)]
        for ref, chunk, start in ((a_ref, chunk_a, 0), (b_ref, chunk_b, a_rows)):
            for c in range(owners):
                low = start + c * chunk
                which, low = low // here, low % here
                ref[c] = parts[which][low : low + chunk]
        for order, ref, outs, chunk in (
            (order_a, a_ref, a_outs, chunk_a),
            (order_b, b_ref, b_outs, chunk_b),
        ):
            each = owners // len(outs)
            for at in range(owners):
                line = at % each
                outs[at // each][line * chunk : (line + 1) * chunk] = ref[rel_of(at, order) ^ place]
        few = few_ref[...]
        line = iota((few_rows, 1), 0)
        few = few + jnp.where(line == experts + 1, back / gain, 0.0)
        wide = jnp.concatenate(
            [jnp.concatenate([tables[h] * (mine == t).astype(f32) for t in range(ways)], axis=1)
             for h in range(heads)],
            axis=0,
        )
        pad = jnp.zeros((heads, width - ways * bins), f32)
        wide = jnp.concatenate([wide, pad], axis=1)
        for h in range(heads):
            few = few + jnp.where(line == experts + 2 + h, wide[h : h + 1], 0.0)
        few = few.astype(bf16)
        for out in b_outs:
            out[b_part : b_part + few_rows] = few
        dn1 = mm_tn(wq_ref[...], dq_ref[...])
        dn1 = dn1 + mm_tn(wk_ref[...], dk_ref[...])
        dn1 = dn1 + mm_tn(wv_ref[...], dv_ref[...])
        all_ref[...] = dn1.astype(bf16)
        dot = jnp.sum(dn1 * n1.astype(f32), axis=0, keepdims=True)
        high, low = split_low(dot)
        line = iota((16, length), 0)
        tail = jnp.where(line == 0, high, jnp.where(line == 1, low, 0.0)).astype(bf16)
        for rel, out in enumerate((kept_ref, sent_ref.at[0], passed_ref, sent_ref.at[1])):
            at = pl.multiple_of((mine ^ rel) * quarter, quarter)
            out[0:quarter] = all_ref[pl.ds(at, quarter), :]
            out[quarter : quarter + 16] = tail

    dh_own, *others = run(
        attend_back_body,
        [
            ((quarter, length), bf16),
            ((quarter + 16, length), bf16),
            ((quarter + 16, length), bf16),
            ((2, quarter + 16, length), bf16),
            *[((a_part, width), bf16)] * first_a,
            *[((b_part + few_rows, width), bf16)] * first_b,
        ],
        (
            me,
            *do_pieces,
            dest_near,
            *fetched,
            few_parts,
            buckets,
        ),
        "attend_back",
        us=0.01,
        scratch=[
            pltpu.VMEM((owners, chunk_a, width), bf16),
            pltpu.VMEM((owners, chunk_b, width), bf16),
            pltpu.VMEM((here, length), bf16),
            pltpu.VMEM((here, length), bf16),
            pltpu.VMEM((here, length), bf16),
            pltpu.VMEM((width, length), bf16),
            pltpu.VMEM((1, span), jnp.int32),
        ],
        limit=32,
    )

    y_rows, *others = lax.optimization_barrier((y_rows, *others))
    dn1_kept, dn1_passed, dn1_sent = others[:3]
    held = {}

    def tokens_body(
        me_ref, kept_ref, beside_ref, across_ref, dh_ref, tok_ref, r1_ref, small_ref, out_ref
    ):
        mine = me_ref[0] & (ways - 1)
        total = kept_ref[...].astype(f32) + beside_ref[0].astype(f32)
        total = total + across_ref[...].astype(f32)
        dn1 = total[0:quarter]
        dot = total[quarter : quarter + 1] + total[quarter + 1 : quarter + 2]
        one = r1_ref[...]
        small = small_ref[...]
        own = small[:, 0:quarter]
        for t in range(1, ways):
            own = jnp.where(mine == t, small[:, t * quarter : (t + 1) * quarter], own)
        gain = spread_row(own, experts, length)
        x = tok_ref[...].astype(f32)
        out_ref[...] = (
            dh_ref[...].astype(f32) + one * gain * dn1 - x * (one * one / width) * dot
        ).astype(bf16)

    def out_rows_body(me_ref, h_ref, aux_ref, y_ref, o0, o1, o2, o3, all_ref):
        mine = me_ref[0] & (ways - 1)
        out = (h_ref[...] + aux_ref[:, LANES - 1 : LANES] * y_ref[...].astype(f32)).astype(bf16)
        eye = (iota((rows, rows), 0) == iota((rows, rows), 1)).astype(bf16)
        all_ref[...] = mm_tn(out, eye).astype(bf16)
        for rel, piece in enumerate((o0, o1, o2, o3)):
            at = pl.multiple_of((mine ^ rel) * quarter, quarter)
            piece[...] = all_ref[pl.ds(at, quarter), :]

    def out_body(dest_ref, l0, l1, l2, l3, out_ref):
        dest = dest_ref[...]
        total = jnp.zeros((quarter, length), f32)
        for rel, piece in enumerate((l0, l1, l2, l3)):
            hot = (iota((rows, length), 0) + rel * rows == dest).astype(bf16)
            total = total + mm(piece[...], hot)
        out_ref[...] = total.astype(bf16)

    def weights_body(me_ref, u0, dy0, act0, dz0, u1, dy1, act1, dz1, gin_ref, gout_ref):
        gin = mm_tn(u0[...], dz0[...]) + mm_tn(u1[...], dz1[...])
        gin_ref[0] = gin.astype(bf16)
        gout = mm_tn(act0[...], dy0[...]) + mm_tn(act1[...], dy1[...])
        gout_ref[0] = gout.astype(bf16)

    def beside(came, block):
        phase = held.setdefault("phase", 0)
        held["phase"] += 1
        last = 2 * len(order_a) - 1
        extras = {}
        if phase == 0:
            extras["dn1_beside"] = swap(dn1_sent, "tp", 1)
            extras["grad_in"], extras["grad_out"] = run(
                weights_body,
                [((1, width, hidden_here), bf16), ((1, hidden_here, width), bf16)],
                (after(me, dn1_sent), *[Far(v) for v in stored]),
                "expert_weights",
                us=12,
            )
        if phase == 1:
            half = dn1_passed + held["dn1_beside"][1]
            extras["dn1_across"] = swap(half, "tp", 2)
            lo = run(
                out_rows_body,
                [((quarter, rows), bf16)] * ways,
                (me, Far(h_rows), Far(aux), y_rows),
                "layer_rows",
                us=12,
                scratch=[pltpu.VMEM((width, rows), bf16)],
            )
            for rel in range(ways):
                extras["lo%d" % rel] = lo[rel]
        if phase == last - 1:
            few = block.astype(f32)
            extras["few"] = few + swap(few, "tp", 1)
            for rel in range(1, ways):
                extras["lo%d" % rel] = swap(held["lo%d" % rel], "tp", rel)
        if phase == last:
            extras["few_other"] = swap(held["few"], "tp", 2)
            (extras["layer_out"],) = run(
                out_body,
                [((quarter, length), bf16)],
                (Far(dest_far), *[held["lo%d" % rel] for rel in range(ways)]),
                "layer_out",
                us=12,
            )
            (extras["grad_tokens"],) = run(
                tokens_body,
                [((quarter, length), bf16)],
                (
                    after(me, held["few"]),
                    dn1_kept,
                    held["dn1_beside"],
                    held["dn1_across"],
                    dh_own,
                    Far(tok_t),
                    Far(r1),
                    Far(small_far),
                ),
                "tokens_back",
                us=0.01,
            )
        names = list(extras)
        got = lax.optimization_barrier((*[extras[n] for n in names], *came))
        held.update(zip(names, got))
        return got[len(names) :]

    a_blocks, b_blocks = two_chains(
        others[3 : 3 + first_a], others[3 + first_a :], order_a, order_b, few_rows, beside
    )
    layer_out, grad_tokens = held["layer_out"], held["grad_tokens"]
    grad_in, grad_out = held["grad_in"], held["grad_out"]

    def unpack_body(me_ref, few_ref, other_ref, *others):
        a_ins, b_ins = others[: len(a_blocks)], others[len(a_blocks) :][:first_b]
        *results, a_ref, b_ref = others[len(a_blocks) + first_b :]
        gq_ref, gk_ref, gv_ref, go_ref, router_ref, g1_ref, g2_ref, table_ref = results
        mine = me_ref[0] & (ways - 1)
        place = me_ref[0] >> shift
        for order, ref, ins, chunk, start in (
            (order_a, a_ref, a_ins, chunk_a, 0),
            (order_b, b_ref, b_ins, chunk_b, a_rows),
        ):
            at = 0
            for piece in ins:
                for line in range(piece.shape[0] // chunk):
                    low = line * chunk
                    ref[rel_of(at, order) ^ place] = piece[low : low + chunk]
                    at += 1
            for c in range(owners):
                low = start + c * chunk
                which, low = low // here, low % here
                (gq_ref, gk_ref, gv_ref, go_ref)[which][low : low + chunk] = ref[c]
        total = few_ref[...] + other_ref[...]
        own = total[:, 0:quarter]
        for t in range(1, ways):
            own = jnp.where(mine == t, total[:, t * quarter : (t + 1) * quarter], own)
        router_ref[...] = own[0:experts].astype(bf16)
        g2_ref[...] = own[experts].astype(bf16)
        g1_ref[...] = own[experts + 1].astype(bf16)
        lines = total[experts + 2 : experts + 2 + heads]
        table = lines[:, 0:bins]
        for t in range(1, ways):
            table = jnp.where(mine == t, lines[:, t * bins : (t + 1) * bins], table)
        table_ref[...] = table.astype(bf16)

    gq, gk, gv, go, g_router, g_one, g_two, g_table = run(
        unpack_body,
        [
            ((here, width), bf16),
            ((here, width), bf16),
            ((here, width), bf16),
            ((here, width), bf16),
            ((experts, quarter), bf16),
            ((quarter,), bf16),
            ((quarter,), bf16),
            ((heads, bins), bf16),
        ],
        (me, held["few"], held["few_other"], *a_blocks, *b_blocks),
        "unpack",
        us=4,
        scratch=[
            pltpu.VMEM((owners, chunk_a, width), bf16),
            pltpu.VMEM((owners, chunk_b, width), bf16),
        ],
    )
    return (
        layer_out.T,
        grad_tokens.T,
        gq.T,
        gk.T,
        gv.T,
        go,
        g_table.T,
        g_router.T,
        grad_in,
        grad_out,
        g_one,
        g_two,
    )


def solution(mesh):
    placed = (
        P("exp", "tp"),
        P(None, "tp"),
        P(None, "tp"),
        P(None, "tp"),
        P("tp", None),
        P(None, "tp"),
        P("tp", None),
        P("exp", None, "tp"),
        P("exp", "tp", None),
        P("tp"),
        P("tp"),
        P("exp", None),
        P("exp", None),
        P(),
        P("exp", "tp"),
    )
    return jax.shard_map(
        local,
        mesh=mesh,
        in_specs=placed,
        out_specs=(
            P("exp", "tp"),
            P("exp", "tp"),
            P(None, "tp"),
            P(None, "tp"),
            P(None, "tp"),
            P("tp", None),
            P(None, "tp"),
            P("tp", None),
            P("exp", None, "tp"),
            P("exp", "tp", None),
            P("tp"),
            P("tp"),
        ),
        check_vma=False,
    )
```
